32 devices in a mesh: rep: 4 (over y, x), shard: 8 (over z, core).
Axes of the slice: x: 2, y: 2, z: 4, core: 2. Of those that a mesh axis runs over, the one named last changes fastest.
Arguments:
- hidden: bfloat16 [32, 256, 2048], P(('rep', 'shard')), may hold values from -6 to 6
- segments: int32 [32, 256], P(('rep', 'shard')), may hold values from 0 to 1, as said below
- cotangent: bfloat16 [32, 256, 2048], P(('rep', 'shard')), may hold values from -6 to 6
- in_master: float32 [2048, 8192], P('shard'), may hold values from -0.125 to 0.125
- in_first: float32 [2048, 8192], P('shard'), may hold values from -32 to 32
- in_second: float32 [2048, 8192], P('shard'), may hold values from 155.648 to 622.592
- x_master: float32 [4096, 160], P('shard'), may hold values from -0.09375 to 0.09375
- x_first: float32 [4096, 160], P('shard'), may hold values from -32 to 32
- x_second: float32 [4096, 160], P('shard'), may hold values from 155.648 to 622.592
- dt_master: float32 [4096, 128], P('shard'), may hold values from -0.5 to 0.5
- dt_first: float32 [4096, 128], P('shard'), may hold values from -1.75 to 1.75
- dt_second: float32 [4096, 128], P('shard'), may hold values from 0.0622592 to 0.24576
- out_master: float32 [4096, 2048], P('shard'), may hold values from -0.25 to 0.25
- out_first: float32 [4096, 2048], P('shard'), may hold values from -20 to 20
- out_second: float32 [4096, 2048], P('shard'), may hold values from 56.5248 to 221.184
- chan_master: float32 [4096, 23], P('shard'), may hold values from -7.5 to 2.8, as said below
- chan_first: float32 [4096, 23], P('shard'), may hold values from -16 to 16
- chan_second: float32 [4096, 23], P('shard'), may hold values from 39.3216 to 155.648
- gain_master: float32 [2048], P('shard'), may hold values from 0.5 to 1.5
- gain_first: float32 [2048], P('shard'), may hold values from -64 to 64
- gain_second: float32 [2048], P('shard'), may hold values from 622.592 to 2457.6
Outputs:
- layer_output: bfloat16 [32, 256, 2048], P(('rep', 'shard'))
- input_grad: bfloat16 [32, 256, 2048], P(('rep', 'shard'))
- in_first_new: float32 [2048, 8192], P('shard')
- in_second_new: float32 [2048, 8192], P('shard')
- in_master_new: float32 [2048, 8192], P('shard')
- x_first_new: float32 [4096, 160], P('shard')
- x_second_new: float32 [4096, 160], P('shard')
- x_master_new: float32 [4096, 160], P('shard')
- dt_first_new: float32 [4096, 128], P('shard')
- dt_second_new: float32 [4096, 128], P('shard')
- dt_master_new: float32 [4096, 128], P('shard')
- out_first_new: float32 [4096, 2048], P('shard')
- out_second_new: float32 [4096, 2048], P('shard')
- out_master_new: float32 [4096, 2048], P('shard')
- chan_first_new: float32 [4096, 23], P('shard')
- chan_second_new: float32 [4096, 23], P('shard')
- chan_master_new: float32 [4096, 23], P('shard')
- gain_first_new: float32 [2048], P('shard')
- gain_second_new: float32 [2048], P('shard')
- gain_master_new: float32 [2048], P('shard')
The draws below stay inside these ranges and needn't reach their ends.
Inputs may be any that keep to these rules, and one draw needn't show every extreme that they name: `segments`: each sequence holds two documents: ids are 0 on its first L tokens and 1 on the rest, with 96 <= L <= 160. `chan_master`: column layout as in the meaning; the logarithms of the rates lie in 0 to 2.8, the step-size biases in -7.5 to -2.5, the skip gains in 0.5 to 1.5.
All inputs are finite; a program needn't handle non-finite values.
Results may differ from the reference program's by a relative error of at most 0.0055.
The reference program's roundings to bfloat16 on the way count: a program that leaves them out, or rounds other values in their place, can miss the bound.
Values may be sent and summed in bfloat16 or wider, within the bound.
A program may use at most 384 MiB of HBM per device.

```python
import math
import jax
import jax.numpy as jnp
from jax import lax

D = 2048
INNER = 4096
NSTATE = 16
RANK = 128
KCONV = 4
SEQ = 256
BLOCK = 16
ADAM_STEP = 10
SEQS = 32
TOKENS = 8192
NBLOCK = 16
XCOLS = 160
CHAN = 23


def draw_segments(key, part):
    key = jax.random.fold_in(key, 23)
    first_len = jax.random.randint(key, (SEQS, 1), 3 * SEQ // 8, 5 * SEQ // 8 + 1)
    positions = jnp.arange(SEQ, dtype=jnp.int32)[None, :]
    return (positions >= first_len).astype(jnp.int32)


def draw_chan_master(key, part):
    key = jax.random.fold_in(key, 11)
    keys = jax.random.split(key, 5)
    taps = 0.5 * jnp.clip(jax.random.normal(keys[0], (INNER, KCONV), jnp.float32), -3.0, 3.0)
    a_log = jax.random.uniform(keys[1], (INNER, NSTATE), jnp.float32, 0.0, 2.77)
    dt_bias = jax.random.uniform(keys[3], (INNER, 1), jnp.float32, -6.5, -2.5)
    conv_bias = 0.5 * jnp.clip(jax.random.normal(keys[2], (INNER, 1), jnp.float32), -3.0, 3.0)
    skip = jax.random.uniform(keys[4], (INNER, 1), jnp.float32, 0.5, 1.5)
    return jnp.concatenate([taps, a_log, conv_bias, dt_bias, skip], axis=1)


def steps_of(own_key, dims, cuts, least, top_value):
    level, own = 1.0, jax.random.fold_in(own_key, 6)
    for position, shards_of in cuts:
        heights = jnp.exp(jax.random.uniform(jax.random.fold_in(own, position), (shards_of,), jnp.float32, least / len(cuts), top_value / len(cuts)))
        level = level * jnp.repeat(heights, dims[position] // shards_of).reshape([-1 if axis == position else 1 for axis in range(len(dims))])
    return level


def normal_values(rng, shape, spread, most, shards=(), held_as=jnp.bfloat16):
    entries = spread * jax.random.normal(rng, shape, jnp.float32)
    if shards:
        entries = entries * steps_of(rng, shape, shards, -0.22, 0.18)
    return jnp.clip(entries, -most, most).astype(held_as)


def setup_inputs(seed: int = 0) -> dict:
    arg_keys = jax.random.split(jax.random.key(seed), 22)
    hidden = normal_values(arg_keys[0], (SEQS, SEQ, D), 1.0, 6.0, ((0, 32),))
    segments = draw_segments(jax.random.fold_in(arg_keys[21], 71), 0)
    cotangent = normal_values(arg_keys[2], (SEQS, SEQ, D), 1.0, 6.0, ((0, 32),))
    in_master = normal_values(arg_keys[3], (D, 2 * INNER), D ** -0.5, 0.125, ((0, 8),), jnp.float32)
    in_first = normal_values(arg_keys[4], (D, 2 * INNER), (0.066 * TOKENS ** 0.5), 32.0, ((0, 8),), jnp.float32)
    in_second = jnp.clip(jnp.exp(math.log(622.592) - 1.3862944 * jax.random.uniform(arg_keys[5], (D, 2 * INNER), jnp.float32) ** steps_of(arg_keys[5], (D, 2 * INNER), ((0, 8),), -0.2, 0.2)), 155.648, 622.592)
    x_master = normal_values(arg_keys[6], (INNER, XCOLS), INNER ** -0.5, 0.09375, ((0, 8),), jnp.float32)
    x_first = normal_values(arg_keys[7], (INNER, XCOLS), (0.066 * TOKENS ** 0.5), 32.0, ((0, 8),), jnp.float32)
    x_second = jnp.clip(jnp.exp(math.log(622.592) - 1.3862944 * jax.random.uniform(arg_keys[8], (INNER, XCOLS), jnp.float32) ** steps_of(arg_keys[8], (INNER, XCOLS), ((0, 8),), -0.2, 0.2)), 155.648, 622.592)
    dt_master = normal_values(arg_keys[9], (INNER, RANK), RANK ** -0.5, 0.5, ((0, 8),), jnp.float32)
    dt_first = normal_values(arg_keys[10], (INNER, RANK), (0.0013 * TOKENS ** 0.5), 1.75, ((0, 8),), jnp.float32)
    dt_second = jnp.clip(jnp.exp(math.log(0.24576) - 1.3730491 * jax.random.uniform(arg_keys[11], (INNER, RANK), jnp.float32) ** steps_of(arg_keys[11], (INNER, RANK), ((0, 8),), -0.2, 0.2)), 0.0622592, 0.24576)
    out_master = normal_values(arg_keys[12], (INNER, D), (INNER // 8) ** -0.5, 0.25, ((0, 8),), jnp.float32)
    out_first = normal_values(arg_keys[13], (INNER, D), (0.04 * TOKENS ** 0.5), 20.0, ((0, 8),), jnp.float32)
    out_second = jnp.clip(jnp.exp(math.log(221.184) - 1.3643155 * jax.random.uniform(arg_keys[14], (INNER, D), jnp.float32) ** steps_of(arg_keys[14], (INNER, D), ((0, 8),), -0.2, 0.2)), 56.5248, 221.184)
    chan_master = draw_chan_master(jax.random.fold_in(arg_keys[21], 71), 0)
    chan_first = normal_values(arg_keys[16], (INNER, CHAN), (0.033 * TOKENS ** 0.5), 16.0, ((0, 8),), jnp.float32)
    chan_second = jnp.clip(jnp.exp(math.log(155.648) - 1.375823 * jax.random.uniform(arg_keys[17], (INNER, CHAN), jnp.float32) ** steps_of(arg_keys[17], (INNER, CHAN), ((0, 8),), -0.2, 0.2)), 39.3216, 155.648)
    gain_master = jnp.clip(1.0 + 0.1 * jax.random.normal(arg_keys[18], (D,), jnp.float32), 0.5, 1.5)
    gain_first = normal_values(arg_keys[19], (D,), (0.13 * TOKENS ** 0.5), 64.0, ((0, 8),), jnp.float32)
    gain_second = jnp.clip(jnp.exp(math.log(2457.6) - 1.3730492 * jax.random.uniform(arg_keys[20], (D,), jnp.float32) ** steps_of(arg_keys[20], (D,), ((0, 8),), -0.2, 0.2)), 622.592, 2457.6)
    return {"hidden": hidden, "segments": segments, "cotangent": cotangent, "in_master": in_master, "in_first": in_first, "in_second": in_second, "x_master": x_master, "x_first": x_first, "x_second": x_second, "dt_master": dt_master, "dt_first": dt_first, "dt_second": dt_second, "out_master": out_master, "out_first": out_first, "out_second": out_second, "chan_master": chan_master, "chan_first": chan_first, "chan_second": chan_second, "gain_master": gain_master, "gain_first": gain_first, "gain_second": gain_second}


norm_eps = 1e-05
beta_first = 0.9
beta_second = 0.95
adam_eps = 1e-08
weight_decay = 0.1
learn_rates = (0.044, 0.03, 0.18, 0.09, 1.0, 0.6)
with_decay = (True, True, True, True, False, False)

@jax.custom_vjp
def low(v):
    return lax.optimization_barrier(v.astype(jnp.bfloat16)).astype(jnp.float32)

@jax.custom_vjp
def low_back(v):
    return v

def low_keep(v):
    return (low(v), None)

def low_pass(kept, grad):
    return (grad,)

def back_keep(v):
    return (v, None)

def back_low(kept, grad):
    return (low(grad),)
low.defvjp(low_keep, low_pass)
low_back.defvjp(back_keep, back_low)

def product(left, right):
    return jnp.dot(left, right, precision=lax.Precision.HIGHEST)

def same_document(doc_ids, offset):
    return jnp.pad(doc_ids, (offset, 0), constant_values=-1)[:SEQ] == doc_ids

def selective_scan(step_size, conv_out, state_in, state_out, carry_mask, rates):

    def token_step(state, inputs_now):
        size_now, conv_now, in_now, out_now, mask_now = inputs_now
        state = jnp.exp(size_now[:, None] * rates) * mask_now * state + (size_now * conv_now)[:, None] * in_now[None, :]
        return (state, lax.optimization_barrier(jnp.sum(state * out_now[None, :], axis=1)))

    def block_step(state, block_inputs):
        return lax.scan(token_step, state, block_inputs)
    blocked = tuple((v.reshape((NBLOCK, BLOCK) + v.shape[1:]) for v in (step_size, conv_out, state_in, state_out, carry_mask)))
    _, outputs = lax.scan(jax.checkpoint(block_step), jnp.zeros((INNER, NSTATE), jnp.float32), blocked)
    return outputs.reshape(SEQ, INNER)

def layer_forward(residual, doc_ids, weights):
    w_in, w_x, w_dt, w_out, channel, gain = weights
    taps = channel[:, :KCONV]
    a_log = channel[:, KCONV:KCONV + NSTATE]
    conv_bias = channel[:, KCONV + NSTATE]
    dt_bias = channel[:, KCONV + NSTATE + 1]
    skip = channel[:, KCONV + NSTATE + 2]
    inv_rms = lax.rsqrt(lax.optimization_barrier(jnp.mean(residual * residual, axis=1, keepdims=True)) + norm_eps)
    normed = low(residual * inv_rms * gain)
    both = low_back(product(normed, w_in))
    inner_part = both[:, :INNER]
    gate_part = both[:, INNER:]
    conv_pre = jnp.zeros_like(inner_part) + conv_bias
    for k in range(KCONV):
        offset = KCONV - 1 - k
        moved = jnp.pad(inner_part, ((offset, 0), (0, 0)))[:SEQ]
        conv_pre = conv_pre + taps[:, k] * jnp.where(same_document(doc_ids, offset)[:, None], moved, 0.0)
    conv_out = low(jax.nn.silu(conv_pre))
    projected = low_back(product(conv_out, w_x))
    dt_in = low(projected[:, :RANK])
    state_in = projected[:, RANK:RANK + NSTATE]
    state_out = projected[:, RANK + NSTATE:]
    step_size = jax.nn.softplus(low_back(product(dt_in, w_dt.T)) + dt_bias)
    carry_mask = same_document(doc_ids, 1).astype(residual.dtype)
    rates = -jnp.exp(a_log)
    mixer_y = selective_scan(step_size, conv_out, state_in, state_out, carry_mask, rates) + skip * conv_out
    mixed = low(mixer_y * jax.nn.silu(gate_part))
    return residual + product(mixed, w_out)

def adam_step(master, first, second, gradient, rate, decays):
    first_new = beta_first * first + (1.0 - beta_first) * gradient
    second_new = beta_second * second + (1.0 - beta_second) * gradient * gradient
    update = first_new / (1.0 - beta_first ** ADAM_STEP) / (jnp.sqrt(second_new / (1.0 - beta_second ** ADAM_STEP)) + adam_eps)
    if decays:
        update = update + weight_decay * master
    return (first_new, second_new, master - rate * update)

def reference(hidden, segments, cotangent, in_master, in_first, in_second, x_master, x_first, x_second, dt_master, dt_first, dt_second, out_master, out_first, out_second, chan_master, chan_first, chan_second, gain_master, gain_first, gain_second):
    masters = (in_master, x_master, dt_master, out_master, chan_master, gain_master)
    copies = tuple((low(m) for m in masters))

    def one_sequence(totals, item):
        seq_hidden, seq_ids, seq_upstream = item
        residual = seq_hidden.astype(jnp.float32)

        def forward(values, weights):
            return layer_forward(values, seq_ids, weights)
        result, pull = jax.vjp(forward, residual, copies)
        grad_resid, grad_weights = pull(seq_upstream.astype(jnp.float32))
        totals = tuple((a + b for a, b in zip(totals, grad_weights)))
        return (totals, (result.astype(jnp.bfloat16), grad_resid.astype(jnp.bfloat16)))
    start_totals = tuple((jnp.zeros_like(c) for c in copies))
    grads, (layer_output, input_grad) = lax.scan(one_sequence, start_totals, (hidden, segments, cotangent))
    in_first_new, in_second_new, in_master_new = adam_step(in_master, in_first, in_second, grads[0], learn_rates[0], with_decay[0])
    x_first_new, x_second_new, x_master_new = adam_step(x_master, x_first, x_second, grads[1], learn_rates[1], with_decay[1])
    dt_first_new, dt_second_new, dt_master_new = adam_step(dt_master, dt_first, dt_second, grads[2], learn_rates[2], with_decay[2])
    out_first_new, out_second_new, out_master_new = adam_step(out_master, out_first, out_second, grads[3], learn_rates[3], with_decay[3])
    chan_first_new, chan_second_new, chan_master_new = adam_step(chan_master, chan_first, chan_second, grads[4], learn_rates[4], with_decay[4])
    gain_first_new, gain_second_new, gain_master_new = adam_step(gain_master, gain_first, gain_second, grads[5], learn_rates[5], with_decay[5])
    return (layer_output, input_grad, in_first_new, in_second_new, in_master_new, x_first_new, x_second_new, x_master_new, dt_first_new, dt_second_new, dt_master_new, out_first_new, out_second_new, out_master_new, chan_first_new, chan_second_new, chan_master_new, gain_first_new, gain_second_new, gain_master_new)
```

```python
import functools

import jax
import jax.numpy as jnp
from jax import lax
from jax.experimental import pallas as pl
from jax.experimental.pallas import tpu as pltpu
from jax.sharding import PartitionSpec as P

NSTATE = 16
RANK = 128
KCONV = 4
ADAM_STEP = 10
CHUNK = 32
LANES = 128
SUBS = 8
CUT = 1e30
LOG2E = 1.4426950408889634

norm_eps = 1e-05
beta_first = 0.9
beta_second = 0.95
adam_eps = 1e-08
weight_decay = 0.1
learn_rates = (0.044, 0.03, 0.18, 0.09, 1.0, 0.6)
with_decay = (True, True, True, True, False, False)

bf16 = jnp.bfloat16
f32 = jnp.float32


def silu_slope(values):
    sigma = jax.nn.sigmoid(values)
    return sigma * (1.0 + values * (1.0 - sigma))


def dot(a, b, dims):
    return lax.dot_general(a, b, (dims, ((), ())), preferred_element_type=f32)


def expand_inputs(bc_ref, bx, sb):
    def one(n, carry):
        v = bc_ref[0, n, pl.ds(sb * SUBS, SUBS), :]
        for t in range(CHUNK):
            bx[t, n] = jnp.broadcast_to(v[:, t : t + 1], (SUBS, LANES))
        return carry

    lax.fori_loop(0, 2 * NSTATE, one, 0)


def spread(scratch, q, values):
    for g in range(scratch.shape[0]):
        scratch[g, pl.ds(q * CHUNK, CHUNK), :] = values[:, g * LANES : (g + 1) * LANES]


def collect(ref, q, scratch):
    for g in range(scratch.shape[0]):
        ref[q, :, pl.ds(g * LANES, LANES)] = scratch[g, pl.ds(q * CHUNK, CHUNK), :]


def scan_fwd_kernel(step_ref, cut_ref, conv_ref, bc_ref, rate_ref, y_ref, starts_ref, state, bx, stepm, drive, ys):
    seqs, _, width = step_ref.shape

    @pl.when(pl.program_id(0) == 0)
    def _():
        state[...] = jnp.zeros_like(state)

    starts_ref[0] = state[...]
    for q in range(seqs):
        step = step_ref[q]
        spread(stepm, q, step + cut_ref[q])
        spread(drive, q, step * conv_ref[q].astype(f32))
    for sb in range(seqs // SUBS):
        expand_inputs(bc_ref, bx, sb)
        sub = pl.ds(sb * SUBS, SUBS)

        def group(g, carry):
            lanes = pl.ds(pl.multiple_of(g * LANES, LANES), LANES)
            rates = [rate_ref[n, :, lanes] for n in range(NSTATE)]

            def token(t, st):
                rows = pl.ds(sb * SUBS * CHUNK + t, SUBS, stride=CHUNK)
                sm = stepm[g, rows, :]
                dx = drive[g, rows, :]
                y = None
                out = []
                for n in range(NSTATE):
                    dec = jnp.exp2(sm * rates[n])
                    s_n = dec * st[n] + dx * bx[t, n]
                    out.append(s_n)
                    part = s_n * bx[t, NSTATE + n]
                    y = part if y is None else y + part
                ys[g, rows, :] = y
                return tuple(out)

            st = tuple(state[n, sub, lanes] for n in range(NSTATE))
            st = lax.fori_loop(0, CHUNK, token, st)
            for n in range(NSTATE):
                state[n, sub, lanes] = st[n]
            return carry

        lax.fori_loop(0, width // LANES, group, 0)
    for q in range(seqs):
        collect(y_ref, q, ys)


def scan_bwd_kernel(
    step_ref, cut_ref, conv_ref, bc_ref, rate_ref, starts_ref, gy_ref,
    gstep_ref, gconv_ref, gbc_ref, grate_ref,
    flow, bx, stepm, step2, conv2, gy2, gs2, gc2, dec_s, pri_s, acc,
):
    seqs, _, width = step_ref.shape

    @pl.when(pl.program_id(0) == 0)
    def _():
        flow[...] = jnp.zeros_like(flow)
        grate_ref[...] = jnp.zeros_like(grate_ref)

    for q in range(seqs):
        step = step_ref[q]
        spread(step2, q, step)
        spread(stepm, q, step + cut_ref[q])
        spread(conv2, q, conv_ref[q].astype(f32))
        spread(gy2, q, gy_ref[q])
    for sb in range(seqs // SUBS):
        expand_inputs(bc_ref, bx, sb)
        sub = pl.ds(sb * SUBS, SUBS)
        acc[...] = jnp.zeros_like(acc)

        def group(g, carry):
            lanes = pl.ds(pl.multiple_of(g * LANES, LANES), LANES)

            def token_f(t, st):
                rows = pl.ds(sb * SUBS * CHUNK + t, SUBS, stride=CHUNK)
                sm = stepm[g, rows, :]
                dx = step2[g, rows, :] * conv2[g, rows, :]
                out = []
                for n in range(NSTATE):
                    dec = jnp.exp2(sm * (rate_ref[n, :, lanes] * LOG2E))
                    dec_s[t, n] = dec
                    pri_s[t, n] = st[n]
                    out.append(dec * st[n] + dx * bx[t, n])
                return tuple(out)

            st = tuple(starts_ref[0, n, sub, lanes] for n in range(NSTATE))
            st = lax.fori_loop(0, CHUNK, token_f, st)
            for n in range(NSTATE):
                pri_s[CHUNK, n] = st[n]

            def token_b(i, carried):
                t = CHUNK - 1 - i
                fl, ga = carried
                rows = pl.ds(sb * SUBS * CHUNK + t, SUBS, stride=CHUNK)
                size = step2[g, rows, :]
                conv = conv2[g, rows, :]
                gy = gy2[g, rows, :]
                dx = size * conv
                along = None
                gsz = None
                nfl, nga = [], []
                for n in range(NSTATE):
                    grad = gy * bx[t, NSTATE + n] + fl[n]
                    dg = dec_s[t, n] * grad
                    th = dg * pri_s[t, n]
                    a = grad * bx[t, n]
                    b = th * rate_ref[n, :, lanes]
                    along = a if along is None else along + a
                    gsz = b if gsz is None else gsz + b
                    acc[t, n] += grad * dx
                    acc[t, NSTATE + n] += pri_s[t + 1, n] * gy
                    nfl.append(dg)
                    nga.append(ga[n] + th * size)
                gs2[g, rows, :] = gsz + conv * along
                gc2[g, rows, :] = size * along
                return (tuple(nfl), tuple(nga))

            fl = tuple(flow[n, sub, lanes] for n in range(NSTATE))
            ga = tuple(grate_ref[n, :, lanes] for n in range(NSTATE))
            fl, ga = lax.fori_loop(0, CHUNK, token_b, (fl, ga))
            for n in range(NSTATE):
                flow[n, sub, lanes] = fl[n]
                grate_ref[n, :, lanes] = ga[n]
            return carry

        lax.fori_loop(0, width // LANES, group, 0)

        def reduce_n(n, carry):
            column = lax.broadcasted_iota(jnp.int32, (SUBS, CHUNK), 1)
            out = jnp.zeros((SUBS, CHUNK), f32)
            for t in range(CHUNK):
                total = jnp.sum(acc[t, n], axis=1, keepdims=True)
                out = jnp.where(column == t, total, out)
            gbc_ref[0, n, sub, :] = out
            return carry

        lax.fori_loop(0, 2 * NSTATE, reduce_n, 0)
    for q in range(seqs):
        collect(gstep_ref, q, gs2)
        collect(gconv_ref, q, gc2)


def scan_specs(seqs, length, width, chunk_of):
    tokens = pl.BlockSpec((seqs, CHUNK, width), lambda i: (0, chunk_of(i), 0))
    cuts = pl.BlockSpec((seqs, CHUNK, 1), lambda i: (0, chunk_of(i), 0))
    bcs = pl.BlockSpec((1, 2 * NSTATE, seqs, CHUNK), lambda i: (chunk_of(i), 0, 0, 0))
    rates = pl.BlockSpec((NSTATE, SUBS, width), lambda i: (0, 0, 0))
    starts = pl.BlockSpec((1, NSTATE, seqs, width), lambda i: (chunk_of(i), 0, 0, 0))
    return tokens, cuts, bcs, rates, starts


def scan_forward(step, cut, conv, bc, rates):
    seqs, length, width = step.shape
    chunks = length // CHUNK
    tokens, cuts, bcs, rate_spec, starts = scan_specs(seqs, length, width, lambda i: i)
    return pl.pallas_call(
        scan_fwd_kernel,
        grid=(chunks,),
        in_specs=[tokens, cuts, tokens, bcs, rate_spec],
        out_specs=[tokens, starts],
        out_shape=[
            jax.ShapeDtypeStruct(step.shape, f32),
            jax.ShapeDtypeStruct((chunks, NSTATE, seqs, width), f32),
        ],
        scratch_shapes=[
            pltpu.VMEM((NSTATE, seqs, width), f32),
            pltpu.VMEM((CHUNK, 2 * NSTATE, SUBS, LANES), f32),
            pltpu.VMEM((width // LANES, seqs * CHUNK, LANES), f32),
            pltpu.VMEM((width // LANES, seqs * CHUNK, LANES), f32),
            pltpu.VMEM((width // LANES, seqs * CHUNK, LANES), f32),
        ],
        compiler_params=pltpu.CompilerParams(vmem_limit_bytes=50 * 2**20),
        cost_estimate=pl.CostEstimate(
            flops=8 * step.size * NSTATE, bytes_accessed=12 * step.size, transcendentals=step.size * NSTATE
        ),
        name="scan_forward",
    )(step, cut, conv, bc, rates * LOG2E)


def scan_backward(step, cut, conv, bc, rates, starts, grad_y):
    seqs, length, width = step.shape
    chunks = length // CHUNK
    tokens, cuts, bcs, rate_spec, start_spec = scan_specs(seqs, length, width, lambda i: chunks - 1 - i)
    tall = pltpu.VMEM((width // LANES, seqs * CHUNK, LANES), f32)
    return pl.pallas_call(
        scan_bwd_kernel,
        grid=(chunks,),
        in_specs=[tokens, cuts, tokens, bcs, rate_spec, start_spec, tokens],
        out_specs=[tokens, tokens, bcs, rate_spec],
        out_shape=[
            jax.ShapeDtypeStruct(step.shape, f32),
            jax.ShapeDtypeStruct(step.shape, f32),
            jax.ShapeDtypeStruct(bc.shape, f32),
            jax.ShapeDtypeStruct((NSTATE, SUBS, width), f32),
        ],
        scratch_shapes=[
            pltpu.VMEM((NSTATE, seqs, width), f32),
            pltpu.VMEM((CHUNK, 2 * NSTATE, SUBS, LANES), f32),
            tall, tall, tall, tall, tall, tall,
            pltpu.VMEM((CHUNK, NSTATE, SUBS, LANES), f32),
            pltpu.VMEM((CHUNK + 1, NSTATE, SUBS, LANES), f32),
            pltpu.VMEM((CHUNK, 2 * NSTATE, SUBS, LANES), f32),
        ],
        compiler_params=pltpu.CompilerParams(vmem_limit_bytes=56 * 2**20),
        cost_estimate=pl.CostEstimate(
            flops=24 * step.size * NSTATE, bytes_accessed=24 * step.size, transcendentals=step.size * NSTATE
        ),
        name="scan_backward",
    )(step, cut, conv, bc, rates, starts, grad_y)


class Links:
    def __init__(self, reps, shard_size):
        self.reps, self.shard_size = reps, shard_size
        self.planes = shard_size // 2
        self.r = lax.axis_index("rep")
        shard = lax.axis_index("shard")
        self.z, self.c = shard // 2, shard % 2

    def rep(self, value, k):
        return lax.ppermute(value, "rep", [(i, i ^ k) for i in range(self.reps)])

    def core(self, value):
        return lax.ppermute(value, "shard", [(i, i ^ 1) for i in range(self.shard_size)])

    def up(self, value, k):
        n = self.shard_size
        return lax.ppermute(value, "shard", [(i, (i + 2 * k) % n) for i in range(n)])

    def gather_rep(self, value):
        if self.reps != 4:
            return [value] + [self.rep(value, k) for k in range(1, self.reps)]
        half = value.shape[0] // 2
        one, two = self.rep(value, 1), self.rep(value, 2)
        three = jnp.concatenate([self.rep(two[:half], 1), self.rep(one[half:], 2)], axis=0)
        return [value, one, two, three]

    def gather_plane(self, value):
        near = jnp.stack(self.gather_rep(value))
        return jnp.concatenate([near, self.core(near)], axis=0)

    def scatter_plane(self, partial, wire):
        reps = self.reps
        pair = partial[:reps].astype(f32) + self.core(partial[reps:].astype(wire)).astype(f32)
        total = pair[0]
        for k in range(1, reps):
            total = total + self.rep(pair[k].astype(wire), k).astype(f32)
        return total

    def gather_z(self, value):
        rows = value.shape[0]
        out = jnp.zeros((self.planes * rows,) + value.shape[1:], value.dtype)
        start = (0,) * (value.ndim - 1)
        out = lax.dynamic_update_slice(out, value, (self.z * rows,) + start)
        for k in range(1, self.planes):
            at = (self.z + self.planes - k) % self.planes
            out = lax.dynamic_update_slice(out, self.up(value, k), (at * rows,) + start)
        return out

    def scatter_z(self, value, wire):
        rows = value.shape[0] // self.planes
        total = lax.dynamic_slice_in_dim(value, self.z * rows, rows, 0).astype(f32)
        for k in range(1, self.planes):
            to = (self.z + k) % self.planes
            block = lax.dynamic_slice_in_dim(value, to * rows, rows, 0)
            total = total + self.up(block.astype(wire), k).astype(f32)
        return total

    def pair_rows(self, own, other):
        first = jnp.where(self.c == 0, own, other)
        second = jnp.where(self.c == 0, other, own)
        return jnp.stack([first, second])

    def order_reps(self, values):
        bit = 1
        while bit < self.reps:
            swap = (self.r & bit) != 0
            values = [jnp.where(swap, values[i ^ bit], values[i]) for i in range(self.reps)]
            bit *= 2
        return jnp.stack(values)


def adam_step(master, first, second, gradient, rate, decays):
    first_new = beta_first * first + (1.0 - beta_first) * gradient
    second_new = beta_second * second + (1.0 - beta_second) * gradient * gradient
    update = (
        first_new
        / (1.0 - beta_first**ADAM_STEP)
        / (jnp.sqrt(second_new / (1.0 - beta_second**ADAM_STEP)) + adam_eps)
    )
    if decays:
        update = update + weight_decay * master
    return (first_new, second_new, master - rate * update)


def to_chunks(values):
    seqs, length, n = values.shape
    return values.reshape(seqs, length // CHUNK, CHUNK, n).transpose(1, 3, 0, 2)


def from_chunks(values):
    chunks, n, seqs, _ = values.shape
    return values.transpose(2, 0, 3, 1).reshape(seqs, chunks * CHUNK, n)


def shift_down(values, offset):
    return jnp.pad(values, ((0, 0), (offset, 0), (0, 0)))[:, : values.shape[1]]


def shift_up(values, offset):
    return jnp.pad(values, ((0, 0), (0, offset), (0, 0)))[:, offset:]


def shards(
    reps, shard_size,
    hidden, segments, cotangent,
    in_master, in_first, in_second,
    x_master, x_first, x_second,
    dt_master, dt_first, dt_second,
    out_master, out_first, out_second,
    chan_master, chan_first, chan_second,
    gain_master, gain_first, gain_second,
):
    net = Links(reps, shard_size)
    planes, r, z, c = net.planes, net.r, net.z, net.c
    length, model = hidden.shape[1:]
    in_rows = in_master.shape[0]
    own_chan = out_master.shape[0]
    sub = own_chan // reps
    width = planes * sub
    xcols = x_master.shape[1]
    chan_cols = chan_master.shape[1]
    seqs = 2 * reps

    def sub_rows(value):
        return lax.dynamic_slice_in_dim(value, r * sub, sub, 0)

    in_view = in_master.reshape(in_rows, 2, planes, 2, reps, sub)
    in_mine = lax.dynamic_index_in_dim(in_view, r, 4, keepdims=False).astype(bf16)
    in_own = lax.dynamic_index_in_dim(in_mine, c, 3, keepdims=False).reshape(in_rows, 2 * width)
    in_other = lax.dynamic_index_in_dim(in_mine, 1 - c, 3, keepdims=False).reshape(in_rows, 2 * width)
    gain_pair = net.pair_rows(gain_master.astype(bf16), net.core(gain_master.astype(bf16)))
    small = jnp.concatenate(
        [
            sub_rows(x_master).astype(bf16),
            sub_rows(dt_master).astype(bf16),
            sub_rows(chan_master).astype(bf16),
            gain_pair.reshape(sub, reps),
        ],
        axis=1,
    )
    small_all = net.gather_z(small)
    w_x = small_all[:, :xcols]
    w_dt = small_all[:, xcols : xcols + RANK]
    channel = small_all[:, xcols + RANK : xcols + RANK + chan_cols].astype(f32)
    gain = small_all[:, xcols + RANK + chan_cols :].reshape(model).astype(f32)
    in_pair = net.pair_rows(in_own, net.core(in_other)).reshape(2 * in_rows, 2 * width)
    w_inner = net.gather_z(in_pair[:, :width])
    w_gate = net.gather_z(in_pair[:, width:])
    w_out = net.gather_z(sub_rows(out_master).astype(bf16))

    taps = channel[:, :KCONV]
    a_log = channel[:, KCONV : KCONV + NSTATE]
    conv_bias = channel[:, KCONV + NSTATE]
    dt_bias = channel[:, KCONV + NSTATE + 1]
    skip = channel[:, KCONV + NSTATE + 2]
    rates = -jnp.exp(a_log)
    rate_tiles = jnp.broadcast_to(rates.T[:, None, :], (NSTATE, SUBS, width))

    hidden_all = net.gather_plane(hidden[0])
    ids = net.gather_plane(segments.astype(f32)).reshape(seqs, length)
    upstream = net.gather_plane(cotangent[0])
    masks = [
        (jnp.pad(ids, ((0, 0), (KCONV - 1 - k, 0)), constant_values=-1)[:, :length] == ids)[:, :, None]
        for k in range(KCONV)
    ]
    cut = jnp.where(masks[KCONV - 2], 0.0, CUT)

    residual = hidden_all.astype(f32)
    inv_rms = lax.rsqrt(jnp.mean(residual * residual, axis=2, keepdims=True) + norm_eps)
    normed = (residual * inv_rms * gain).astype(bf16)
    inner_part = dot(normed, w_inner, ((2,), (0,)))
    conv_pre = jnp.zeros_like(inner_part) + conv_bias
    moved_list = []
    for k in range(KCONV):
        moved = jnp.where(masks[k], shift_down(inner_part, KCONV - 1 - k), 0.0)
        moved_list.append(moved)
        conv_pre = conv_pre + taps[:, k] * moved
    conv_out = jax.nn.silu(conv_pre).astype(bf16)
    conv_f = conv_out.astype(f32)
    projected = net.scatter_plane(dot(conv_out, w_x, ((2,), (0,))), f32)
    projected = net.gather_plane(projected)
    dt_in = projected[:, :, :RANK].astype(bf16)
    bc = to_chunks(projected[:, :, RANK:])
    dt_pre = dot(dt_in, w_dt, ((2,), (1,))) + dt_bias
    step_size = jax.nn.softplus(dt_pre)
    scanned, starts = scan_forward(step_size, cut, conv_out, bc, rate_tiles)

    gate_part = dot(normed, w_gate, ((2,), (0,)))
    mixer_y = scanned + skip * conv_f
    gate_act = jax.nn.silu(gate_part)
    mixed = (mixer_y * gate_act).astype(bf16)
    out_part = dot(mixed, w_out, ((2,), (0,)))
    layer_output = (hidden[0].astype(f32) + net.scatter_plane(out_part, bf16)).astype(bf16)

    grad_out = dot(mixed.reshape(-1, width), upstream.reshape(-1, model), ((0,), (0,)))
    grad_mixed = dot(upstream, w_out, ((2,), (1,)))
    grad_y = grad_mixed * gate_act
    grad_gate = (grad_mixed * mixer_y * silu_slope(gate_part)).astype(bf16)
    grad_skip = jnp.sum(grad_y * conv_f, axis=(0, 1))
    flat_normed = normed.reshape(-1, model)
    gin_gate = dot(flat_normed, grad_gate.reshape(-1, width), ((0,), (0,)))

    grad_step, grad_conv, grad_bc, grad_rates = scan_backward(
        step_size, cut, conv_out, bc, rate_tiles, starts, grad_y
    )
    grad_rates = jnp.sum(grad_rates, axis=1).T
    grad_conv = grad_conv + skip * grad_y
    grad_dtpre = grad_step * jax.nn.sigmoid(dt_pre)
    grad_dtbias = jnp.sum(grad_dtpre, axis=(0, 1))
    grad_dtlow = grad_dtpre.astype(bf16)
    grad_dt = dot(grad_dtlow.reshape(-1, width), dt_in.reshape(-1, RANK), ((0,), (0,)))
    grad_dtin = dot(grad_dtlow, w_dt, ((2,), (0,)))
    proj_part = jnp.concatenate([grad_dtin, from_chunks(grad_bc)], axis=2)
    grad_proj = net.gather_plane(net.scatter_plane(proj_part, f32).astype(bf16))
    grad_x = dot(conv_out.reshape(-1, width), grad_proj.reshape(-1, xcols), ((0,), (0,)))
    grad_conv = grad_conv + dot(grad_proj, w_x, ((2,), (1,)))
    grad_pre = grad_conv * silu_slope(conv_pre)
    grad_inner = jnp.zeros_like(grad_pre)
    tap_grads = []
    for k in range(KCONV):
        tap_grads.append(jnp.sum(grad_pre * moved_list[k], axis=(0, 1)))
        masked = jnp.where(masks[k], grad_pre, 0.0)
        grad_inner = grad_inner + taps[:, k] * shift_up(masked, KCONV - 1 - k)
    grad_convbias = jnp.sum(grad_pre, axis=(0, 1))
    grad_inner = grad_inner.astype(bf16)
    gin_inner = dot(flat_normed, grad_inner.reshape(-1, width), ((0,), (0,)))
    normed_part = dot(grad_inner, w_inner, ((2,), (1,))) + dot(grad_gate, w_gate, ((2,), (1,)))
    grad_gain = jnp.sum(normed_part * residual * inv_rms, axis=(0, 1))
    grad_normed = net.scatter_plane(normed_part, bf16)
    own_res, own_inv = residual[0], inv_rms[0]
    grad_scaled = grad_normed * gain
    input_grad = (
        own_inv * grad_scaled
        - own_res * own_inv**3 * jnp.mean(grad_scaled * own_res, axis=1, keepdims=True)
        + cotangent[0].astype(f32)
    ).astype(bf16)

    def full_in(gin):
        rows = net.scatter_z(gin, bf16).astype(bf16).reshape(2, in_rows, width)
        own = lax.dynamic_index_in_dim(rows, c, 0, keepdims=False)
        other = net.core(lax.dynamic_index_in_dim(rows, 1 - c, 0, keepdims=False))
        cols = net.pair_rows(own, other).reshape(2, in_rows, planes, sub)
        every = net.order_reps(net.gather_rep(cols.transpose(1, 2, 0, 3)))
        return every.transpose(1, 2, 3, 0, 4).reshape(in_rows, 2 * width * reps)

    out_sum = net.order_reps(net.gather_rep(net.scatter_z(grad_out, bf16).astype(bf16)))
    out_sum = out_sum.reshape(own_chan, model).astype(f32)
    in_sum = jnp.concatenate([full_in(gin_inner), full_in(gin_gate)], axis=1).astype(f32)
    grad_small = jnp.concatenate(
        [
            grad_x,
            grad_dt,
            jnp.stack(tap_grads, axis=1),
            grad_rates * rates,
            grad_convbias[:, None],
            grad_dtbias[:, None],
            grad_skip[:, None],
            grad_gain.reshape(width, reps),
        ],
        axis=1,
    )
    small_sum = net.order_reps(net.gather_rep(net.scatter_z(grad_small, f32)))
    gain_two = jnp.sum(small_sum[:, :, xcols + RANK + chan_cols :], axis=0).reshape(2, in_rows)
    gain_own = lax.dynamic_index_in_dim(gain_two, c, 0, keepdims=False)
    gain_sum = gain_own + net.core(lax.dynamic_index_in_dim(gain_two, 1 - c, 0, keepdims=False))
    small_sum = small_sum.reshape(own_chan, -1)
    x_sum = small_sum[:, :xcols]
    dt_sum = small_sum[:, xcols : xcols + RANK]
    chan_sum = small_sum[:, xcols + RANK : xcols + RANK + chan_cols]

    moments = (
        (in_master, in_first, in_second, in_sum),
        (x_master, x_first, x_second, x_sum),
        (dt_master, dt_first, dt_second, dt_sum),
        (out_master, out_first, out_second, out_sum),
        (chan_master, chan_first, chan_second, chan_sum),
        (gain_master, gain_first, gain_second, gain_sum),
    )
    updated = []
    for position, (master, first, second, gradient) in enumerate(moments):
        updated += adam_step(master, first, second, gradient, learn_rates[position], with_decay[position])
    return (layer_output[None], input_grad[None], *updated)


def solution(mesh):
    token = P(("rep", "shard"), None, None)
    rows = P("shard", None)
    placed = (token, P(("rep", "shard"), None), token) + (rows,) * 15 + (P("shard"),) * 3
    return jax.shard_map(
        functools.partial(shards, mesh.shape["rep"], mesh.shape["shard"]),
        mesh=mesh,
        in_specs=placed,
        out_specs=(token, token) + (rows,) * 15 + (P("shard"),) * 3,
        check_vma=False,
    )
```

```python
import functools

import jax
import jax.numpy as jnp
from jax import lax
from jax.experimental import pallas as pl
from jax.experimental.pallas import tpu as pltpu
from jax.sharding import PartitionSpec as P

NSTATE = 16
RANK = 128
KCONV = 4
ADAM_STEP = 10
CHUNK = 32
LANES = 128
SUBS = 8
CUT = 1e30
MASKS = 8
FWD_UNROLL = 8
BWD_UNROLL = 4
LOG2E = 1.4426950408889634

norm_eps = 1e-05
beta_first = 0.9
beta_second = 0.95
adam_eps = 1e-08
weight_decay = 0.1
learn_rates = (0.044, 0.03, 0.18, 0.09, 1.0, 0.6)
with_decay = (True, True, True, True, False, False)

bf16 = jnp.bfloat16
f32 = jnp.float32
PARTS = bf16


def silu_slope(values):
    sigma = jax.nn.sigmoid(values)
    return sigma * (1.0 + values * (1.0 - sigma))


def dot(a, b, dims):
    return lax.dot_general(a, b, (dims, ((), ())), preferred_element_type=f32)


def expand_inputs(bc_ref, bx, sb):
    rows = 2 * NSTATE * SUBS
    v = bc_ref[0, :, pl.ds(sb * SUBS, SUBS), :].reshape(rows, CHUNK)
    high = v.astype(bf16)
    rest = v - high.astype(f32)
    middle = rest.astype(bf16)
    low = (rest - middle.astype(f32)).astype(bf16)
    pieces = jnp.concatenate([high, middle, low], axis=1)
    token = lax.broadcasted_iota(jnp.int32, (3 * CHUNK, LANES), 0) % CHUNK
    for t in range(CHUNK):
        bx[t] = dot(pieces, (token == t).astype(bf16), ((1,), (0,))).reshape(2 * NSTATE, SUBS, LANES)


def lane_sums(acc, gbc_ref, sb):
    rows = 2 * NSTATE * SUBS
    ones = jnp.ones((SUBS, 2 * LANES), bf16)
    for t in range(CHUNK):
        v = acc[t].reshape(rows, LANES)
        high = v.astype(bf16)
        low = (v - high.astype(f32)).astype(bf16)
        sums = dot(ones, jnp.concatenate([high, low], axis=1), ((1,), (1,)))
        gbc_ref[sb, pl.ds(t, 1), :] = sums[:1]


def spread(scratch, q, values):
    for g in range(scratch.shape[0]):
        scratch[g, pl.ds(q * CHUNK, CHUNK), :] = values[:, g * LANES : (g + 1) * LANES]


def collect(ref, q, scratch):
    for g in range(scratch.shape[0]):
        ref[q, :, pl.ds(g * LANES, LANES)] = scratch[g, pl.ds(q * CHUNK, CHUNK), :]


def tree(values):
    while len(values) > 1:
        values = [a + b for a, b in zip(values[::2], values[1::2])]
    return values[0]


def softplus(v):
    return jnp.maximum(v, 0.0) + jnp.log1p(jnp.exp(-jnp.abs(v)))


def dt_products(dt_ref, wdt_ref, chan_ref, q):
    return dot(dt_ref[q], wdt_ref[...], ((1,), (1,))) + chan_ref[pl.ds(KCONV + NSTATE + 1, 1), :]


def scan_fwd_kernel(
    dt_ref, mask_ref, conv_ref, bc_ref, rate_ref, wdt_ref, chan_ref, y_ref, starts_ref, state, bx, stepm, drive, ys
):
    seqs = dt_ref.shape[0]
    width = conv_ref.shape[2]

    @pl.when(pl.program_id(0) == 0)
    def _():
        state[...] = jnp.zeros_like(state)

    starts_ref[0] = state[...]
    for q in range(seqs):
        step = softplus(dt_products(dt_ref, wdt_ref, chan_ref, q))
        spread(stepm, q, step + mask_ref[q, :, pl.ds(KCONV - 1, 1)])
        spread(drive, q, step * conv_ref[q].astype(f32))
    for sb in range(seqs // SUBS):
        expand_inputs(bc_ref, bx, sb)
        sub = pl.ds(sb * SUBS, SUBS)

        def group(g, carry):
            lanes = pl.ds(pl.multiple_of(g * LANES, LANES), LANES)
            rates = [rate_ref[n, :, lanes] * LOG2E for n in range(NSTATE)]

            def token(t, st):
                rows = pl.ds(sb * SUBS * CHUNK + t, SUBS, stride=CHUNK)
                sm = stepm[g, rows, :]
                dx = drive[g, rows, :]
                parts = []
                out = []
                for n in range(NSTATE):
                    dec = jnp.exp2(sm * rates[n])
                    s_n = dec * st[n] + dx * bx[t, n]
                    out.append(s_n)
                    parts.append(s_n * bx[t, NSTATE + n])
                ys[g, rows, :] = tree(parts)
                return tuple(out)

            st = tuple(state[n, sub, lanes] for n in range(NSTATE))
            st = lax.fori_loop(0, CHUNK, token, st, unroll=FWD_UNROLL)
            for n in range(NSTATE):
                state[n, sub, lanes] = st[n]
            return carry

        lax.fori_loop(0, width // LANES, group, 0)
    for q in range(seqs):
        collect(y_ref, q, ys)


def scan_bwd_kernel(
    dt_ref, mask_ref, conv_ref, bc_ref, rate_ref, wdt_ref, chan_ref, starts_ref, gy_ref,
    gconv_ref, glow_ref, gdtin_ref, gbc_ref, grate_ref, gbias_ref,
    flow, bx, stepm, step2, conv2, gy2, gs2, gc2, dec_s, pri_s, acc,
):
    seqs = dt_ref.shape[0]
    width = conv_ref.shape[2]

    @pl.when(pl.program_id(0) == 0)
    def _():
        flow[...] = jnp.zeros_like(flow)
        grate_ref[...] = jnp.zeros_like(grate_ref)
        gbias_ref[...] = jnp.zeros_like(gbias_ref)

    for q in range(seqs):
        step = softplus(dt_products(dt_ref, wdt_ref, chan_ref, q))
        spread(step2, q, step)
        spread(stepm, q, step + mask_ref[q, :, pl.ds(KCONV - 1, 1)])
        spread(conv2, q, conv_ref[q].astype(f32))
        spread(gy2, q, gy_ref[q])
    for sb in range(seqs // SUBS):
        expand_inputs(bc_ref, bx, sb)
        sub = pl.ds(sb * SUBS, SUBS)
        acc[...] = jnp.zeros_like(acc)

        def group(g, carry):
            lanes = pl.ds(pl.multiple_of(g * LANES, LANES), LANES)

            def token_f(t, st):
                rows = pl.ds(sb * SUBS * CHUNK + t, SUBS, stride=CHUNK)
                sm = stepm[g, rows, :]
                dx = step2[g, rows, :] * conv2[g, rows, :]
                out = []
                for n in range(NSTATE):
                    dec = jnp.exp2(sm * (rate_ref[n, :, lanes] * LOG2E))
                    dec_s[t, n] = dec
                    pri_s[t, n] = st[n]
                    out.append(dec * st[n] + dx * bx[t, n])
                return tuple(out)

            st = tuple(starts_ref[0, n, sub, lanes] for n in range(NSTATE))
            st = lax.fori_loop(0, CHUNK, token_f, st, unroll=FWD_UNROLL)
            for n in range(NSTATE):
                pri_s[CHUNK, n] = st[n]

            def token_b(i, carried):
                t = CHUNK - 1 - i
                fl, ga = carried
                rows = pl.ds(sb * SUBS * CHUNK + t, SUBS, stride=CHUNK)
                size = step2[g, rows, :]
                conv = conv2[g, rows, :]
                gy = gy2[g, rows, :]
                dx = size * conv
                along, gsz = [], []
                nfl, nga = [], []
                for n in range(NSTATE):
                    grad = gy * bx[t, NSTATE + n] + fl[n]
                    dg = dec_s[t, n] * grad
                    th = dg * pri_s[t, n]
                    along.append(grad * bx[t, n])
                    gsz.append(th * rate_ref[n, :, lanes])
                    acc[t, n] += grad * dx
                    acc[t, NSTATE + n] += pri_s[t + 1, n] * gy
                    nfl.append(dg)
                    nga.append(ga[n] + th * size)
                along = tree(along)
                gs2[g, rows, :] = tree(gsz) + conv * along
                gc2[g, rows, :] = size * along
                return (tuple(nfl), tuple(nga))

            fl = tuple(flow[n, sub, lanes] for n in range(NSTATE))
            ga = tuple(grate_ref[n, :, lanes] for n in range(NSTATE))
            fl, ga = lax.fori_loop(0, CHUNK, token_b, (fl, ga), unroll=BWD_UNROLL)
            for n in range(NSTATE):
                flow[n, sub, lanes] = fl[n]
                grate_ref[n, :, lanes] = ga[n]
            return carry

        lax.fori_loop(0, width // LANES, group, 0)
        lane_sums(acc, gbc_ref, sb)
    skip = chan_ref[pl.ds(KCONV + NSTATE + 2, 1), :]
    for q in range(seqs):
        collect(gconv_ref, q, gc2)
        gconv_ref[q] += skip * gy_ref[q]
        gstep = jnp.concatenate([gs2[g, pl.ds(q * CHUNK, CHUNK), :] for g in range(width // LANES)], axis=1)
        grad = gstep * jax.nn.sigmoid(dt_products(dt_ref, wdt_ref, chan_ref, q))
        gbias_ref[...] += jnp.sum(grad.reshape(CHUNK // SUBS, SUBS, width), axis=0)
        low = grad.astype(bf16)
        glow_ref[q] = low
        gdtin_ref[q] = dot(low, wdt_ref[...], ((1,), (0,)))


def whole(shape):
    return pl.BlockSpec(shape, lambda i, *_: (0,) * len(shape))


def scan_specs(seqs, width, chan_cols, chunk_of):
    def tokens(columns):
        return pl.BlockSpec((seqs, CHUNK, columns), lambda i: (0, chunk_of(i), 0))

    bcs = pl.BlockSpec((1, 2 * NSTATE, seqs, CHUNK), lambda i: (chunk_of(i), 0, 0, 0))
    starts = pl.BlockSpec((1, NSTATE, seqs, width), lambda i: (chunk_of(i), 0, 0, 0))
    sums = pl.BlockSpec((seqs // SUBS, CHUNK, 2 * NSTATE * SUBS), lambda i: (0, chunk_of(i), 0))
    ins = [
        tokens(RANK), tokens(MASKS), tokens(width), bcs,
        whole((NSTATE, SUBS, width)), whole((width, RANK)), whole((chan_cols, width)),
    ]
    return tokens, starts, sums, ins


def scan_forward(dt_in, masks, conv, bc, rates, w_dt, chan):
    seqs, length, width = conv.shape
    chunks = length // CHUNK
    tokens, starts, _, ins = scan_specs(seqs, width, chan.shape[0], lambda i: i)
    tall = pltpu.VMEM((width // LANES, seqs * CHUNK, LANES), f32)
    return pl.pallas_call(
        scan_fwd_kernel,
        grid=(chunks,),
        in_specs=ins,
        out_specs=[tokens(width), starts],
        out_shape=[
            jax.ShapeDtypeStruct(conv.shape, f32),
            jax.ShapeDtypeStruct((chunks, NSTATE, seqs, width), f32),
        ],
        scratch_shapes=[
            pltpu.VMEM((NSTATE, seqs, width), f32),
            pltpu.VMEM((CHUNK, 2 * NSTATE, SUBS, LANES), f32),
            tall, tall, tall,
        ],
        compiler_params=pltpu.CompilerParams(vmem_limit_bytes=50 * 2**20),
        cost_estimate=pl.CostEstimate(
            flops=8 * conv.size * NSTATE, bytes_accessed=100 * 10**6, transcendentals=conv.size * NSTATE
        ),
        name="scan_forward",
    )(dt_in, masks, conv, bc, rates, w_dt, chan)


def scan_backward(dt_in, masks, conv, bc, rates, w_dt, chan, starts, grad_y):
    seqs, length, width = conv.shape
    chunks = length // CHUNK
    tokens, start_spec, sums, ins = scan_specs(seqs, width, chan.shape[0], lambda i: chunks - 1 - i)
    tall = pltpu.VMEM((width // LANES, seqs * CHUNK, LANES), f32)
    return pl.pallas_call(
        scan_bwd_kernel,
        grid=(chunks,),
        in_specs=ins + [start_spec, tokens(width)],
        out_specs=[
            tokens(width), tokens(width), tokens(RANK), sums,
            whole((NSTATE, SUBS, width)), whole((SUBS, width)),
        ],
        out_shape=[
            jax.ShapeDtypeStruct(conv.shape, f32),
            jax.ShapeDtypeStruct(conv.shape, bf16),
            jax.ShapeDtypeStruct((seqs, length, RANK), f32),
            jax.ShapeDtypeStruct((seqs // SUBS, length, 2 * NSTATE * SUBS), f32),
            jax.ShapeDtypeStruct((NSTATE, SUBS, width), f32),
            jax.ShapeDtypeStruct((SUBS, width), f32),
        ],
        scratch_shapes=[
            pltpu.VMEM((NSTATE, seqs, width), f32),
            pltpu.VMEM((CHUNK, 2 * NSTATE, SUBS, LANES), f32),
            tall, tall, tall, tall, tall, tall,
            pltpu.VMEM((CHUNK, NSTATE, SUBS, LANES), f32),
            pltpu.VMEM((CHUNK + 1, NSTATE, SUBS, LANES), f32),
            pltpu.VMEM((CHUNK, 2 * NSTATE, SUBS, LANES), f32),
        ],
        compiler_params=pltpu.CompilerParams(vmem_limit_bytes=56 * 2**20),
        cost_estimate=pl.CostEstimate(
            flops=24 * conv.size * NSTATE, bytes_accessed=300 * 10**6, transcendentals=conv.size * NSTATE
        ),
        name="scan_backward",
    )(dt_in, masks, conv, bc, rates, w_dt, chan, starts, grad_y)


def put_blocks(place_ref, blocks, out):
    @pl.when(pl.program_id(0) == 0)
    def _():
        for k, block in enumerate(blocks):
            rows = block.shape[0]
            out[pl.ds(pl.multiple_of((place_ref[2] ^ k) * rows, rows), rows), :] = block[...]


def normalised(hid):
    residual = hid.astype(f32)
    return residual * lax.rsqrt(jnp.mean(residual * residual, axis=1, keepdims=True) + norm_eps)


def earlier_rows(inner, masks):
    terms = []
    for k in range(KCONV - 1):
        terms.append(pltpu.roll(inner, KCONV - 1 - k, 0) * masks[:, k : k + 1])
    return terms + [inner]


def conv_sum(terms, chan_ref):
    total = chan_ref[pl.ds(KCONV + NSTATE, 1), :]
    for k, term in enumerate(terms):
        total = total + chan_ref[pl.ds(k, 1), :] * term
    return total


def put_columns(ref, start, values):
    count = values.shape[0]
    for i in range(values.shape[1] // LANES):
        ref[0, pl.ds(start + i * count, count), :] = values[:, i * LANES : (i + 1) * LANES]


def front_kernel(planes, place_ref, hid_ref, gain_ref, mask_ref, chan_ref, wx_ref, wbc_ref, *refs):
    blocks = refs[:planes]
    normed_ref, inner_ref, conv_ref, proj_ref, weights = refs[planes:]
    put_blocks(place_ref, blocks, weights)
    normed = (normalised(hid_ref[0]) * gain_ref[...]).astype(bf16)
    normed_ref[0] = normed
    inner = dot(normed, weights[...], ((1,), (0,)))
    inner_ref[0] = inner
    pre = conv_sum(earlier_rows(inner, mask_ref[0]), chan_ref)
    conv = jax.nn.silu(pre).astype(bf16)
    conv_ref[0] = conv
    length = conv.shape[0]
    proj_ref[0, pl.ds(0, length), :] = dot(conv, wx_ref[...], ((1,), (1,)))
    put_columns(proj_ref, length, dot(wbc_ref[...], conv, ((1,), (1,))))


def per_sequence(kernel, place, stacked, fixed, outs, scratch, flops, name):
    seqs = stacked[0].shape[0]

    def block(shape):
        return pl.BlockSpec((1,) + tuple(shape[1:]), lambda i, p: (i, 0, 0))

    return pl.pallas_call(
        kernel,
        grid_spec=pltpu.PrefetchScalarGridSpec(
            num_scalar_prefetch=1,
            grid=(seqs,),
            in_specs=[block(v.shape) for v in stacked] + [whole(v.shape) for v in fixed],
            out_specs=[block(shape) if per else whole(shape) for shape, _, per in outs],
            scratch_shapes=scratch,
        ),
        out_shape=[jax.ShapeDtypeStruct(shape, kind) for shape, kind, _ in outs],
        compiler_params=pltpu.CompilerParams(vmem_limit_bytes=56 * 2**20),
        cost_estimate=pl.CostEstimate(flops=flops, bytes_accessed=40 * 10**6, transcendentals=0),
        name=name,
    )(place, *stacked, *fixed)


def front(place, hidden_all, gain, masks, chan, w_xdt, w_xbc, inner_blocks):
    seqs, length, model = hidden_all.shape
    width = w_xbc.shape[1]
    packed = length + 2 * NSTATE * length // LANES

    def kernel(place_ref, hid, mask, gain_ref, chan_ref, wx, wbc, *refs):
        front_kernel(len(inner_blocks), place_ref, hid, gain_ref, mask, chan_ref, wx, wbc, *refs)

    return per_sequence(
        kernel,
        place,
        [hidden_all, masks],
        [gain, chan, w_xdt, w_xbc, *inner_blocks],
        [
            ((seqs, length, model), bf16, True),
            ((seqs, length, width), f32, True),
            ((seqs, length, width), bf16, True),
            ((seqs, packed, RANK), f32, True),
        ],
        [pltpu.VMEM((model, width), bf16)],
        2 * seqs * length * model * width,
        "front",
    )


def middle(place, normed, upstream, scanned, conv_out, chan, gate_blocks, out_blocks):
    seqs, length, model = normed.shape
    width = conv_out.shape[2]
    planes = len(gate_blocks)

    def kernel(place_ref, normed_ref, up_ref, y_ref, conv_ref, chan_ref, *refs):
        gates, outs = refs[:planes], refs[planes : 2 * planes]
        part_ref, mixed_ref, gy_ref, ggate_ref, gskip_ref, w_gate, w_out = refs[2 * planes :]
        put_blocks(place_ref, gates, w_gate)
        put_blocks(place_ref, outs, w_out)

        @pl.when(pl.program_id(0) == 0)
        def _():
            gskip_ref[...] = jnp.zeros_like(gskip_ref)

        gate = dot(normed_ref[0], w_gate[...], ((1,), (0,)))
        conv = conv_ref[0].astype(f32)
        sigma = jax.nn.sigmoid(gate)
        act = gate * sigma
        mixer = y_ref[0] + chan_ref[pl.ds(KCONV + NSTATE + 2, 1), :] * conv
        mixed = (mixer * act).astype(bf16)
        mixed_ref[0] = mixed
        part_ref[0] = dot(mixed, w_out[...], ((1,), (0,))).astype(part_ref.dtype)
        grad_mixed = dot(up_ref[0], w_out[...], ((1,), (1,)))
        gy = grad_mixed * act
        gy_ref[0] = gy
        ggate_ref[0] = (grad_mixed * mixer * (sigma * (1.0 + gate * (1.0 - sigma)))).astype(bf16)
        gskip_ref[...] += jnp.sum((gy * conv).reshape(length // SUBS, SUBS, width), axis=0)

    return per_sequence(
        kernel,
        place,
        [normed, upstream, scanned, conv_out],
        [chan, *gate_blocks, *out_blocks],
        [
            ((seqs, length, model), PARTS, True),
            ((seqs, length, width), bf16, True),
            ((seqs, length, width), f32, True),
            ((seqs, length, width), bf16, True),
            ((SUBS, width), f32, False),
        ],
        [pltpu.VMEM((model, width), bf16), pltpu.VMEM((width, model), bf16)],
        6 * seqs * length * model * width,
        "middle",
    )


def back_conv(place, grad_conv, gp_dt, gp_bc, inner, masks, chan, w_xdt, w_xbc):
    seqs, length, width = grad_conv.shape

    def kernel(place_ref, gconv_ref, gdt_ref, gbc_ref, inner_ref, mask_ref, chan_ref, wx_ref, wbc_ref, ginner_ref, sums_ref):
        @pl.when(pl.program_id(0) == 0)
        def _():
            sums_ref[...] = jnp.zeros_like(sums_ref)

        masks_now = mask_ref[0]
        terms = earlier_rows(inner_ref[0], masks_now)
        pre = conv_sum(terms, chan_ref)
        total = gconv_ref[0] + dot(gdt_ref[0], wx_ref[...], ((1,), (0,)))
        total = total + dot(gbc_ref[0], wbc_ref[...], ((0,), (0,)))
        grad = total * silu_slope(pre)
        for k in range(KCONV):
            sums_ref[k] += jnp.sum((grad * terms[k]).reshape(length // SUBS, SUBS, width), axis=0)
        sums_ref[KCONV] += jnp.sum(grad.reshape(length // SUBS, SUBS, width), axis=0)
        ginner = chan_ref[pl.ds(KCONV - 1, 1), :] * grad
        for k in range(KCONV - 1):
            moved = pltpu.roll(grad * masks_now[:, k : k + 1], length - (KCONV - 1 - k), 0)
            ginner = ginner + chan_ref[pl.ds(k, 1), :] * moved
        ginner_ref[0] = ginner.astype(bf16)

    return per_sequence(
        kernel,
        place,
        [grad_conv, gp_dt, gp_bc, inner, masks],
        [chan, w_xdt, w_xbc],
        [((seqs, length, width), bf16, True), ((KCONV + 1, SUBS, width), f32, False)],
        [],
        2 * seqs * length * width * RANK,
        "back_conv",
    )


def back_normed(place, grad_inner, grad_gate, hidden_all, inner_blocks, gate_blocks):
    seqs, length, width = grad_inner.shape
    model = hidden_all.shape[2]
    planes = len(gate_blocks)

    def kernel(place_ref, ginner_ref, ggate_ref, hid_ref, *refs):
        inners, gates = refs[:planes], refs[planes : 2 * planes]
        part_ref, ggain_ref, w_inner, w_gate = refs[2 * planes :]
        put_blocks(place_ref, inners, w_inner)
        put_blocks(place_ref, gates, w_gate)

        @pl.when(pl.program_id(0) == 0)
        def _():
            ggain_ref[...] = jnp.zeros_like(ggain_ref)

        part = dot(ginner_ref[0], w_inner[...], ((1,), (1,))) + dot(ggate_ref[0], w_gate[...], ((1,), (1,)))
        part_ref[0] = part.astype(part_ref.dtype)
        ggain_ref[...] += jnp.sum((part * normalised(hid_ref[0])).reshape(length // SUBS, SUBS, model), axis=0)

    return per_sequence(
        kernel,
        place,
        [grad_inner, grad_gate, hidden_all],
        [*inner_blocks, *gate_blocks],
        [((seqs, length, model), PARTS, True), ((SUBS, model), f32, False)],
        [pltpu.VMEM((model, width), bf16), pltpu.VMEM((model, width), bf16)],
        4 * seqs * length * model * width,
        "back_normed",
    )


MESH = pl.DeviceIdType.MESH


class Peers:
    def __init__(self):
        self.r = lax.axis_index("rep")
        shard = lax.axis_index("shard")
        self.z, self.c = shard // 2, shard % 2

    @staticmethod
    def flip(i, k):
        return (i, i + 1 - 2 * (i % 2), (i + 2) % 4, 3 - i)[k]

    def rep(self, k):
        return {"rep": self.flip(self.r, k)}

    def plane(self, k):
        return {"shard": 2 * self.flip(self.z, k) + self.c}

    def core(self):
        return {"shard": 2 * self.z + 1 - self.c}

    def greet(self, planes):
        devices = [self.core()] + [self.rep(k) for k in (1, 2, 3)]
        if planes:
            devices += [self.plane(k) for k in (1, 2, 3)]
        barrier = pltpu.get_barrier_semaphore()
        for device in devices:
            pl.semaphore_signal(barrier, inc=1, device_id=device, device_id_type=MESH)
        pl.semaphore_wait(barrier, len(devices))


class Sends:
    def __init__(self, send_sems, recv_sems):
        self.send_sems, self.recv_sems = send_sems, recv_sems
        self.made = {}

    def make(self, slot, source, target, device):
        copy = pltpu.make_async_remote_copy(
            src_ref=source,
            dst_ref=target,
            send_sem=self.send_sems.at[slot],
            recv_sem=self.recv_sems.at[slot],
            device_id=device,
            device_id_type=MESH,
        )
        self.made[slot] = copy
        return copy

    def start(self, slot, source, target, device):
        self.make(slot, source, target, device).start()

    def arrived(self, *slots):
        for slot in slots:
            self.made[slot].wait_recv()

    def sent(self, *slots):
        for slot in slots:
            self.made[slot].wait_send()


def gather_first_kernel(
    hid, in_own, in_other, small, gain, ids, hid_all, weights, small_all, gain_all, ids_all, send_sems, recv_sems, local_sems
):
    me = Peers()
    net = Sends(send_sems, recv_sems)
    rows = in_own.shape[0]
    half = hid.shape[0] // 2
    low, high = pl.ds(0, half), pl.ds(half, half)
    inside = (me.z == 1) | (me.z == 2)
    outside = (me.z == 0) | (me.z == 3)
    mine = pl.ds(pl.multiple_of(me.c * rows, rows), rows)
    local = [
        pltpu.make_async_copy(source, target, local_sems.at[i])
        for i, (source, target) in enumerate(
            [
                (in_own, weights.at[0, mine]),
                (hid, hid_all.at[0]),
                (small, small_all.at[0]),
                (gain, gain_all.at[0]),
                (ids, ids_all.at[0]),
            ]
        )
    ]
    for copy in local:
        copy.start()
    me.greet(True)
    net.start(0, in_other, weights.at[0, mine], me.core())
    for k in (1, 2, 3):
        net.start(k, ids, ids_all.at[k], me.rep(k))
        net.start(3 + k, gain, gain_all.at[k], me.plane(k))
        net.start(6 + k, small, small_all.at[k], me.plane(k))
    net.start(10, hid.at[high], hid_all.at[1, high], me.rep(1))
    net.start(11, hid.at[low], hid_all.at[2, low], me.rep(2))
    net.start(12, hid.at[low], hid_all.at[1, low], me.rep(1))
    net.start(13, hid.at[high], hid_all.at[2, high], me.rep(2))
    net.start(14, hid, hid_all.at[4], me.core())
    local[0].wait()
    net.arrived(0)
    own = weights.at[0]
    net.start(15, own, weights.at[2], me.plane(2))
    net.start(16, own, weights.at[1], me.plane(1))
    across = net.make(17, own, weights.at[3], me.plane(3))
    local[3].wait()
    local[4].wait()
    net.arrived(1, 2, 3, 4, 5, 6)
    net.start(18, ids_all.at[pl.ds(0, 4)], ids_all.at[pl.ds(4, 4)], me.core())
    net.start(19, gain_all.at[pl.ds(0, 4)], gain_all.at[pl.ds(4, 4)], me.core())
    net.arrived(10, 11)
    net.start(20, hid_all.at[1, high], hid_all.at[3, high], me.rep(2))
    net.start(21, hid_all.at[2, low], hid_all.at[3, low], me.rep(1))
    net.arrived(12)
    net.start(22, hid_all.at[1], hid_all.at[5], me.core())
    net.arrived(13)
    net.start(23, hid_all.at[2], hid_all.at[6], me.core())
    net.arrived(15)
    onward = net.make(24, weights.at[2], weights.at[3], me.plane(1))

    @pl.when(inside)
    def _():
        across.start()
        onward.start()

    net.arrived(20, 21)
    net.start(25, hid_all.at[3], hid_all.at[7], me.core())
    net.arrived(16)

    @pl.when(inside)
    def _():
        across.wait_recv()

    @pl.when(outside)
    def _():
        onward.wait_recv()

    net.arrived(7, 8, 9, 14, 18, 19, 22, 23, 25)
    local[1].wait()
    local[2].wait()
    net.sent(*[slot for slot in net.made if slot not in (17, 24)])

    @pl.when(inside)
    def _():
        across.wait_send()
        onward.wait_send()


def gather_first(hid, in_own, in_other, small, gain, ids):
    length, model = hid.shape
    anywhere = pl.BlockSpec(memory_space=pl.ANY)
    return pl.pallas_call(
        gather_first_kernel,
        in_specs=[anywhere] * 6,
        out_specs=[anywhere] * 5,
        out_shape=[
            jax.ShapeDtypeStruct((8, length, model), bf16),
            jax.ShapeDtypeStruct((4, 2 * in_own.shape[0], in_own.shape[1]), bf16),
            jax.ShapeDtypeStruct((4,) + small.shape, bf16),
            jax.ShapeDtypeStruct((8,) + gain.shape, f32),
            jax.ShapeDtypeStruct((8,) + ids.shape, f32),
        ],
        scratch_shapes=[
            pltpu.SemaphoreType.DMA((26,)),
            pltpu.SemaphoreType.DMA((26,)),
            pltpu.SemaphoreType.DMA((5,)),
        ],
        compiler_params=pltpu.CompilerParams(collective_id=1, has_side_effects=True),
        cost_estimate=pl.CostEstimate(flops=0, bytes_accessed=100 * 10**6, transcendentals=0),
        name="gather_first",
    )(hid, in_own, in_other, small, gain, ids)


def reduce_plane_kernel(part, dt_all, bc_all, near, pair, far, send_sems, recv_sems):
    me = Peers()
    net = Sends(send_sems, recv_sems)
    tokens = dt_all.shape[1]
    me.greet(False)
    for k in (1, 2, 3, 0):
        net.start(k, part.at[4 + k], near.at[k], me.core())
    for k in (1, 2, 3):
        net.arrived(k)
        pair[k - 1] = part[k] + near[k]
        net.start(3 + k, pair.at[k - 1], far.at[k - 1], me.rep(k))
    net.arrived(0)
    total = part[0] + near[0]
    for k in (1, 2, 3):
        net.arrived(3 + k)
        total = total + far[k - 1]
    dt_all[0] = total[:tokens].astype(bf16)
    bc_all[0] = total[tokens:]
    for k in (1, 2, 3):
        net.start(6 + k, dt_all.at[0], dt_all.at[k], me.rep(k))
        net.start(9 + k, bc_all.at[0], bc_all.at[k], me.rep(k))
    net.start(13, dt_all.at[0], dt_all.at[4], me.core())
    net.start(14, bc_all.at[0], bc_all.at[4], me.core())
    for k in (1, 2, 3):
        net.arrived(6 + k, 9 + k)
        net.start(14 + k, dt_all.at[k], dt_all.at[4 + k], me.core())
        net.start(17 + k, bc_all.at[k], bc_all.at[4 + k], me.core())
    net.arrived(13, 14, 15, 16, 17, 18, 19, 20)
    net.sent(*net.made)


def reduce_plane(part, collective):
    seqs, rows, _ = part.shape
    tokens = rows - 2 * 2 * NSTATE
    vmem = pl.BlockSpec(memory_space=pltpu.VMEM)
    return pl.pallas_call(
        reduce_plane_kernel,
        in_specs=[vmem],
        out_specs=[vmem, vmem],
        out_shape=[
            jax.ShapeDtypeStruct((seqs, tokens, RANK), bf16),
            jax.ShapeDtypeStruct((seqs, rows - tokens, RANK), f32),
        ],
        scratch_shapes=[
            pltpu.VMEM((4, rows, RANK), f32),
            pltpu.VMEM((3, rows, RANK), f32),
            pltpu.VMEM((3, rows, RANK), f32),
            pltpu.SemaphoreType.DMA((21,)),
            pltpu.SemaphoreType.DMA((21,)),
        ],
        compiler_params=pltpu.CompilerParams(
            collective_id=collective, has_side_effects=True, vmem_limit_bytes=16 * 2**20
        ),
        cost_estimate=pl.CostEstimate(flops=0, bytes_accessed=50 * 10**6, transcendentals=0),
        name="reduce_plane",
    )(part)


def finish_kernel(
    part, gin, small, grad_normed, pieces, small_all,
    own_part, core_part, pair, far_one, far_two, from_one, from_two,
    blocks, ends, middle_block, block_one, block_two, two_out, total, small_own, small_in, small_total,
    send_sems, recv_sems, local_sems,
):
    me = Peers()
    net = Sends(send_sems, recv_sems)
    half = part.shape[1] // 2
    low, high = pl.ds(0, half), pl.ds(half, half)
    rows = gin.shape[0] // 4
    small_rows = small.shape[0] // 4
    own_rows = rows // 2
    inside = (me.z == 1) | (me.z == 2)
    outside = (me.z == 0) | (me.z == 3)

    def block(ref, k, size):
        return ref.at[pl.ds(pl.multiple_of(me.flip(me.z, k) * size, size), size)]

    local = [
        pltpu.make_async_copy(part.at[pl.ds(0, 4)], own_part, local_sems.at[0]),
        pltpu.make_async_copy(block(gin, 0, rows), blocks.at[0], local_sems.at[1]),
        pltpu.make_async_copy(block(gin, 2, rows), blocks.at[1], local_sems.at[2]),
        pltpu.make_async_copy(block(small, 0, small_rows), small_own, local_sems.at[3]),
    ]
    for copy in local:
        copy.start()
    me.greet(True)
    for i, k in enumerate((3, 1, 2, 0)):
        net.start(i, part.at[4 + k], core_part.at[k], me.core())
    for k in (1, 2, 3):
        net.start(3 + k, block(small, k, small_rows), small_in.at[k - 1], me.plane(k))
    to_ends = net.make(7, block(gin, 3, rows), ends, me.plane(1))
    to_middle = net.make(8, block(gin, 3, rows), middle_block, me.plane(3))

    @pl.when(outside)
    def _():
        to_ends.start()

    @pl.when(inside)
    def _():
        to_middle.start()

    two = net.make(9, two_out, block_two, me.plane(2))
    local[2].wait()

    @pl.when(outside)
    def _():
        two_out[...] = blocks[1]
        two.start()

    net.start(10, block(gin, 1, rows), block_one, me.plane(1))
    local[0].wait()
    for i, k in enumerate((3, 1, 2)):
        net.arrived(i)
        pair[k - 1] = (own_part[k].astype(f32) + core_part[k].astype(f32)).astype(bf16)
        if k == 3:
            net.start(11, pair.at[2, low], far_one, me.rep(1))
            net.start(12, pair.at[2, high], far_two, me.rep(2))
        elif k == 1:
            net.start(13, pair.at[0, low], from_one.at[low], me.rep(1))
        else:
            net.start(14, pair.at[1, high], from_two.at[high], me.rep(2))

    @pl.when(inside)
    def _():
        to_ends.wait_recv()
        two_out[...] = (blocks[1].astype(f32) + ends[...].astype(f32)).astype(bf16)
        two.start()

    net.arrived(11)
    pair[1, low] = (pair[1, low].astype(f32) + far_one[...].astype(f32)).astype(bf16)
    net.start(15, pair.at[1, low], from_two.at[low], me.rep(2))
    net.arrived(12)
    pair[0, high] = (pair[0, high].astype(f32) + far_two[...].astype(f32)).astype(bf16)
    net.start(16, pair.at[0, high], from_one.at[high], me.rep(1))
    local[3].wait()
    net.arrived(4, 5, 6)
    small_total[...] = small_own[...] + small_in[0] + small_in[1] + small_in[2]
    kept_small = pltpu.make_async_copy(small_total, small_all.at[0], local_sems.at[4])
    kept_small.start()
    for k in (1, 2, 3):
        net.start(16 + k, small_total, small_all.at[k], me.rep(k))
    local[1].wait()
    net.arrived(10, 9)
    summed = blocks[0].astype(f32) + block_one[...].astype(f32) + block_two[...].astype(f32)

    @pl.when(inside)
    def _():
        to_middle.wait_recv()
        total[...] = (summed + middle_block[...].astype(f32)).astype(bf16)

    @pl.when(outside)
    def _():
        total[...] = summed.astype(bf16)

    mine = total.at[pl.ds(pl.multiple_of(me.c * own_rows, own_rows), own_rows)]
    other = total.at[pl.ds(pl.multiple_of((1 - me.c) * own_rows, own_rows), own_rows)]
    net.start(20, other, pieces.at[1, 0], me.core())
    kept = pltpu.make_async_copy(mine, pieces.at[0, 0], local_sems.at[5])
    kept.start()
    for k in (1, 2, 3):
        net.start(20 + k, mine, pieces.at[0, k], me.rep(k))
    net.arrived(20)
    for k in (1, 2, 3):
        net.start(23 + k, pieces.at[1, 0], pieces.at[1, k], me.rep(k))
    net.arrived(3)
    net.arrived(13, 14, 15, 16)
    grad_normed[...] = (
        own_part[0].astype(f32) + core_part[0].astype(f32) + from_one[...].astype(f32) + from_two[...].astype(f32)
    )
    net.arrived(17, 18, 19, 21, 22, 23, 24, 25, 26)
    kept.wait()
    kept_small.wait()
    net.sent(*[slot for slot in net.made if slot not in (7, 8)])

    @pl.when(outside)
    def _():
        to_ends.wait_send()

    @pl.when(inside)
    def _():
        to_middle.wait_send()


def finish(part, gin, small):
    _, length, model = part.shape
    rows, width = gin.shape[0] // 4, gin.shape[1]
    small_rows, cols = small.shape[0] // 4, small.shape[1]
    anywhere = pl.BlockSpec(memory_space=pl.ANY)
    big = (length, model)
    return pl.pallas_call(
        finish_kernel,
        in_specs=[anywhere] * 3,
        out_specs=[pl.BlockSpec(memory_space=pltpu.VMEM), anywhere, anywhere],
        out_shape=[
            jax.ShapeDtypeStruct(big, f32),
            jax.ShapeDtypeStruct((2, 4, rows // 2, width), bf16),
            jax.ShapeDtypeStruct((4, small_rows, cols), f32),
        ],
        scratch_shapes=[
            pltpu.VMEM((4,) + big, bf16),
            pltpu.VMEM((4,) + big, bf16),
            pltpu.VMEM((3,) + big, bf16),
            pltpu.VMEM((length // 2, model), bf16),
            pltpu.VMEM((length // 2, model), bf16),
            pltpu.VMEM(big, bf16),
            pltpu.VMEM(big, bf16),
            pltpu.VMEM((2, rows, width), bf16),
            pltpu.VMEM((rows, width), bf16),
            pltpu.VMEM((rows, width), bf16),
            pltpu.VMEM((rows, width), bf16),
            pltpu.VMEM((rows, width), bf16),
            pltpu.VMEM((rows, width), bf16),
            pltpu.VMEM((rows, width), bf16),
            pltpu.VMEM((small_rows, cols), f32),
            pltpu.VMEM((3, small_rows, cols), f32),
            pltpu.VMEM((small_rows, cols), f32),
            pltpu.SemaphoreType.DMA((27,)),
            pltpu.SemaphoreType.DMA((27,)),
            pltpu.SemaphoreType.DMA((6,)),
        ],
        compiler_params=pltpu.CompilerParams(
            collective_id=4, has_side_effects=True, vmem_limit_bytes=40 * 2**20
        ),
        cost_estimate=pl.CostEstimate(flops=0, bytes_accessed=150 * 10**6, transcendentals=0),
        name="finish",
    )(part, gin, small)


class Links:
    def __init__(self, reps, shard_size):
        self.reps, self.shard_size = reps, shard_size
        self.planes = shard_size // 2
        self.r = lax.axis_index("rep")
        shard = lax.axis_index("shard")
        self.plane, self.c = shard // 2, shard % 2

    def rep(self, value, k):
        return lax.ppermute(value, "rep", [(i, i ^ k) for i in range(self.reps)])

    def core(self, value):
        return lax.ppermute(value, "shard", [(i, i ^ 1) for i in range(self.shard_size)])

    def planes_pairs(self, pairs):
        return [(2 * a + core, 2 * b + core) for a, b in pairs for core in range(2)]

    def z(self, value, pairs):
        return lax.ppermute(value, "shard", self.planes_pairs(pairs))

    def z_xor(self, value, k):
        return self.z(value, [(i, i ^ k) for i in range(self.planes)])

    def gather_rep(self, value):
        if self.reps != 4:
            return [value] + [self.rep(value, k) for k in range(1, self.reps)]
        half = value.shape[0] // 2
        one, two = self.rep(value, 1), self.rep(value, 2)
        return [value, one, two, self.across(one, two, half)]

    def gather_near(self, value):
        return [value] + [self.rep(value, k) for k in ((1, 2) if self.reps == 4 else range(1, self.reps))]

    def gather_far(self, near):
        return [self.across(near[1], near[2], near[0].shape[0] // 2)] if self.reps == 4 else []

    def across(self, one, two, half):
        return jnp.concatenate([self.rep(two[:half], 1), self.rep(one[half:], 2)], axis=0)

    def gather_plane(self, value):
        near = jnp.stack([value] + [self.rep(value, k) for k in range(1, self.reps)])
        return jnp.concatenate([near, self.core(near)], axis=0)

    def scatter_plane(self, partial, wire):
        reps = self.reps
        pair = partial[:reps].astype(f32) + self.core(partial[reps:].astype(wire)).astype(f32)
        total = pair[0]
        for k in range(1, reps):
            total = total + self.rep(pair[k].astype(wire), k).astype(f32)
        return total

    def place_z(self, values):
        rows = values[0].shape[0]
        out = jnp.zeros((self.planes * rows,) + values[0].shape[1:], values[0].dtype)
        start = (0,) * (values[0].ndim - 1)
        for k, value in enumerate(values):
            out = lax.dynamic_update_slice(out, value, ((self.plane ^ k) * rows,) + start)
        return out

    def gather_z_list(self, value):
        return [value] + [self.z_xor(value, k) for k in range(1, self.planes)]

    def gather_z(self, value):
        return self.place_z(self.gather_z_list(value))

    def block_z(self, value, k):
        rows = value.shape[0] // self.planes
        return lax.dynamic_slice_in_dim(value, (self.plane ^ k) * rows, rows, 0)

    def send_z(self, value):
        return [self.z_xor(self.block_z(value, k), k) for k in range(1, self.planes)]

    def sum_z(self, value, moved):
        total = self.block_z(value, 0).astype(f32)
        for other in moved:
            total = total + other.astype(f32)
        return total.astype(value.dtype)

    def add_pair(self, part, far):
        return (part[: self.reps].astype(f32) + far.astype(f32)).astype(bf16)

    def pair_rows(self, own, other):
        first = jnp.where(self.c == 0, own, other)
        second = jnp.where(self.c == 0, other, own)
        return jnp.stack([first, second])

    def order_reps(self, values):
        return order(values, self.r)

    def sum_plane(self, part, length, collective):
        if self.reps == 4 and self.planes == 4:
            return reduce_plane(part, collective)
        total = self.gather_plane(self.scatter_plane(part, f32))
        return total[:, :length].astype(bf16), total[:, length:]


def adam_step(master, first, second, gradient, rate, decays):
    first_new = beta_first * first + (1.0 - beta_first) * gradient
    second_new = beta_second * second + (1.0 - beta_second) * gradient * gradient
    update = (
        first_new
        / (1.0 - beta_first**ADAM_STEP)
        / (jnp.sqrt(second_new / (1.0 - beta_second**ADAM_STEP)) + adam_eps)
    )
    if decays:
        update = update + weight_decay * master
    return (first_new, second_new, master - rate * update)


def adam_in_kernel(place_ref, *refs):
    reps = (len(refs) - 9) // 2
    pieces = refs[: 2 * reps]
    master_ref, first_ref, second_ref = refs[2 * reps : 2 * reps + 3]
    first_out, second_out, master_out = refs[-3:]
    r, c = place_ref[0], place_ref[1]
    sub = pieces[0].shape[1]
    for e in range(2):
        for k in range(reps):
            at = ((c ^ e) * reps + (r ^ k)) * sub
            lanes = pl.ds(pl.multiple_of(at, sub), sub)
            gradient = pieces[e * reps + k][...].astype(f32)
            first, second, master = adam_step(
                master_ref[:, lanes], first_ref[:, lanes], second_ref[:, lanes], gradient,
                learn_rates[0], with_decay[0],
            )
            first_out[:, lanes] = first
            second_out[:, lanes] = second
            master_out[:, lanes] = master


def adam_in(place, half, pieces, master, first, second, earlier):
    rows, columns = master.shape
    reps = len(pieces) // 2
    sub = LANES
    block = 2 * reps * sub
    steps = columns // 2 // block
    wide = pl.BlockSpec((rows, block), lambda i, place_ref: (0, half * steps + i))
    thin = pl.BlockSpec((rows, sub), lambda i, place_ref: (0, i))
    anywhere = pl.BlockSpec(memory_space=pl.ANY)
    if earlier is None:
        earlier = (master, first, second)
        aliases = {}
    else:
        aliases = {1 + 2 * reps + 3 + i: i for i in range(3)}
    return pl.pallas_call(
        adam_in_kernel,
        grid_spec=pltpu.PrefetchScalarGridSpec(
            num_scalar_prefetch=1,
            grid=(steps,),
            in_specs=[thin] * (2 * reps) + [wide] * 3 + [anywhere] * 3,
            out_specs=[wide] * 3,
        ),
        out_shape=[jax.ShapeDtypeStruct(master.shape, f32)] * 3,
        input_output_aliases=aliases,
        compiler_params=pltpu.CompilerParams(vmem_limit_bytes=32 * 2**20),
        cost_estimate=pl.CostEstimate(flops=10 * master.size, bytes_accessed=13 * master.size, transcendentals=master.size),
        name="adam_in",
    )(place, *pieces, master, first, second, *earlier)


def adam_out_kernel(place_ref, *refs):
    reps = len(refs) - 6
    master_ref, first_ref, second_ref, first_out, second_out, master_out = refs[reps:]
    for k in range(reps):

        @pl.when(pl.program_id(0) == k)
        def _():
            first_out[...], second_out[...], master_out[...] = adam_step(
                master_ref[...], first_ref[...], second_ref[...], refs[k][...].astype(f32),
                learn_rates[3], with_decay[3],
            )


def adam_out(place, pieces, master, first, second):
    rows, columns = master.shape
    reps = len(pieces)
    sub = rows // reps
    wide = columns // 2
    mine = pl.BlockSpec((sub, wide), lambda k, j, p: (p[0] ^ k, j))
    piece = pl.BlockSpec((sub, wide), lambda k, j, p: (0, j))
    return pl.pallas_call(
        adam_out_kernel,
        grid_spec=pltpu.PrefetchScalarGridSpec(
            num_scalar_prefetch=1,
            grid=(reps, 2),
            in_specs=[piece] * reps + [mine] * 3,
            out_specs=[mine] * 3,
        ),
        out_shape=[jax.ShapeDtypeStruct(master.shape, f32)] * 3,
        compiler_params=pltpu.CompilerParams(vmem_limit_bytes=32 * 2**20),
        cost_estimate=pl.CostEstimate(flops=10 * master.size, bytes_accessed=26 * master.size, transcendentals=master.size),
        name="adam_out",
    )(place, *pieces, master, first, second)


def slice_in_kernel(place_ref, own_ref, other_ref, out_ref):
    out_ref[0] = own_ref[...].astype(bf16)
    out_ref[1] = other_ref[...].astype(bf16)


def slice_in(place, master, reps):
    rows, columns = master.shape
    blocks = columns // (2 * reps * LANES)

    def of_core(e):
        return pl.BlockSpec((rows, LANES), lambda b, p: (0, (2 * b + (p[1] ^ e)) * reps + p[0]))

    return pl.pallas_call(
        slice_in_kernel,
        grid_spec=pltpu.PrefetchScalarGridSpec(
            num_scalar_prefetch=1,
            grid=(blocks,),
            in_specs=[of_core(0), of_core(1)],
            out_specs=pl.BlockSpec((2, rows, LANES), lambda b, p: (0, 0, b)),
        ),
        out_shape=jax.ShapeDtypeStruct((2, rows, blocks * LANES), bf16),
        name="slice_in",
    )(place, master, master)


def after(value, *earlier):
    return lax.optimization_barrier((value, *earlier))[0]


def after_all(values, *earlier):
    return list(lax.optimization_barrier((*values, *earlier))[: len(values)])


def unpack(values):
    seqs, rows, _ = values.shape
    parts = values.reshape(seqs, rows // (2 * NSTATE), 2 * NSTATE, LANES)
    return parts.transpose(0, 2, 1, 3).reshape(seqs, 2 * NSTATE, -1)


def pack(values):
    seqs, count, length = values.shape
    return values.reshape(seqs, count, length // LANES, LANES).transpose(0, 2, 1, 3).reshape(seqs, -1, LANES)


def to_chunks(values):
    seqs, count, length = values.shape
    return values.reshape(seqs, count, length // CHUNK, CHUNK).transpose(2, 1, 0, 3)


def from_sums(values):
    groups, length, _ = values.shape
    parts = values.reshape(groups, length, 2 * NSTATE, SUBS).transpose(0, 3, 2, 1)
    return parts.reshape(groups * SUBS, 2 * NSTATE, length)


def order(values, index):
    bit = 1
    while bit < len(values):
        swap = (index & bit) != 0
        values = [jnp.where(swap, values[i ^ bit], values[i]) for i in range(len(values))]
        bit *= 2
    return jnp.stack(values)


def shards(
    reps, shard_size,
    hidden, segments, cotangent,
    in_master, in_first, in_second,
    x_master, x_first, x_second,
    dt_master, dt_first, dt_second,
    out_master, out_first, out_second,
    chan_master, chan_first, chan_second,
    gain_master, gain_first, gain_second,
):
    net = Links(reps, shard_size)
    planes, r, c = net.planes, net.r, net.c
    length, model = hidden.shape[1:]
    in_rows = in_master.shape[0]
    own_chan = out_master.shape[0]
    sub = own_chan // reps
    width = planes * sub
    xcols = x_master.shape[1]
    chan_cols = chan_master.shape[1]
    seqs = 2 * reps

    def sub_rows(value):
        return lax.dynamic_slice_in_dim(value, r * sub, sub, 0)

    place = jnp.stack([r, c, net.plane]).astype(jnp.int32)
    own_hidden = hidden[0]
    tiled = sub % LANES == 0
    fast = tiled and reps == 4 and planes == 4
    if tiled:
        in_own, in_other = slice_in(place, in_master, reps)
    else:
        in_view = in_master.reshape(in_rows, 2, planes, 2, reps, sub)
        in_mine = lax.dynamic_index_in_dim(in_view, r, 4, keepdims=False).astype(bf16)
        in_own = lax.dynamic_index_in_dim(in_mine, c, 3, keepdims=False).reshape(in_rows, 2 * width)
        in_other = lax.dynamic_index_in_dim(in_mine, 1 - c, 3, keepdims=False).reshape(in_rows, 2 * width)
    small = jnp.concatenate(
        [sub_rows(x_master).astype(bf16), sub_rows(dt_master).astype(bf16), sub_rows(chan_master).astype(bf16)], axis=1
    )
    own_gain = lax.reduce_precision(gain_master, 8, 7)[None]
    own_ids = segments.astype(f32)
    if fast:
        small = jnp.pad(small, ((0, 0), (0, -small.shape[1] % LANES)))
        hidden_all, inner_blocks, small_parts, gain_parts, ids = gather_first(
            own_hidden, in_own[:, :width], in_other[:, :width], small, own_gain, own_ids
        )
        inner_blocks = [inner_blocks[k] for k in range(planes)]
        small_all = order(list(small_parts), net.plane).reshape(width, -1)
        two = [order([gain_parts[e * planes + k] for k in range(planes)], net.plane) for e in range(2)]
        gain = jnp.stack(order(two, c), axis=1).reshape(model)
        ids = ids.reshape(seqs, length)
        own_up = after(cotangent[0], hidden_all)
        gate_pair = net.pair_rows(in_own[:, width:], net.core(in_other[:, width:])).reshape(2 * in_rows, width)
        gate_blocks = net.gather_z_list(after(gate_pair, hidden_all))
        out_blocks = net.gather_z_list(after(sub_rows(out_master).astype(bf16), hidden_all))
    else:
        ids = net.gather_plane(own_ids).reshape(seqs, length)
        gain_pair = net.pair_rows(own_gain[0], net.core(own_gain[0])).reshape(2 * in_rows)
        gain = net.gather_z(gain_pair)
        small_all = net.gather_z(small)
        in_pair = net.pair_rows(in_own, net.core(in_other)).reshape(2 * in_rows, 2 * width)
        inner_blocks = net.gather_z_list(in_pair[:, :width])
        hidden_all = net.gather_plane(own_hidden)
        own_up = after(cotangent[0], hidden_all)
        gate_blocks = net.gather_z_list(in_pair[:, width:])
        out_blocks = net.gather_z_list(sub_rows(out_master).astype(bf16))
    up_near = net.gather_near(own_up)
    w_xdt = small_all[:, :RANK]
    w_xdt_t = w_xdt.T
    w_xbc = small_all[:, RANK:xcols].T
    w_dt = small_all[:, xcols : xcols + RANK]
    channel = small_all[:, xcols + RANK : xcols + RANK + chan_cols].astype(f32)
    a_log = channel[:, KCONV : KCONV + NSTATE]
    rates = -jnp.exp(a_log)
    rate_tiles = jnp.broadcast_to(rates.T[:, None, :], (NSTATE, SUBS, width))
    chan = channel.T
    same = [
        (jnp.pad(ids, ((0, 0), (KCONV - 1 - k, 0)), constant_values=-1)[:, :length] == ids).astype(f32)
        for k in range(KCONV - 1)
    ]
    cut = jnp.where(same[-1] > 0, 0.0, CUT)
    masks = jnp.stack(same + [cut] + [jnp.zeros_like(cut)] * (MASKS - KCONV), axis=2)

    normed, inner, conv_out, proj_part = front(
        place, hidden_all, gain[None], masks, chan, w_xdt_t, w_xbc, inner_blocks
    )
    dt_in, bc = net.sum_plane(proj_part, length, 2)
    up_all = jnp.stack(up_near + net.gather_far(after_all(up_near, dt_in)))
    upstream = jnp.concatenate([up_all, net.core(up_all)])
    bc = to_chunks(unpack(bc))
    scanned, starts = scan_forward(dt_in, masks, conv_out, bc, rate_tiles, w_dt, chan)
    out_part, mixed, grad_y, grad_gate, grad_skip = middle(
        place, normed, upstream, scanned, conv_out, chan, gate_blocks, out_blocks
    )
    out_far = net.core(out_part[reps:])
    grad_out = dot(mixed.reshape(-1, width), upstream.reshape(-1, model), ((0,), (0,))).astype(bf16)
    flat_normed = normed.reshape(-1, model)
    gin_gate = dot(flat_normed, grad_gate.reshape(-1, width), ((0,), (0,))).astype(bf16)
    pair, grad_y = lax.optimization_barrier((net.add_pair(out_part, out_far), grad_y))
    out_moved = [net.rep(pair[k], k) for k in range(1, reps)]
    grad_out_moved = net.send_z(grad_out)
    gin_gate_moved = net.send_z(gin_gate)
    grad_y = after(grad_y, grad_out, gin_gate)

    grad_conv, grad_dtlow, grad_dtin, grad_bc, grad_rates, grad_dtbias = scan_backward(
        dt_in, masks, conv_out, bc, rate_tiles, w_dt, chan, starts, grad_y
    )
    grad_rates = jnp.sum(grad_rates, axis=1).T
    grad_dt = dot(grad_dtlow.reshape(-1, width), dt_in.reshape(-1, RANK), ((0,), (0,)))
    out_sum = pair[0].astype(f32)
    for moved in after_all(out_moved, grad_dtin):
        out_sum = out_sum + moved.astype(f32)
    layer_output = (hidden[0].astype(f32) + out_sum).astype(bf16)
    grad_out_own = net.sum_z(grad_out, after_all(grad_out_moved, grad_dtin))
    gin_gate_rows = net.sum_z(gin_gate, after_all(gin_gate_moved, grad_dtin))
    proj_back = jnp.concatenate([grad_dtin, pack(from_sums(grad_bc))], axis=1)
    gp_dt, gp_bc = net.sum_plane(proj_back, length, 3)
    gp_bc = unpack(gp_bc).astype(bf16)
    flat_conv = conv_out.reshape(-1, width)
    grad_xdt = dot(flat_conv, gp_dt.reshape(-1, RANK), ((0,), (0,)))
    grad_xbc = lax.dot_general(
        conv_out, gp_bc, (((1,), (2,)), ((0,), (0,))), preferred_element_type=f32
    ).sum(axis=0)
    grad_x = jnp.concatenate([grad_xdt, grad_xbc], axis=1)
    grad_inner, conv_sums = back_conv(place, grad_conv, gp_dt, gp_bc, inner, masks, chan, w_xdt_t, w_xbc)
    gin_inner = dot(flat_normed, grad_inner.reshape(-1, width), ((0,), (0,))).astype(bf16)
    normed_part, grad_gain = back_normed(place, grad_inner, grad_gate, hidden_all, inner_blocks, gate_blocks)
    def pieces_in(rows):
        rows = rows.reshape(2, in_rows, width)
        own = lax.dynamic_index_in_dim(rows, c, 0, keepdims=False)
        other = net.core(lax.dynamic_index_in_dim(rows, 1 - c, 0, keepdims=False))
        return net.gather_rep(own) + net.gather_rep(other)

    def full_in(pieces):
        own = net.order_reps(pieces[:reps])
        other = net.order_reps(pieces[reps:])
        every = net.pair_rows(own, other).reshape(2, reps, in_rows, planes, sub)
        return every.transpose(2, 3, 0, 1, 4).reshape(in_rows, width * seqs).astype(f32)

    out_new = adam_out(
        place, net.gather_rep(grad_out_own), out_master, out_first, out_second
    )
    grad_small = jnp.concatenate(
        [
            grad_x,
            grad_dt,
            jnp.sum(conv_sums[:KCONV], axis=1).T,
            grad_rates * rates,
            jnp.sum(conv_sums[KCONV], axis=0)[:, None],
            jnp.sum(grad_dtbias, axis=0)[:, None],
            jnp.sum(grad_skip, axis=0)[:, None],
            jnp.sum(grad_gain, axis=0).reshape(width, reps),
        ],
        axis=1,
    )
    if fast:
        grad_small = jnp.pad(grad_small, ((0, 0), (0, -grad_small.shape[1] % LANES)))
        grad_normed, inner_pieces, small_sum = finish(normed_part, gin_inner, grad_small)
        inner_pieces = [inner_pieces[e, k] for e in range(2) for k in range(reps)]
        small_sum = net.order_reps(list(small_sum))
    else:
        grad_normed = net.scatter_plane(normed_part, bf16)
        inner_pieces = pieces_in(net.sum_z(gin_inner, net.send_z(gin_inner)))
        small_sum = net.order_reps(net.gather_rep(net.sum_z(grad_small, net.send_z(grad_small))))
    own_res = hidden[0].astype(f32)
    own_inv = lax.rsqrt(jnp.mean(own_res * own_res, axis=1, keepdims=True) + norm_eps)
    grad_scaled = grad_normed * gain
    input_grad = (
        own_inv * grad_scaled
        - own_res * own_inv**3 * jnp.mean(grad_scaled * own_res, axis=1, keepdims=True)
        + cotangent[0].astype(f32)
    ).astype(bf16)

    if tiled:
        in_new = adam_in(place, 1, pieces_in(gin_gate_rows), in_master, in_first, in_second, None)
        in_new = adam_in(place, 0, inner_pieces, in_master, in_first, in_second, in_new)
    else:
        in_sum = jnp.concatenate([full_in(inner_pieces), full_in(pieces_in(gin_gate_rows))], axis=1)
        in_new = adam_step(in_master, in_first, in_second, in_sum, learn_rates[0], with_decay[0])
    gain_cols = slice(xcols + RANK + chan_cols, xcols + RANK + chan_cols + reps)
    gain_two = jnp.sum(small_sum[:, :, gain_cols], axis=0).reshape(2, in_rows)
    gain_own = lax.dynamic_index_in_dim(gain_two, c, 0, keepdims=False)
    gain_sum = gain_own + net.core(lax.dynamic_index_in_dim(gain_two, 1 - c, 0, keepdims=False))
    small_sum = small_sum.reshape(own_chan, -1)
    x_sum = small_sum[:, :xcols]
    dt_sum = small_sum[:, xcols : xcols + RANK]
    chan_sum = small_sum[:, xcols + RANK : xcols + RANK + chan_cols]

    def update(position, master, first, second, gradient):
        return adam_step(master, first, second, gradient, learn_rates[position], with_decay[position])

    updated = (
        *in_new,
        *update(1, x_master, x_first, x_second, x_sum),
        *update(2, dt_master, dt_first, dt_second, dt_sum),
        *out_new,
        *update(4, chan_master, chan_first, chan_second, chan_sum),
        *update(5, gain_master, gain_first, gain_second, gain_sum),
    )
    return (layer_output[None], input_grad[None], *updated)


def solution(mesh):
    token = P(("rep", "shard"), None, None)
    rows = P("shard", None)
    placed = (token, P(("rep", "shard"), None), token) + (rows,) * 15 + (P("shard"),) * 3
    return jax.shard_map(
        functools.partial(shards, mesh.shape["rep"], mesh.shape["shard"]),
        mesh=mesh,
        in_specs=placed,
        out_specs=(token, token) + (rows,) * 15 + (P("shard"),) * 3,
        check_vma=False,
    )
```

```python
import functools

import jax
import jax.numpy as jnp
from jax import lax
from jax.experimental import pallas as pl
from jax.experimental.pallas import tpu as pltpu
from jax.sharding import PartitionSpec as P

NSTATE = 16
RANK = 128
KCONV = 4
ADAM_STEP = 10
CHUNK = 32
LANES = 128
SUBS = 8
CUT = 1e30
MASKS = 8
TOKENS = 256
BC_ROWS = TOKENS * 2 * NSTATE // LANES
CH = 2 * NSTATE
FWD_UNROLL = 8
BWD_UNROLL = 4
LOG2E = 1.4426950408889634

norm_eps = 1e-05
beta_first = 0.9
beta_second = 0.95
adam_eps = 1e-08
weight_decay = 0.1
learn_rates = (0.044, 0.03, 0.18, 0.09, 1.0, 0.6)
with_decay = (True, True, True, True, False, False)

bf16 = jnp.bfloat16
f32 = jnp.float32


def silu_slope(values):
    sigma = jax.nn.sigmoid(values)
    return sigma * (1.0 + values * (1.0 - sigma))


def dot(a, b, dims):
    return lax.dot_general(a, b, (dims, ((), ())), preferred_element_type=f32)


def expand_inputs(bc_ref, bx, sb, chunk):
    per = LANES // CHUNK
    packed = BC_ROWS
    first = sb * SUBS * packed + (chunk // per) * 2 * NSTATE
    v = jnp.concatenate([bc_ref[pl.ds(first + n, SUBS, stride=packed), :] for n in range(2 * NSTATE)], axis=0)
    v = pltpu.roll(v, (per - chunk % per) % per * CHUNK, 1)[:, :CHUNK]
    high = v.astype(bf16)
    rest = v - high.astype(f32)
    middle = rest.astype(bf16)
    low = (rest - middle.astype(f32)).astype(bf16)
    pieces = jnp.concatenate([high, middle, low], axis=1)
    token = lax.broadcasted_iota(jnp.int32, (3 * CHUNK, LANES), 0) % CHUNK
    for t in range(CHUNK):
        bx[t] = dot(pieces, (token == t).astype(bf16), ((1,), (0,))).reshape(2 * NSTATE, SUBS, LANES)


def lane_sums(acc, out_ref, sb, chunk):
    rows = 2 * NSTATE * SUBS
    per = LANES // CHUNK
    lane = lax.broadcasted_iota(jnp.int32, (2 * LANES, LANES), 1) - chunk % per * CHUNK
    total = jnp.zeros((rows, LANES), f32)
    for t in range(CHUNK):
        v = acc[t].reshape(rows, LANES)
        high = v.astype(bf16)
        low = (v - high.astype(f32)).astype(bf16)
        total = total + dot(jnp.concatenate([high, low], axis=1), (lane == t).astype(bf16), ((1,), (0,)))
    packed = BC_ROWS + TOKENS
    first = sb * SUBS * packed + TOKENS + (chunk // per) * 2 * NSTATE
    for n in range(2 * NSTATE):
        at = pl.ds(first + n, SUBS, stride=packed)
        out_ref[at, :] = out_ref[at, :] + total[n * SUBS : (n + 1) * SUBS]


def spread(scratch, q, values):
    for g in range(scratch.shape[0]):
        scratch[g, pl.ds(q * CHUNK, CHUNK), :] = values[:, g * LANES : (g + 1) * LANES]


def collect(ref, q, scratch):
    for g in range(scratch.shape[0]):
        ref[q, :, pl.ds(g * LANES, LANES)] = scratch[g, pl.ds(q * CHUNK, CHUNK), :]


def tree(values):
    while len(values) > 1:
        values = [a + b for a, b in zip(values[::2], values[1::2])]
    return values[0]


def softplus(v):
    return jnp.maximum(v, 0.0) + jnp.log1p(jnp.exp(-jnp.abs(v)))


def chan_row(rest_ref, column):
    return rest_ref[pl.ds(CH + column, 1), :]


def dt_products(dt_ref, small_ref, rest_ref, q):
    w_dt = small_ref[:, pl.ds(RANK, RANK)]
    return dot(dt_ref[q], w_dt, ((1,), (1,))) + chan_row(rest_ref, KCONV + NSTATE + 1)


def put_rates(rest_ref, rate_ref):
    for n in range(NSTATE):
        row = -jnp.exp(chan_row(rest_ref, KCONV + n))
        rate_ref[n] = jnp.broadcast_to(row, rate_ref.shape[1:])


def scan_fwd_kernel(
    dt_ref, mask_ref, conv_ref, bc_ref, small_ref, rest_ref, y_ref, starts_ref, state, bx, stepm, drive, ys, rate_ref
):
    seqs = dt_ref.shape[0]
    width = conv_ref.shape[2]

    @pl.when(pl.program_id(0) == 0)
    def _():
        state[...] = jnp.zeros_like(state)
        put_rates(rest_ref, rate_ref)

    starts_ref[0] = state[...]
    for q in range(seqs):
        step = softplus(dt_products(dt_ref, small_ref, rest_ref, q))
        spread(stepm, q, step + mask_ref[q, :, pl.ds(KCONV - 1, 1)])
        spread(drive, q, step * conv_ref[q].astype(f32))
    for sb in range(seqs // SUBS):
        expand_inputs(bc_ref, bx, sb, pl.program_id(0))
        sub = pl.ds(sb * SUBS, SUBS)

        def group(g, carry):
            lanes = pl.ds(pl.multiple_of(g * LANES, LANES), LANES)
            rates = [rate_ref[n, :, lanes] * LOG2E for n in range(NSTATE)]

            def token(t, st):
                rows = pl.ds(sb * SUBS * CHUNK + t, SUBS, stride=CHUNK)
                sm = stepm[g, rows, :]
                dx = drive[g, rows, :]
                parts = []
                out = []
                for n in range(NSTATE):
                    dec = jnp.exp2(sm * rates[n])
                    s_n = dec * st[n] + dx * bx[t, n]
                    out.append(s_n)
                    parts.append(s_n * bx[t, NSTATE + n])
                ys[g, rows, :] = tree(parts)
                return tuple(out)

            st = tuple(state[n, sub, lanes] for n in range(NSTATE))
            st = lax.fori_loop(0, CHUNK, token, st, unroll=FWD_UNROLL)
            for n in range(NSTATE):
                state[n, sub, lanes] = st[n]
            return carry

        lax.fori_loop(0, width // LANES, group, 0)
    for q in range(seqs):
        collect(y_ref, q, ys)


def scan_bwd_kernel(
    dt_ref, mask_ref, conv_ref, bc_ref, small_ref, rest_ref, starts_ref, gy_ref,
    gconv_ref, glow_ref, proj_ref, grate_ref, gbias_ref,
    flow, bx, stepm, step2, conv2, gy2, gs2, gc2, dec_s, pri_s, acc, rate_ref,
):
    seqs = dt_ref.shape[0]
    width = conv_ref.shape[2]
    chunk = pl.num_programs(0) - 1 - pl.program_id(0)

    @pl.when(pl.program_id(0) == 0)
    def _():
        flow[...] = jnp.zeros_like(flow)
        proj_ref[...] = jnp.zeros_like(proj_ref)
        put_rates(rest_ref, rate_ref)
        grate_ref[...] = jnp.zeros_like(grate_ref)
        gbias_ref[...] = jnp.zeros_like(gbias_ref)

    for q in range(seqs):
        step = softplus(dt_products(dt_ref, small_ref, rest_ref, q))
        spread(step2, q, step)
        spread(stepm, q, step + mask_ref[q, :, pl.ds(KCONV - 1, 1)])
        spread(conv2, q, conv_ref[q].astype(f32))
        spread(gy2, q, gy_ref[q])
    for sb in range(seqs // SUBS):
        expand_inputs(bc_ref, bx, sb, chunk)
        sub = pl.ds(sb * SUBS, SUBS)
        acc[...] = jnp.zeros_like(acc)

        def group(g, carry):
            lanes = pl.ds(pl.multiple_of(g * LANES, LANES), LANES)

            def token_f(t, st):
                rows = pl.ds(sb * SUBS * CHUNK + t, SUBS, stride=CHUNK)
                sm = stepm[g, rows, :]
                dx = step2[g, rows, :] * conv2[g, rows, :]
                out = []
                for n in range(NSTATE):
                    dec = jnp.exp2(sm * (rate_ref[n, :, lanes] * LOG2E))
                    dec_s[t, n] = dec
                    pri_s[t, n] = st[n]
                    out.append(dec * st[n] + dx * bx[t, n])
                return tuple(out)

            st = tuple(starts_ref[0, n, sub, lanes] for n in range(NSTATE))
            st = lax.fori_loop(0, CHUNK, token_f, st, unroll=FWD_UNROLL)
            for n in range(NSTATE):
                pri_s[CHUNK, n] = st[n]

            def token_b(i, carried):
                t = CHUNK - 1 - i
                fl, ga = carried
                rows = pl.ds(sb * SUBS * CHUNK + t, SUBS, stride=CHUNK)
                size = step2[g, rows, :]
                conv = conv2[g, rows, :]
                gy = gy2[g, rows, :]
                dx = size * conv
                along, gsz = [], []
                nfl, nga = [], []
                for n in range(NSTATE):
                    grad = gy * bx[t, NSTATE + n] + fl[n]
                    dg = dec_s[t, n] * grad
                    th = dg * pri_s[t, n]
                    along.append(grad * bx[t, n])
                    gsz.append(th * rate_ref[n, :, lanes])
                    acc[t, n] += grad * dx
                    acc[t, NSTATE + n] += pri_s[t + 1, n] * gy
                    nfl.append(dg)
                    nga.append(ga[n] + th * size)
                along = tree(along)
                gs2[g, rows, :] = tree(gsz) + conv * along
                gc2[g, rows, :] = size * along
                return (tuple(nfl), tuple(nga))

            fl = tuple(flow[n, sub, lanes] for n in range(NSTATE))
            ga = tuple(grate_ref[n, :, lanes] for n in range(NSTATE))
            fl, ga = lax.fori_loop(0, CHUNK, token_b, (fl, ga), unroll=BWD_UNROLL)
            for n in range(NSTATE):
                flow[n, sub, lanes] = fl[n]
                grate_ref[n, :, lanes] = ga[n]
            return carry

        lax.fori_loop(0, width // LANES, group, 0)
        lane_sums(acc, proj_ref, sb, chunk)
    skip = chan_row(rest_ref, KCONV + NSTATE + 2)
    for q in range(seqs):
        collect(gconv_ref, q, gc2)
        gconv_ref[q] += skip * gy_ref[q]
        gstep = jnp.concatenate([gs2[g, pl.ds(q * CHUNK, CHUNK), :] for g in range(width // LANES)], axis=1)
        grad = gstep * jax.nn.sigmoid(dt_products(dt_ref, small_ref, rest_ref, q))
        gbias_ref[...] += jnp.sum(grad.reshape(CHUNK // SUBS, SUBS, width), axis=0)
        low = grad.astype(bf16)
        glow_ref[q] = low
        at = pl.multiple_of(q * (TOKENS + BC_ROWS) + chunk * CHUNK, CHUNK)
        proj_ref[pl.ds(at, CHUNK), :] = dot(low, small_ref[:, pl.ds(RANK, RANK)], ((1,), (0,)))


def whole(shape):
    return pl.BlockSpec(shape, lambda i, *_: (0,) * len(shape))


def scan_specs(seqs, width, small, rest, chunk_of):
    def tokens(columns):
        return pl.BlockSpec((seqs, CHUNK, columns), lambda i: (0, chunk_of(i), 0))

    starts = pl.BlockSpec((1, NSTATE, seqs, width), lambda i: (chunk_of(i), 0, 0, 0))
    ins = [
        tokens(RANK), tokens(MASKS), tokens(width), whole((seqs * BC_ROWS, LANES)), whole(small.shape), whole(rest.shape),
    ]
    return tokens, starts, ins


def scan_forward(dt_in, masks, conv, bc, small, rest):
    seqs, length, width = conv.shape
    chunks = length // CHUNK
    tokens, starts, ins = scan_specs(seqs, width, small, rest, lambda i: i)
    tall = pltpu.VMEM((width // LANES, seqs * CHUNK, LANES), f32)
    return pl.pallas_call(
        scan_fwd_kernel,
        grid=(chunks,),
        in_specs=ins,
        out_specs=[tokens(width), starts],
        out_shape=[
            jax.ShapeDtypeStruct(conv.shape, f32),
            jax.ShapeDtypeStruct((chunks, NSTATE, seqs, width), f32),
        ],
        scratch_shapes=[
            pltpu.VMEM((NSTATE, seqs, width), f32),
            pltpu.VMEM((CHUNK, 2 * NSTATE, SUBS, LANES), f32),
            tall, tall, tall,
            pltpu.VMEM((NSTATE, SUBS, width), f32),
        ],
        compiler_params=pltpu.CompilerParams(vmem_limit_bytes=50 * 2**20),
        cost_estimate=pl.CostEstimate(
            flops=8 * conv.size * NSTATE, bytes_accessed=100 * 10**6, transcendentals=conv.size * NSTATE
        ),
        name="scan_forward",
    )(dt_in, masks, conv, bc, small, rest)


def scan_backward(dt_in, masks, conv, bc, small, rest, starts, grad_y):
    seqs, length, width = conv.shape
    chunks = length // CHUNK
    tokens, start_spec, ins = scan_specs(seqs, width, small, rest, lambda i: chunks - 1 - i)
    packed = (seqs * (TOKENS + BC_ROWS), LANES)
    tall = pltpu.VMEM((width // LANES, seqs * CHUNK, LANES), f32)
    return pl.pallas_call(
        scan_bwd_kernel,
        grid=(chunks,),
        in_specs=ins + [start_spec, tokens(width)],
        out_specs=[
            tokens(width), tokens(width), whole(packed),
            whole((NSTATE, SUBS, width)), whole((SUBS, width)),
        ],
        out_shape=[
            jax.ShapeDtypeStruct(conv.shape, f32),
            jax.ShapeDtypeStruct(conv.shape, bf16),
            jax.ShapeDtypeStruct(packed, f32),
            jax.ShapeDtypeStruct((NSTATE, SUBS, width), f32),
            jax.ShapeDtypeStruct((SUBS, width), f32),
        ],
        scratch_shapes=[
            pltpu.VMEM((NSTATE, seqs, width), f32),
            pltpu.VMEM((CHUNK, 2 * NSTATE, SUBS, LANES), f32),
            tall, tall, tall, tall, tall, tall,
            pltpu.VMEM((CHUNK, NSTATE, SUBS, LANES), f32),
            pltpu.VMEM((CHUNK + 1, NSTATE, SUBS, LANES), f32),
            pltpu.VMEM((CHUNK, 2 * NSTATE, SUBS, LANES), f32),
            pltpu.VMEM((NSTATE, SUBS, width), f32),
        ],
        compiler_params=pltpu.CompilerParams(vmem_limit_bytes=56 * 2**20),
        cost_estimate=pl.CostEstimate(
            flops=24 * conv.size * NSTATE, bytes_accessed=300 * 10**6, transcendentals=conv.size * NSTATE
        ),
        name="scan_backward",
    )(dt_in, masks, conv, bc, small, rest, starts, grad_y)


def put_combined(place_ref, blocks, w_gate, w_out):
    @pl.when(pl.program_id(0) == 0)
    def _():
        for k, block in enumerate(blocks):
            at = place_ref[2] ^ k
            rows, width = block.shape[0] // 2, block.shape[1]
            w_gate[pl.ds(pl.multiple_of(at * rows, rows), rows), :] = block[pl.ds(0, rows), :]
            if w_out is not None:
                count = w_out.shape[1] // width
                sub = rows // count
                for i in range(count):
                    part = block[pl.ds(rows + i * sub, sub), :]
                    w_out[pl.ds(pl.multiple_of(at * sub, sub), sub), pl.ds(i * width, width)] = part


def put_blocks(place_ref, blocks, out):
    @pl.when(pl.program_id(0) == 0)
    def _():
        for k, block in enumerate(blocks):
            rows = block.shape[0]
            out[pl.ds(pl.multiple_of((place_ref[2] ^ k) * rows, rows), rows), :] = block[...]


def normalised(hid):
    residual = hid.astype(f32)
    return residual * lax.rsqrt(jnp.mean(residual * residual, axis=1, keepdims=True) + norm_eps)


def earlier_rows(inner, masks):
    terms = []
    for k in range(KCONV - 1):
        terms.append(pltpu.roll(inner, KCONV - 1 - k, 0) * masks[:, k : k + 1])
    return terms + [inner]


def conv_sum(terms, chan_ref):
    total = chan_row(chan_ref, KCONV + NSTATE)
    for k, term in enumerate(terms):
        total = total + chan_row(chan_ref, k) * term
    return total


def put_columns(ref, start, values):
    count = values.shape[0]
    for i in range(values.shape[1] // LANES):
        ref[0, pl.ds(start + i * count, count), :] = values[:, i * LANES : (i + 1) * LANES]


def token_masks(ids):
    length = ids.shape[1]
    at = lax.broadcasted_iota(jnp.int32, (SUBS, length), 1)
    row = lax.broadcasted_iota(jnp.int32, (SUBS, length), 0)
    every = jnp.broadcast_to(ids, (SUBS, length))
    rows = jnp.zeros((SUBS, length), f32)
    for k in range(KCONV):
        offset = max(KCONV - 1 - k, 1)
        same = (pltpu.roll(every, offset, 1) == every) & (at >= offset)
        if k == KCONV - 1:
            same = ~same
        rows = jnp.where((row == k) & same, 1.0, rows)
    unit = lax.broadcasted_iota(jnp.int32, (length, length), 0) == lax.broadcasted_iota(jnp.int32, (length, length), 1)
    columns = dot(unit.astype(bf16), rows.astype(bf16), ((1,), (1,)))
    column = lax.broadcasted_iota(jnp.int32, columns.shape, 1)
    return jnp.where(column == KCONV - 1, columns * CUT, columns)


def front_kernel(gain_parts, planes, place_ref, hid_ref, ids_ref, *refs):
    gains, smalls, blocks = refs[:1], refs[1 : 1 + planes], refs[1 + planes : 1 + 2 * planes]
    normed_ref, inner_ref, conv_ref, proj_ref, mask_ref, small_ref, rest_ref, gain_ref, weights = refs[1 + 2 * planes :]
    put_blocks(place_ref, blocks, weights)
    put_blocks(place_ref, smalls, small_ref)

    @pl.when(pl.program_id(0) == 0)
    def _():
        rest_ref[...] = small_ref[:, pl.ds(2 * RANK, LANES)].astype(f32).T
        if gain_parts == 1:
            gain_ref[...] = gains[0][0]
        else:
            for e in range(2):
                for k in range(planes):
                    columns = gains[0].shape[2]
                    at = ((place_ref[2] ^ k) * 2 + (place_ref[1] ^ e)) * columns
                    gain_ref[:, pl.ds(pl.multiple_of(at, columns), columns)] = gains[0][e * planes + k]

    normed = (normalised(hid_ref[0]) * gain_ref[...]).astype(bf16)
    normed_ref[0] = normed
    inner = dot(normed, weights[...], ((1,), (0,)))
    inner_ref[0] = inner
    masks = token_masks(ids_ref[0])
    mask_ref[0] = masks
    pre = conv_sum(earlier_rows(inner, masks), rest_ref)
    conv = jax.nn.silu(pre).astype(bf16)
    conv_ref[0] = conv
    proj_ref[0, pl.ds(0, TOKENS), :] = dot(conv, small_ref[:, pl.ds(0, RANK)], ((1,), (0,)))
    put_columns(proj_ref, TOKENS, dot(rest_ref[pl.ds(0, CH), :].astype(bf16), conv, ((1,), (1,))))


def per_sequence(kernel, place, stacked, fixed, outs, scratch, flops, name):
    seqs = stacked[0].shape[0]
    half = seqs // 2
    index = {
        "every": lambda i, p: ((i + half) % seqs, 0, 0),
        "other": lambda i, p: (jnp.minimum(i, half - 1), 0, 0),
        "own": lambda i, p: (jnp.maximum(i - half, 0), 0, 0),
    }

    def block(shape, kind="every"):
        return pl.BlockSpec((1,) + tuple(shape[1:]), index[kind])

    return pl.pallas_call(
        kernel,
        grid_spec=pltpu.PrefetchScalarGridSpec(
            num_scalar_prefetch=1,
            grid=(seqs,),
            in_specs=[block(v.shape) for v in stacked] + [whole(v.shape) for v in fixed],
            out_specs=[whole(shape) if kind == "whole" else block(shape, kind) for shape, _, kind in outs],
            scratch_shapes=scratch,
        ),
        out_shape=[jax.ShapeDtypeStruct(shape, dtype) for shape, dtype, _ in outs],
        compiler_params=pltpu.CompilerParams(vmem_limit_bytes=56 * 2**20),
        cost_estimate=pl.CostEstimate(flops=flops, bytes_accessed=40 * 10**6, transcendentals=0),
        name=name,
    )(place, *stacked, *fixed)


def put_part(part, own_ref, other_ref):
    half = pl.num_programs(0) // 2

    @pl.when(pl.program_id(0) < half)
    def _():
        other_ref[0] = part.astype(bf16)

    @pl.when(pl.program_id(0) >= half)
    def _():
        own_ref[0] = part.astype(bf16)


def front(place, hidden_all, ids, gains, small_blocks, inner_blocks):
    seqs, length, model = hidden_all.shape
    planes = len(inner_blocks)
    width = inner_blocks[0].shape[1]
    packed = TOKENS + BC_ROWS

    def kernel(*refs):
        front_kernel(gains.shape[0], planes, *refs)

    columns = small_blocks[0].shape[1]
    return per_sequence(
        kernel,
        place,
        [hidden_all, ids],
        [gains, *small_blocks, *inner_blocks],
        [
            ((seqs, length, model), bf16, "every"),
            ((seqs, length, width), f32, "every"),
            ((seqs, length, width), bf16, "every"),
            ((seqs, packed, RANK), f32, "every"),
            ((seqs, length, MASKS), f32, "every"),
            ((width, columns), bf16, "whole"),
            ((LANES, width), f32, "whole"),
            ((1, model), f32, "whole"),
        ],
        [pltpu.VMEM((model, width), bf16)],
        2 * seqs * length * model * width,
        "front",
    )


def middle(place, normed, upstream, scanned, conv_out, rest, blocks):
    seqs, length, model = normed.shape
    width = conv_out.shape[2]
    planes = len(blocks)

    def kernel(place_ref, normed_ref, up_ref, y_ref, conv_ref, chan_ref, *refs):
        own_ref, other_ref, mixed_ref, gy_ref, ggate_ref, gskip_ref, w_gate, w_out = refs[planes:]
        put_combined(place_ref, refs[:planes], w_gate, w_out)

        @pl.when(pl.program_id(0) == 0)
        def _():
            gskip_ref[...] = jnp.zeros_like(gskip_ref)

        gate = dot(normed_ref[0], w_gate[...], ((1,), (0,)))
        conv = conv_ref[0].astype(f32)
        sigma = jax.nn.sigmoid(gate)
        act = gate * sigma
        mixer = y_ref[0] + chan_row(chan_ref, KCONV + NSTATE + 2) * conv
        mixed = (mixer * act).astype(bf16)
        mixed_ref[0] = mixed
        put_part(dot(mixed, w_out[...], ((1,), (0,))), own_ref, other_ref)
        grad_mixed = dot(up_ref[0], w_out[...], ((1,), (1,)))
        gy = grad_mixed * act
        gy_ref[0] = gy
        ggate_ref[0] = (grad_mixed * mixer * (sigma * (1.0 + gate * (1.0 - sigma)))).astype(bf16)
        gskip_ref[...] += jnp.sum((gy * conv).reshape(length // SUBS, SUBS, width), axis=0)

    return per_sequence(
        kernel,
        place,
        [normed, upstream, scanned, conv_out],
        [rest, *blocks],
        [
            ((seqs // 2, length, model), bf16, "own"),
            ((seqs // 2, length, model), bf16, "other"),
            ((seqs, length, width), bf16, "every"),
            ((seqs, length, width), f32, "every"),
            ((seqs, length, width), bf16, "every"),
            ((SUBS, width), f32, "whole"),
        ],
        [pltpu.VMEM((model, width), bf16), pltpu.VMEM((width, model), bf16)],
        6 * seqs * length * model * width,
        "middle",
    )


def back_conv(place, grad_conv, gp_dt, gp_bc, inner, conv_out, masks, small, rest):
    seqs, length, width = grad_conv.shape

    def kernel(
        place_ref, gconv_ref, gdt_ref, gbc_ref, inner_ref, conv_ref, mask_ref, small_ref, rest_ref,
        ginner_ref, sums_ref, gxbc_ref,
    ):
        @pl.when(pl.program_id(0) == 0)
        def _():
            sums_ref[...] = jnp.zeros_like(sums_ref)
            gxbc_ref[...] = jnp.zeros_like(gxbc_ref)

        masks_now = mask_ref[0]
        terms = earlier_rows(inner_ref[0], masks_now)
        pre = conv_sum(terms, rest_ref)
        packed = gbc_ref[0].astype(bf16)
        gbc = jnp.concatenate([packed[i * CH : (i + 1) * CH] for i in range(length // LANES)], axis=1)
        gxbc_ref[...] += dot(gbc, conv_ref[0], ((1,), (0,)))
        total = gconv_ref[0] + dot(gdt_ref[0], small_ref[:, pl.ds(0, RANK)], ((1,), (1,)))
        total = total + dot(gbc, rest_ref[pl.ds(0, CH), :].astype(bf16), ((0,), (0,)))
        grad = total * silu_slope(pre)
        for k in range(KCONV):
            sums_ref[k] += jnp.sum((grad * terms[k]).reshape(length // SUBS, SUBS, width), axis=0)
        sums_ref[KCONV] += jnp.sum(grad.reshape(length // SUBS, SUBS, width), axis=0)
        ginner = chan_row(rest_ref, KCONV - 1) * grad
        for k in range(KCONV - 1):
            moved = pltpu.roll(grad * masks_now[:, k : k + 1], length - (KCONV - 1 - k), 0)
            ginner = ginner + chan_row(rest_ref, k) * moved
        ginner_ref[0] = ginner.astype(bf16)

    return per_sequence(
        kernel,
        place,
        [grad_conv, gp_dt, gp_bc, inner, conv_out, masks],
        [small, rest],
        [
            ((seqs, length, width), bf16, "every"),
            ((KCONV + 1, SUBS, width), f32, "whole"),
            ((CH, width), f32, "whole"),
        ],
        [],
        2 * seqs * length * width * RANK,
        "back_conv",
    )


def back_normed(place, grad_inner, grad_gate, hidden_all, inner_blocks, blocks):
    seqs, length, width = grad_inner.shape
    model = hidden_all.shape[2]
    planes = len(blocks)

    def kernel(place_ref, ginner_ref, ggate_ref, hid_ref, *refs):
        inners, gates = refs[:planes], refs[planes : 2 * planes]
        own_ref, other_ref, ggain_ref, w_inner, w_gate = refs[2 * planes :]
        put_blocks(place_ref, inners, w_inner)
        put_combined(place_ref, gates, w_gate, None)

        @pl.when(pl.program_id(0) == 0)
        def _():
            ggain_ref[...] = jnp.zeros_like(ggain_ref)

        part = dot(ginner_ref[0], w_inner[...], ((1,), (1,))) + dot(ggate_ref[0], w_gate[...], ((1,), (1,)))
        put_part(part, own_ref, other_ref)
        ggain_ref[...] += jnp.sum((part * normalised(hid_ref[0])).reshape(length // SUBS, SUBS, model), axis=0)

    return per_sequence(
        kernel,
        place,
        [grad_inner, grad_gate, hidden_all],
        [*inner_blocks, *blocks],
        [
            ((seqs // 2, length, model), bf16, "own"),
            ((seqs // 2, length, model), bf16, "other"),
            ((SUBS, model), f32, "whole"),
        ],
        [pltpu.VMEM((model, width), bf16), pltpu.VMEM((model, width), bf16)],
        4 * seqs * length * model * width,
        "back_normed",
    )


MESH = pl.DeviceIdType.MESH


class Peers:
    def __init__(self):
        self.r = lax.axis_index("rep")
        shard = lax.axis_index("shard")
        self.z, self.c = shard // 2, shard % 2

    @staticmethod
    def flip(i, k):
        return (i, i + 1 - 2 * (i % 2), (i + 2) % 4, 3 - i)[k]

    def rep(self, k):
        return {"rep": self.flip(self.r, k)}

    def plane(self, k):
        return {"shard": 2 * self.flip(self.z, k) + self.c}

    def core(self):
        return {"shard": 2 * self.z + 1 - self.c}

    def greet(self, planes):
        devices = [self.core()] + [self.rep(k) for k in (1, 2, 3)]
        if planes:
            devices += [self.plane(k) for k in (1, 2, 3)]
        barrier = pltpu.get_barrier_semaphore()
        for device in devices:
            pl.semaphore_signal(barrier, inc=1, device_id=device, device_id_type=MESH)
        pl.semaphore_wait(barrier, len(devices))


class Sends:
    def __init__(self, send_sems, recv_sems):
        self.send_sems, self.recv_sems = send_sems, recv_sems
        self.made = {}

    def make(self, slot, source, target, device):
        copy = pltpu.make_async_remote_copy(
            src_ref=source,
            dst_ref=target,
            send_sem=self.send_sems.at[slot],
            recv_sem=self.recv_sems.at[slot],
            device_id=device,
            device_id_type=MESH,
        )
        self.made[slot] = copy
        return copy

    def start(self, slot, source, target, device):
        self.make(slot, source, target, device).start()

    def arrived(self, *slots):
        for slot in slots:
            self.made[slot].wait_recv()

    def sent(self, *slots):
        for slot in slots:
            self.made[slot].wait_send()


def gather_first_kernel(
    hid, cot, in_own, in_other, small, gain, ids,
    hid_all, cot_all, weights, gate, small_all, gain_all, ids_all, send_sems, recv_sems, local_sems,
):
    me = Peers()
    net = Sends(send_sems, recv_sems)
    rows = in_own.shape[0]
    width = in_own.shape[1] // 2
    half = hid.shape[0] // 2
    low, high = pl.ds(0, half), pl.ds(half, half)
    inside = (me.z == 1) | (me.z == 2)
    outside = (me.z == 0) | (me.z == 3)
    mine = pl.ds(pl.multiple_of(me.c * rows, rows), rows)
    local = [
        pltpu.make_async_copy(hid, hid_all.at[0], local_sems.at[0]),
        pltpu.make_async_copy(cot, cot_all.at[0], local_sems.at[1]),
    ]
    for copy in local:
        copy.start()
    weights[0, mine, :] = in_own[:, :width]
    gate[mine, :] = in_own[:, width:]
    small_all[0] = small[...]
    gain_all[0] = gain[...]
    ids_all[0] = ids[...]
    me.greet(True)
    net.start(0, in_other.at[:, pl.ds(0, width)], weights.at[0, mine], me.core())
    net.start(26, in_other.at[:, pl.ds(width, width)], gate.at[mine], me.core())
    for k in (1, 2, 3):
        net.start(k, ids, ids_all.at[k], me.rep(k))
        net.start(3 + k, gain, gain_all.at[k], me.plane(k))
        net.start(6 + k, small, small_all.at[k], me.plane(k))
    net.start(10, hid.at[high], hid_all.at[1, high], me.rep(1))
    net.start(11, hid.at[low], hid_all.at[2, low], me.rep(2))
    net.start(12, hid.at[low], hid_all.at[1, low], me.rep(1))
    net.start(13, hid.at[high], hid_all.at[2, high], me.rep(2))
    net.start(14, hid, hid_all.at[4], me.core())
    net.arrived(0)
    own = weights.at[0]
    net.start(15, own, weights.at[2], me.plane(2))
    net.start(16, own, weights.at[1], me.plane(1))
    across = net.make(17, own, weights.at[3], me.plane(3))
    net.arrived(1, 2, 3, 4, 5, 6)
    net.start(18, ids_all.at[pl.ds(0, 4)], ids_all.at[pl.ds(4, 4)], me.core())
    net.start(19, gain_all.at[pl.ds(0, 4)], gain_all.at[pl.ds(4, 4)], me.core())
    net.arrived(10, 11)
    net.start(20, hid_all.at[1, high], hid_all.at[3, high], me.rep(2))
    net.start(21, hid_all.at[2, low], hid_all.at[3, low], me.rep(1))
    net.start(27, cot.at[high], cot_all.at[1, high], me.rep(1))
    net.start(28, cot.at[low], cot_all.at[2, low], me.rep(2))
    net.start(29, cot.at[low], cot_all.at[1, low], me.rep(1))
    net.start(30, cot.at[high], cot_all.at[2, high], me.rep(2))
    net.start(31, cot, cot_all.at[4], me.core())
    net.arrived(12)
    net.start(22, hid_all.at[1], hid_all.at[5], me.core())
    net.arrived(13)
    net.start(23, hid_all.at[2], hid_all.at[6], me.core())
    net.arrived(15)
    onward = net.make(24, weights.at[2], weights.at[3], me.plane(1))

    @pl.when(inside)
    def _():
        across.start()
        onward.start()

    net.arrived(20, 21)
    net.start(25, hid_all.at[3], hid_all.at[7], me.core())
    net.arrived(16)

    @pl.when(inside)
    def _():
        across.wait_recv()

    @pl.when(outside)
    def _():
        onward.wait_recv()

    net.arrived(27, 28)
    net.start(32, cot_all.at[1, high], cot_all.at[3, high], me.rep(2))
    net.start(33, cot_all.at[2, low], cot_all.at[3, low], me.rep(1))
    net.arrived(29)
    net.start(34, cot_all.at[1], cot_all.at[5], me.core())
    net.arrived(30)
    net.start(35, cot_all.at[2], cot_all.at[6], me.core())
    net.arrived(32, 33)
    net.start(36, cot_all.at[3], cot_all.at[7], me.core())
    net.arrived(7, 8, 9, 14, 18, 19, 22, 23, 25, 26, 31, 34, 35, 36)
    for copy in local:
        copy.wait()
    net.sent(*[slot for slot in net.made if slot not in (17, 24)])

    @pl.when(inside)
    def _():
        across.wait_send()
        onward.wait_send()


def gather_first(hid, cot, in_own, in_other, small, gain, ids):
    length, model = hid.shape
    rows, width = in_own.shape[0], in_own.shape[1] // 2
    anywhere = pl.BlockSpec(memory_space=pl.ANY)
    vmem = pl.BlockSpec(memory_space=pltpu.VMEM)
    return pl.pallas_call(
        gather_first_kernel,
        in_specs=[vmem] * 7,
        out_specs=[anywhere] * 2 + [vmem] * 5,
        out_shape=[
            jax.ShapeDtypeStruct((8, length, model), bf16),
            jax.ShapeDtypeStruct((8, length, model), bf16),
            jax.ShapeDtypeStruct((4, 2 * rows, width), bf16),
            jax.ShapeDtypeStruct((2 * rows, width), bf16),
            jax.ShapeDtypeStruct((4,) + small.shape, bf16),
            jax.ShapeDtypeStruct((8,) + gain.shape, f32),
            jax.ShapeDtypeStruct((8,) + ids.shape, f32),
        ],
        scratch_shapes=[
            pltpu.SemaphoreType.DMA((37,)),
            pltpu.SemaphoreType.DMA((37,)),
            pltpu.SemaphoreType.DMA((2,)),
        ],
        compiler_params=pltpu.CompilerParams(
            collective_id=1, has_side_effects=True, vmem_limit_bytes=24 * 2**20
        ),
        cost_estimate=pl.CostEstimate(flops=0, bytes_accessed=100 * 10**6, transcendentals=0),
        name="gather_first",
    )(hid, cot, in_own, in_other, small, gain, ids)


def reduce_plane_kernel(part, dt_all, bc_all, near, pair, far, send_sems, recv_sems):
    me = Peers()
    net = Sends(send_sems, recv_sems)
    tokens = dt_all.shape[1]
    me.greet(False)
    for k in (1, 2, 3, 0):
        net.start(k, part.at[4 + k], near.at[k], me.core())
    for k in (1, 2, 3):
        net.arrived(k)
        pair[k - 1] = part[k] + near[k]
        net.start(3 + k, pair.at[k - 1], far.at[k - 1], me.rep(k))
    net.arrived(0)
    total = part[0] + near[0]
    for k in (1, 2, 3):
        net.arrived(3 + k)
        total = total + far[k - 1]
    dt_all[0] = total[:tokens].astype(bf16)
    bc_all[0] = total[tokens:]
    for k in (1, 2, 3):
        net.start(6 + k, dt_all.at[0], dt_all.at[k], me.rep(k))
        net.start(9 + k, bc_all.at[0], bc_all.at[k], me.rep(k))
    net.start(13, dt_all.at[0], dt_all.at[4], me.core())
    net.start(14, bc_all.at[0], bc_all.at[4], me.core())
    for k in (1, 2, 3):
        net.arrived(6 + k, 9 + k)
        net.start(14 + k, dt_all.at[k], dt_all.at[4 + k], me.core())
        net.start(17 + k, bc_all.at[k], bc_all.at[4 + k], me.core())
    net.arrived(13, 14, 15, 16, 17, 18, 19, 20)
    net.sent(*net.made)


def reduce_plane(part, collective):
    seqs, rows, _ = part.shape
    tokens = rows - 2 * 2 * NSTATE
    vmem = pl.BlockSpec(memory_space=pltpu.VMEM)
    return pl.pallas_call(
        reduce_plane_kernel,
        in_specs=[vmem],
        out_specs=[vmem, vmem],
        out_shape=[
            jax.ShapeDtypeStruct((seqs, tokens, RANK), bf16),
            jax.ShapeDtypeStruct((seqs, rows - tokens, RANK), f32),
        ],
        scratch_shapes=[
            pltpu.VMEM((4, rows, RANK), f32),
            pltpu.VMEM((3, rows, RANK), f32),
            pltpu.VMEM((3, rows, RANK), f32),
            pltpu.SemaphoreType.DMA((21,)),
            pltpu.SemaphoreType.DMA((21,)),
        ],
        compiler_params=pltpu.CompilerParams(
            collective_id=collective, has_side_effects=True, vmem_limit_bytes=16 * 2**20
        ),
        cost_estimate=pl.CostEstimate(flops=0, bytes_accessed=50 * 10**6, transcendentals=0),
        name="reduce_plane",
    )(part)


def finish_kernel(
    part, other_part, gin, small, grad_normed, pieces, small_all,
    own_part, core_part, pair, far_one, far_two, from_one, from_two,
    blocks, ends, middle_block, block_one, block_two, two_out, total, small_own, small_in, small_total,
    send_sems, recv_sems, local_sems,
):
    me = Peers()
    net = Sends(send_sems, recv_sems)
    half = part.shape[1] // 2
    low, high = pl.ds(0, half), pl.ds(half, half)
    rows = gin.shape[0] // 4
    small_rows = small.shape[0] // 4
    own_rows = rows // 2
    inside = (me.z == 1) | (me.z == 2)
    outside = (me.z == 0) | (me.z == 3)

    def block(ref, k, size):
        return ref.at[pl.ds(pl.multiple_of(me.flip(me.z, k) * size, size), size)]

    local = [
        pltpu.make_async_copy(part, own_part, local_sems.at[0]),
        pltpu.make_async_copy(block(gin, 0, rows), blocks.at[0], local_sems.at[1]),
        pltpu.make_async_copy(block(gin, 2, rows), blocks.at[1], local_sems.at[2]),
        pltpu.make_async_copy(block(small, 0, small_rows), small_own, local_sems.at[3]),
    ]
    for copy in local:
        copy.start()
    me.greet(True)
    for i, k in enumerate((3, 1, 2, 0)):
        net.start(i, other_part.at[k], core_part.at[k], me.core())
    to_ends = net.make(7, block(gin, 3, rows), ends, me.plane(1))
    to_middle = net.make(8, block(gin, 3, rows), middle_block, me.plane(3))

    @pl.when(outside)
    def _():
        to_ends.start()

    @pl.when(inside)
    def _():
        to_middle.start()

    two = net.make(9, two_out, block_two, me.plane(2))
    local[2].wait()
    local[0].wait()
    for i, k in enumerate((3, 1, 2)):
        net.arrived(i)
        pair[k - 1] = (own_part[k].astype(f32) + core_part[k].astype(f32)).astype(bf16)
        if k == 3:
            net.start(11, pair.at[2, low], far_one, me.rep(1))
            net.start(12, pair.at[2, high], far_two, me.rep(2))
        elif k == 1:
            net.start(13, pair.at[0, low], from_one.at[low], me.rep(1))
        else:
            net.start(14, pair.at[1, high], from_two.at[high], me.rep(2))

    @pl.when(outside)
    def _():
        to_ends.wait_send()
        two_out[...] = blocks[1]
        two.start()

    net.start(10, block(gin, 1, rows), block_one, me.plane(1))

    @pl.when(inside)
    def _():
        to_ends.wait_recv()
        two_out[...] = (blocks[1].astype(f32) + ends[...].astype(f32)).astype(bf16)
        two.start()

    for k in (1, 2, 3):
        net.start(3 + k, block(small, k, small_rows), small_in.at[k - 1], me.plane(k))
    net.arrived(11)
    pair[1, low] = (pair[1, low].astype(f32) + far_one[...].astype(f32)).astype(bf16)
    net.start(15, pair.at[1, low], from_two.at[low], me.rep(2))
    net.arrived(12)
    pair[0, high] = (pair[0, high].astype(f32) + far_two[...].astype(f32)).astype(bf16)
    net.start(16, pair.at[0, high], from_one.at[high], me.rep(1))
    local[1].wait()
    net.arrived(10, 9)
    summed = blocks[0].astype(f32) + block_one[...].astype(f32) + block_two[...].astype(f32)

    @pl.when(inside)
    def _():
        to_middle.wait_recv()
        total[...] = (summed + middle_block[...].astype(f32)).astype(bf16)

    @pl.when(outside)
    def _():
        total[...] = summed.astype(bf16)

    mine = total.at[pl.ds(pl.multiple_of(me.c * own_rows, own_rows), own_rows)]
    other = total.at[pl.ds(pl.multiple_of((1 - me.c) * own_rows, own_rows), own_rows)]
    net.start(20, other, pieces.at[4], me.core())
    kept = pltpu.make_async_copy(mine, pieces.at[0], local_sems.at[5])
    kept.start()
    for k in (1, 2, 3):
        net.start(20 + k, mine, pieces.at[k], me.rep(k))
    net.arrived(20)
    for k in (1, 2, 3):
        net.start(23 + k, pieces.at[4], pieces.at[4 + k], me.rep(k))
    local[3].wait()
    net.arrived(4, 5, 6)
    small_total[...] = small_own[...] + small_in[0] + small_in[1] + small_in[2]
    kept_small = pltpu.make_async_copy(small_total, small_all.at[0], local_sems.at[4])
    kept_small.start()
    for k in (1, 2, 3):
        net.start(16 + k, small_total, small_all.at[k], me.rep(k))
    net.arrived(3)
    net.arrived(13, 14, 15, 16)
    grad_normed[...] = (
        own_part[0].astype(f32) + core_part[0].astype(f32) + from_one[...].astype(f32) + from_two[...].astype(f32)
    )
    net.arrived(17, 18, 19, 21, 22, 23, 24, 25, 26)
    kept.wait()
    kept_small.wait()
    net.sent(*[slot for slot in net.made if slot not in (7, 8)])

    @pl.when(inside)
    def _():
        to_middle.wait_send()


def finish(part, other_part, gin, small):
    _, length, model = part.shape
    rows, width = gin.shape[0] // 4, gin.shape[1]
    small_rows, cols = small.shape[0] // 4, small.shape[1]
    anywhere = pl.BlockSpec(memory_space=pl.ANY)
    big = (length, model)
    return pl.pallas_call(
        finish_kernel,
        in_specs=[anywhere] * 4,
        out_specs=[pl.BlockSpec(memory_space=pltpu.VMEM), anywhere, anywhere],
        out_shape=[
            jax.ShapeDtypeStruct(big, f32),
            jax.ShapeDtypeStruct((8, rows // 2, width), bf16),
            jax.ShapeDtypeStruct((4, small_rows, cols), f32),
        ],
        scratch_shapes=[
            pltpu.VMEM((4,) + big, bf16),
            pltpu.VMEM((4,) + big, bf16),
            pltpu.VMEM((3,) + big, bf16),
            pltpu.VMEM((length // 2, model), bf16),
            pltpu.VMEM((length // 2, model), bf16),
            pltpu.VMEM(big, bf16),
            pltpu.VMEM(big, bf16),
            pltpu.VMEM((2, rows, width), bf16),
            pltpu.VMEM((rows, width), bf16),
            pltpu.VMEM((rows, width), bf16),
            pltpu.VMEM((rows, width), bf16),
            pltpu.VMEM((rows, width), bf16),
            pltpu.VMEM((rows, width), bf16),
            pltpu.VMEM((rows, width), bf16),
            pltpu.VMEM((small_rows, cols), f32),
            pltpu.VMEM((3, small_rows, cols), f32),
            pltpu.VMEM((small_rows, cols), f32),
            pltpu.SemaphoreType.DMA((27,)),
            pltpu.SemaphoreType.DMA((27,)),
            pltpu.SemaphoreType.DMA((6,)),
        ],
        compiler_params=pltpu.CompilerParams(
            collective_id=4, has_side_effects=True, vmem_limit_bytes=40 * 2**20
        ),
        cost_estimate=pl.CostEstimate(flops=0, bytes_accessed=150 * 10**6, transcendentals=0),
        name="finish",
    )(part, other_part, gin, small)


class Links:
    def __init__(self, reps, shard_size):
        self.reps, self.shard_size = reps, shard_size
        self.planes = shard_size // 2
        self.r = lax.axis_index("rep")
        shard = lax.axis_index("shard")
        self.plane, self.c = shard // 2, shard % 2

    def rep(self, value, k):
        return lax.ppermute(value, "rep", [(i, i ^ k) for i in range(self.reps)])

    def core(self, value):
        return lax.ppermute(value, "shard", [(i, i ^ 1) for i in range(self.shard_size)])

    def planes_pairs(self, pairs):
        return [(2 * a + core, 2 * b + core) for a, b in pairs for core in range(2)]

    def z(self, value, pairs):
        return lax.ppermute(value, "shard", self.planes_pairs(pairs))

    def z_xor(self, value, k):
        return self.z(value, [(i, i ^ k) for i in range(self.planes)])

    def gather_rep(self, value):
        if self.reps != 4:
            return [value] + [self.rep(value, k) for k in range(1, self.reps)]
        half = value.shape[0] // 2
        one, two = self.rep(value, 1), self.rep(value, 2)
        return [value, one, two, self.across(one, two, half)]

    def gather_rep_list(self, value):
        return [value] + [self.rep(value, k) for k in range(1, self.reps)]

    def gather_plane(self, value):
        near = jnp.stack([value] + [self.rep(value, k) for k in range(1, self.reps)])
        return jnp.concatenate([near, self.core(near)], axis=0)

    def scatter_plane(self, partial, wire):
        reps = self.reps
        pair = partial[:reps].astype(f32) + self.core(partial[reps:].astype(wire)).astype(f32)
        total = pair[0]
        for k in range(1, reps):
            total = total + self.rep(pair[k].astype(wire), k).astype(f32)
        return total

    def place_z(self, values):
        rows = values[0].shape[0]
        out = jnp.zeros((self.planes * rows,) + values[0].shape[1:], values[0].dtype)
        start = (0,) * (values[0].ndim - 1)
        for k, value in enumerate(values):
            out = lax.dynamic_update_slice(out, value, ((self.plane ^ k) * rows,) + start)
        return out

    def gather_z_list(self, value):
        return [value] + [self.z_xor(value, k) for k in range(1, self.planes)]

    def gather_z(self, value):
        return self.place_z(self.gather_z_list(value))

    def block_z(self, value, k):
        rows = value.shape[0] // self.planes
        return lax.dynamic_slice_in_dim(value, (self.plane ^ k) * rows, rows, 0)

    def send_z(self, value):
        return [self.z_xor(self.block_z(value, k), k) for k in range(1, self.planes)]

    def sum_z(self, value, moved):
        total = self.block_z(value, 0).astype(f32)
        for other in moved:
            total = total + other.astype(f32)
        return total.astype(value.dtype)

    def send_half(self, part, k):
        return self.rep(part[k : 2 * k], k)

    def sum_halves(self, part, moved):
        k = self.reps // 2
        while k > 1:
            part = (part[:k].astype(f32) + moved.astype(f32)).astype(part.dtype)
            k //= 2
            moved = self.send_half(part, k)
        return part[0].astype(f32) + moved[0].astype(f32)

    def add_pair(self, part, far):
        return (part.astype(f32) + far.astype(f32)).astype(bf16)

    def pair_rows(self, own, other):
        first = jnp.where(self.c == 0, own, other)
        second = jnp.where(self.c == 0, other, own)
        return jnp.stack([first, second])

    def order_reps(self, values):
        return order(values, self.r)

    def sum_plane(self, part, length, collective):
        if self.reps == 4 and self.planes == 4:
            return reduce_plane(part, collective)
        total = self.gather_plane(self.scatter_plane(part, f32))
        return total[:, :length].astype(bf16), total[:, length:]


def adam_step(master, first, second, gradient, rate, decays):
    first_new = beta_first * first + (1.0 - beta_first) * gradient
    second_new = beta_second * second + (1.0 - beta_second) * gradient * gradient
    update = (
        first_new
        / (1.0 - beta_first**ADAM_STEP)
        / (jnp.sqrt(second_new / (1.0 - beta_second**ADAM_STEP)) + adam_eps)
    )
    if decays:
        update = update + weight_decay * master
    return (first_new, second_new, master - rate * update)


def adam_in_kernel(place_ref, *refs):
    reps = (len(refs) - 9) // 2
    pieces = refs[: 2 * reps]
    master_ref, first_ref, second_ref = refs[2 * reps : 2 * reps + 3]
    first_out, second_out, master_out = refs[-3:]
    r, c = place_ref[0], place_ref[1]
    sub = LANES
    for e in range(2):
        for k in range(reps):
            at = ((c ^ e) * reps + (r ^ k)) * sub
            lanes = pl.ds(pl.multiple_of(at, sub), sub)
            gradient = pieces[e * reps + k][...].astype(f32)
            first, second, master = adam_step(
                master_ref[:, lanes], first_ref[:, lanes], second_ref[:, lanes], gradient,
                learn_rates[0], with_decay[0],
            )
            first_out[:, lanes] = first
            second_out[:, lanes] = second
            master_out[:, lanes] = master


def adam_in(place, half, pieces, master, first, second, earlier):
    rows, columns = master.shape
    reps = len(pieces) // 2
    sub = LANES
    block = 2 * reps * sub
    steps = columns // 2 // block
    wide = pl.BlockSpec((rows, block), lambda i, p: (0, half * steps + i))
    thin = [pl.BlockSpec((rows, sub), functools.partial(lambda at, i, p: (at, i), at)) for _, at in pieces]
    anywhere = pl.BlockSpec(memory_space=pl.ANY)
    if earlier is None:
        earlier = (master, first, second)
        aliases = {}
    else:
        aliases = {1 + 2 * reps + 3 + i: i for i in range(3)}
    return pl.pallas_call(
        adam_in_kernel,
        grid_spec=pltpu.PrefetchScalarGridSpec(
            num_scalar_prefetch=1,
            grid=(steps,),
            in_specs=thin + [wide] * 3 + [anywhere] * 3,
            out_specs=[wide] * 3,
        ),
        out_shape=[jax.ShapeDtypeStruct(master.shape, f32)] * 3,
        input_output_aliases=aliases,
        compiler_params=pltpu.CompilerParams(vmem_limit_bytes=32 * 2**20),
        cost_estimate=pl.CostEstimate(flops=10 * master.size, bytes_accessed=13 * master.size, transcendentals=master.size),
        name="adam_in",
    )(place, *[array for array, _ in pieces], master, first, second, *earlier)


def adam_out_kernel(place_ref, *refs):
    reps = len(refs) - 6
    master_ref, first_ref, second_ref, first_out, second_out, master_out = refs[reps:]
    for k in range(reps):

        @pl.when(pl.program_id(0) == k)
        def _():
            first_out[...], second_out[...], master_out[...] = adam_step(
                master_ref[...], first_ref[...], second_ref[...], refs[k][...].astype(f32),
                learn_rates[3], with_decay[3],
            )


def adam_out(place, pieces, master, first, second):
    rows, columns = master.shape
    reps = len(pieces)
    sub = rows // reps
    high, wide = pieces[0].shape
    first_block = high // 2 // sub
    mine = pl.BlockSpec((sub, wide), lambda k, j, p: (p[0] ^ k, j))
    piece = pl.BlockSpec((sub, wide), lambda k, j, p: (first_block + j, 0))
    return pl.pallas_call(
        adam_out_kernel,
        grid_spec=pltpu.PrefetchScalarGridSpec(
            num_scalar_prefetch=1,
            grid=(reps, columns // wide),
            in_specs=[piece] * reps + [mine] * 3,
            out_specs=[mine] * 3,
        ),
        out_shape=[jax.ShapeDtypeStruct(master.shape, f32)] * 3,
        compiler_params=pltpu.CompilerParams(vmem_limit_bytes=32 * 2**20),
        cost_estimate=pl.CostEstimate(flops=10 * master.size, bytes_accessed=26 * master.size, transcendentals=master.size),
        name="adam_out",
    )(place, *pieces, master, first, second)


def slice_in_kernel(place_ref, own_ref, other_ref, out_ref):
    out_ref[0] = own_ref[...].astype(bf16)
    out_ref[1] = other_ref[...].astype(bf16)


def slice_in(place, master, reps):
    rows, columns = master.shape
    blocks = columns // (2 * reps * LANES)

    def of_core(e):
        return pl.BlockSpec((rows, LANES), lambda b, p: (0, (2 * b + (p[1] ^ e)) * reps + p[0]))

    return pl.pallas_call(
        slice_in_kernel,
        grid_spec=pltpu.PrefetchScalarGridSpec(
            num_scalar_prefetch=1,
            grid=(blocks,),
            in_specs=[of_core(0), of_core(1)],
            out_specs=pl.BlockSpec((2, rows, LANES), lambda b, p: (0, 0, b)),
        ),
        out_shape=jax.ShapeDtypeStruct((2, rows, blocks * LANES), bf16),
        name="slice_in",
    )(place, master, master)


def after(value, *earlier):
    return lax.optimization_barrier((value, *earlier))[0]


def after_all(values, *earlier):
    return list(lax.optimization_barrier((*values, *earlier))[: len(values)])


def to_columns(values, width):
    *lead, rows, columns = values.shape
    blocks = values.reshape(*lead, rows, columns // width, width)
    return jnp.swapaxes(blocks, -3, -2).reshape(*lead, rows * columns // width, width)


def order(values, index):
    bit = 1
    while bit < len(values):
        swap = (index & bit) != 0
        values = [jnp.where(swap, values[i ^ bit], values[i]) for i in range(len(values))]
        bit *= 2
    return jnp.stack(values)


def shards(
    reps, shard_size,
    hidden, segments, cotangent,
    in_master, in_first, in_second,
    x_master, x_first, x_second,
    dt_master, dt_first, dt_second,
    out_master, out_first, out_second,
    chan_master, chan_first, chan_second,
    gain_master, gain_first, gain_second,
):
    net = Links(reps, shard_size)
    planes, r, c = net.planes, net.r, net.c
    length, model = hidden.shape[1:]
    in_rows = in_master.shape[0]
    own_chan = out_master.shape[0]
    sub = own_chan // reps
    width = planes * sub
    xcols = x_master.shape[1]
    chan_cols = chan_master.shape[1]
    seqs = 2 * reps

    def sub_rows(value):
        return lax.dynamic_slice_in_dim(value, r * sub, sub, 0)

    def own_rows(rows):
        rows = rows.reshape(2, in_rows, width)
        own = lax.dynamic_index_in_dim(rows, c, 0, keepdims=False)
        return own, net.core(lax.dynamic_index_in_dim(rows, 1 - c, 0, keepdims=False))

    def full_in(pieces):
        own = net.order_reps(pieces[:reps])
        other = net.order_reps(pieces[reps:])
        every = net.pair_rows(own, other).reshape(2, reps, in_rows, planes, sub)
        return every.transpose(2, 3, 0, 1, 4).reshape(in_rows, width * seqs).astype(f32)

    place = jnp.stack([r, c, net.plane]).astype(jnp.int32)
    own_hidden = hidden[0]
    tiled = sub % LANES == 0
    fast = tiled and reps == 4 and planes == 4
    if tiled:
        in_own, in_other = slice_in(place, in_master, reps)
    else:
        in_view = in_master.reshape(in_rows, 2, planes, 2, reps, sub)
        in_mine = lax.dynamic_index_in_dim(in_view, r, 4, keepdims=False).astype(bf16)
        in_own = lax.dynamic_index_in_dim(in_mine, c, 3, keepdims=False).reshape(in_rows, 2 * width)
        in_other = lax.dynamic_index_in_dim(in_mine, 1 - c, 3, keepdims=False).reshape(in_rows, 2 * width)
    x_mine = sub_rows(x_master)
    small = jnp.concatenate([x_mine[:, :RANK], sub_rows(dt_master), x_mine[:, RANK:], sub_rows(chan_master)], axis=1)
    small = jnp.pad(small.astype(bf16), ((0, 0), (0, -small.shape[1] % LANES)))
    out_mine = sub_rows(out_master).astype(bf16)
    own_gain = lax.reduce_precision(gain_master, 8, 7)[None]
    own_ids = segments.astype(f32)
    if fast:
        hidden_all, upstream, inner_blocks, gate_pair, small_parts, gains, ids = gather_first(
            own_hidden, cotangent[0], in_own, in_other, small, own_gain, own_ids
        )
        inner_blocks = [inner_blocks[k] for k in range(planes)]
        small_blocks = [small_parts[k] for k in range(planes)]
    else:
        ids = net.gather_plane(own_ids).reshape(seqs, 1, length)
        gain_pair = net.pair_rows(own_gain[0], net.core(own_gain[0])).reshape(2 * in_rows)
        gains = net.gather_z(gain_pair).reshape(1, 1, model)
        small_blocks = net.gather_z_list(small)
        in_pair = net.pair_rows(in_own, net.core(in_other)).reshape(2 * in_rows, 2 * width)
        inner_blocks = net.gather_z_list(in_pair[:, :width])
        hidden_all = net.gather_plane(own_hidden)
        upstream = net.gather_plane(cotangent[0])
        gate_pair = in_pair[:, width:]
    blocks = net.gather_z_list(jnp.concatenate([gate_pair, to_columns(out_mine, width)]))
    normed, inner, conv_out, proj_part, masks, small_all, rest, gain = front(
        place, hidden_all, ids, gains, small_blocks, inner_blocks
    )
    dt_in, bc = net.sum_plane(proj_part, length, 2)
    bc = bc.reshape(-1, LANES)
    scanned, starts = scan_forward(dt_in, masks, conv_out, bc, small_all, rest)
    out_own, out_other, mixed, grad_y, grad_gate, grad_skip = middle(
        place, normed, upstream, scanned, conv_out, rest, blocks
    )
    out_far = net.core(out_other)
    grad_out = dot(mixed.reshape(-1, width), upstream.reshape(-1, model), ((0,), (0,))).astype(bf16)
    flat_normed = normed.reshape(-1, model)
    gin_gate = dot(flat_normed, grad_gate.reshape(-1, width), ((0,), (0,))).astype(bf16)
    grad_rows = jnp.concatenate(
        [gin_gate.reshape(planes, -1, width), to_columns(grad_out.reshape(planes, sub, model), width)], axis=1
    ).reshape(-1, width)
    grad_rows_moved = net.send_z(grad_rows)
    pair = net.add_pair(out_own, out_far)
    out_first_half = net.send_half(pair, reps // 2)
    grad_y = after(grad_y, grad_rows, pair)

    grad_conv, grad_dtlow, proj_back, grad_rates, grad_dtbias = scan_backward(
        dt_in, masks, conv_out, bc, small_all, rest, starts, grad_y
    )
    grad_rates = jnp.sum(grad_rates, axis=1).T
    rates = -jnp.exp(rest[CH + KCONV : CH + KCONV + NSTATE].T)
    grad_dt = dot(grad_dtlow.reshape(-1, width), dt_in.reshape(-1, RANK), ((0,), (0,)))
    out_sum = net.sum_halves(pair, after(out_first_half, proj_back))
    layer_output = (hidden[0].astype(f32) + out_sum).astype(bf16)
    grad_rows = net.sum_z(grad_rows, after_all(grad_rows_moved, proj_back))
    gate_rows = own_rows(grad_rows[: 2 * in_rows])
    pieces = jnp.concatenate([*gate_rows, grad_rows[2 * in_rows :]])
    proj_back = after(proj_back, pieces)
    gp_dt, gp_bc = net.sum_plane(proj_back.reshape(seqs, TOKENS + BC_ROWS, LANES), length, 3)
    pieces = net.gather_rep_list(after(pieces, gp_dt))
    grad_xdt = dot(conv_out.reshape(-1, width), gp_dt.reshape(-1, RANK), ((0,), (0,)))
    grad_inner, conv_sums, grad_xbc = back_conv(
        place, grad_conv, gp_dt, gp_bc, inner, conv_out, masks, small_all, rest
    )
    grad_x = jnp.concatenate([grad_xdt, grad_xbc.T], axis=1)
    gin_inner = dot(flat_normed, grad_inner.reshape(-1, width), ((0,), (0,))).astype(bf16)
    back_own, back_other, grad_gain = back_normed(place, grad_inner, grad_gate, hidden_all, inner_blocks, blocks)
    out_new = adam_out(
        place, pieces, out_master, out_first, out_second
    )
    grad_small = jnp.concatenate(
        [
            grad_x,
            grad_dt,
            jnp.sum(conv_sums[:KCONV], axis=1).T,
            grad_rates * rates,
            jnp.sum(conv_sums[KCONV], axis=0)[:, None],
            jnp.sum(grad_dtbias, axis=0)[:, None],
            jnp.sum(grad_skip, axis=0)[:, None],
            jnp.sum(grad_gain, axis=0).reshape(width, reps),
        ],
        axis=1,
    )
    if fast:
        grad_small = jnp.pad(grad_small, ((0, 0), (0, -grad_small.shape[1] % LANES)))
        grad_small = after(grad_small, *pieces)
        grad_normed, inner_pieces, small_sum = finish(back_own, back_other, gin_inner, grad_small)
        inner_pieces = [(inner_pieces.reshape(-1, width), e * reps + k) for e in range(2) for k in range(reps)]
        small_sum = net.order_reps(list(small_sum))
    else:
        grad_normed = net.scatter_plane(jnp.concatenate([back_own, back_other]), bf16)
        inner_own_rows, inner_other_rows = own_rows(net.sum_z(gin_inner, net.send_z(gin_inner)))
        inner_pieces = net.gather_rep(inner_own_rows) + net.gather_rep(inner_other_rows)
        small_sum = net.order_reps(net.gather_rep(net.sum_z(grad_small, net.send_z(grad_small))))
    own_res = hidden[0].astype(f32)
    own_inv = lax.rsqrt(jnp.mean(own_res * own_res, axis=1, keepdims=True) + norm_eps)
    grad_scaled = grad_normed * gain
    input_grad = (
        own_inv * grad_scaled
        - own_res * own_inv**3 * jnp.mean(grad_scaled * own_res, axis=1, keepdims=True)
        + cotangent[0].astype(f32)
    ).astype(bf16)

    if tiled:
        gate_pieces = [(pieces[k], e) for e in range(2) for k in range(reps)]
        in_new = adam_in(place, 1, gate_pieces, in_master, in_first, in_second, None)
        in_new = adam_in(place, 0, inner_pieces, in_master, in_first, in_second, in_new)
    else:
        gate_pieces = [pieces[k][e * in_rows : (e + 1) * in_rows] for e in range(2) for k in range(reps)]
        in_sum = jnp.concatenate([full_in(inner_pieces), full_in(gate_pieces)], axis=1)
        in_new = adam_step(in_master, in_first, in_second, in_sum, learn_rates[0], with_decay[0])
    gain_cols = slice(xcols + RANK + chan_cols, xcols + RANK + chan_cols + reps)
    gain_two = jnp.sum(small_sum[:, :, gain_cols], axis=0).reshape(2, in_rows)
    gain_own = lax.dynamic_index_in_dim(gain_two, c, 0, keepdims=False)
    gain_sum = gain_own + net.core(lax.dynamic_index_in_dim(gain_two, 1 - c, 0, keepdims=False))
    small_sum = small_sum.reshape(own_chan, -1)
    x_sum = small_sum[:, :xcols]
    dt_sum = small_sum[:, xcols : xcols + RANK]
    chan_sum = small_sum[:, xcols + RANK : xcols + RANK + chan_cols]

    def update(position, master, first, second, gradient):
        return adam_step(master, first, second, gradient, learn_rates[position], with_decay[position])

    updated = (
        *in_new,
        *update(1, x_master, x_first, x_second, x_sum),
        *update(2, dt_master, dt_first, dt_second, dt_sum),
        *out_new,
        *update(4, chan_master, chan_first, chan_second, chan_sum),
        *update(5, gain_master, gain_first, gain_second, gain_sum),
    )
    return (layer_output[None], input_grad[None], *updated)


def solution(mesh):
    token = P(("rep", "shard"), None, None)
    rows = P("shard", None)
    placed = (token, P(("rep", "shard"), None), token) + (rows,) * 15 + (P("shard"),) * 3
    return jax.shard_map(
        functools.partial(shards, mesh.shape["rep"], mesh.shape["shard"]),
        mesh=mesh,
        in_specs=placed,
        out_specs=(token, token) + (rows,) * 15 + (P("shard"),) * 3,
        check_vma=False,
    )
```

```python
import functools

import jax
import jax.numpy as jnp
from jax import lax
from jax.experimental import pallas as pl
from jax.experimental.pallas import tpu as pltpu
from jax.sharding import PartitionSpec as P

NSTATE = 16
RANK = 128
KCONV = 4
ADAM_STEP = 10
CHUNK = 32
LANES = 128
SUBS = 8
CUT = 1e30
MASKS = 8
MOST = 58 * 2**20
TOKENS = 256
BC_ROWS = TOKENS * 2 * NSTATE // LANES
CH = 2 * NSTATE
FWD_UNROLL = 8
BWD_UNROLL = 4
LOG2E = 1.4426950408889634

norm_eps = 1e-05
beta_first = 0.9
beta_second = 0.95
adam_eps = 1e-08
weight_decay = 0.1
learn_rates = (0.044, 0.03, 0.18, 0.09, 1.0, 0.6)
with_decay = (True, True, True, True, False, False)

bf16 = jnp.bfloat16
f32 = jnp.float32


def silu_slope(values):
    sigma = jax.nn.sigmoid(values)
    return sigma * (1.0 + values * (1.0 - sigma))


def dot(a, b, dims):
    return lax.dot_general(a, b, (dims, ((), ())), preferred_element_type=f32)


def expand_inputs(bc_ref, bx, sb, chunk):
    per = LANES // CHUNK
    packed = BC_ROWS
    first = sb * SUBS * packed + (chunk // per) * 2 * NSTATE
    v = jnp.concatenate([bc_ref[pl.ds(first + n, SUBS, stride=packed), :] for n in range(2 * NSTATE)], axis=0)
    v = pltpu.roll(v, (per - chunk % per) % per * CHUNK, 1)[:, :CHUNK]
    high = v.astype(bf16)
    rest = v - high.astype(f32)
    middle = rest.astype(bf16)
    low = (rest - middle.astype(f32)).astype(bf16)
    pieces = jnp.concatenate([high, middle, low], axis=1)
    token = lax.broadcasted_iota(jnp.int32, (3 * CHUNK, LANES), 0) % CHUNK
    for t in range(CHUNK):
        bx[t] = dot(pieces, (token == t).astype(bf16), ((1,), (0,))).reshape(2 * NSTATE, SUBS, LANES)


def lane_sums(acc, out_ref, sb, chunk):
    rows = 2 * NSTATE * SUBS
    per = LANES // CHUNK
    lane = lax.broadcasted_iota(jnp.int32, (2 * LANES, LANES), 1) - chunk % per * CHUNK
    total = jnp.zeros((rows, LANES), f32)
    for t in range(CHUNK):
        v = acc[t].reshape(rows, LANES)
        high = v.astype(bf16)
        low = (v - high.astype(f32)).astype(bf16)
        total = total + dot(jnp.concatenate([high, low], axis=1), (lane == t).astype(bf16), ((1,), (0,)))
    packed = BC_ROWS + TOKENS
    first = sb * SUBS * packed + TOKENS + (chunk // per) * 2 * NSTATE
    for n in range(2 * NSTATE):
        at = pl.ds(first + n, SUBS, stride=packed)
        out_ref[at, :] = out_ref[at, :] + total[n * SUBS : (n + 1) * SUBS]


def spread(scratch, q, values):
    for g in range(scratch.shape[0]):
        scratch[g, pl.ds(q * CHUNK, CHUNK), :] = values[:, g * LANES : (g + 1) * LANES]


def collect(ref, q, scratch):
    for g in range(scratch.shape[0]):
        ref[q, :, pl.ds(g * LANES, LANES)] = scratch[g, pl.ds(q * CHUNK, CHUNK), :]


def tree(values):
    while len(values) > 1:
        values = [a + b for a, b in zip(values[::2], values[1::2])]
    return values[0]


def softplus(v):
    return jnp.maximum(v, 0.0) + jnp.log1p(jnp.exp(-jnp.abs(v)))


def chan_row(rest_ref, column):
    return rest_ref[pl.ds(CH + column, 1), :]


def dt_products(dt_ref, small_ref, rest_ref, q):
    w_dt = small_ref[:, pl.ds(RANK, RANK)]
    return dot(dt_ref[q], w_dt, ((1,), (1,))) + chan_row(rest_ref, KCONV + NSTATE + 1)


def put_rates(rest_ref, rate_ref):
    for n in range(NSTATE):
        row = -jnp.exp(chan_row(rest_ref, KCONV + n))
        rate_ref[n] = jnp.broadcast_to(row, rate_ref.shape[1:])


def scan_fwd_kernel(
    dt_ref, mask_ref, conv_ref, bc_ref, small_ref, rest_ref, y_ref, starts_ref, state, bx, stepm, drive, ys, rate_ref
):
    seqs = dt_ref.shape[0]
    width = conv_ref.shape[2]

    @pl.when(pl.program_id(0) == 0)
    def _():
        state[...] = jnp.zeros_like(state)
        put_rates(rest_ref, rate_ref)

    starts_ref[0] = state[...]
    for q in range(seqs):
        step = softplus(dt_products(dt_ref, small_ref, rest_ref, q))
        spread(stepm, q, step + mask_ref[q, :, pl.ds(KCONV - 1, 1)])
        spread(drive, q, step * conv_ref[q].astype(f32))
    for sb in range(seqs // SUBS):
        expand_inputs(bc_ref, bx, sb, pl.program_id(0))
        sub = pl.ds(sb * SUBS, SUBS)

        def group(g, carry):
            lanes = pl.ds(pl.multiple_of(g * LANES, LANES), LANES)
            rates = [rate_ref[n, :, lanes] * LOG2E for n in range(NSTATE)]

            def token(t, st):
                rows = pl.ds(sb * SUBS * CHUNK + t, SUBS, stride=CHUNK)
                sm = stepm[g, rows, :]
                dx = drive[g, rows, :]
                parts = []
                out = []
                for n in range(NSTATE):
                    dec = jnp.exp2(sm * rates[n])
                    s_n = dec * st[n] + dx * bx[t, n]
                    out.append(s_n)
                    parts.append(s_n * bx[t, NSTATE + n])
                ys[g, rows, :] = tree(parts)
                return tuple(out)

            st = tuple(state[n, sub, lanes] for n in range(NSTATE))
            st = lax.fori_loop(0, CHUNK, token, st, unroll=FWD_UNROLL)
            for n in range(NSTATE):
                state[n, sub, lanes] = st[n]
            return carry

        lax.fori_loop(0, width // LANES, group, 0)
    for q in range(seqs):
        collect(y_ref, q, ys)


def scan_bwd_kernel(
    dt_ref, mask_ref, conv_ref, bc_ref, small_ref, rest_ref, starts_ref, gy_ref,
    gconv_ref, glow_ref, proj_ref, grate_ref, gbias_ref,
    flow, bx, stepm, step2, conv2, gy2, gs2, gc2, dec_s, pri_s, acc, rate_ref,
):
    seqs = dt_ref.shape[0]
    width = conv_ref.shape[2]
    chunk = pl.num_programs(0) - 1 - pl.program_id(0)

    @pl.when(pl.program_id(0) == 0)
    def _():
        flow[...] = jnp.zeros_like(flow)
        proj_ref[...] = jnp.zeros_like(proj_ref)
        put_rates(rest_ref, rate_ref)
        grate_ref[...] = jnp.zeros_like(grate_ref)
        gbias_ref[...] = jnp.zeros_like(gbias_ref)

    for q in range(seqs):
        step = softplus(dt_products(dt_ref, small_ref, rest_ref, q))
        spread(step2, q, step)
        spread(stepm, q, step + mask_ref[q, :, pl.ds(KCONV - 1, 1)])
        spread(conv2, q, conv_ref[q].astype(f32))
        spread(gy2, q, gy_ref[q])
    for sb in range(seqs // SUBS):
        expand_inputs(bc_ref, bx, sb, chunk)
        sub = pl.ds(sb * SUBS, SUBS)
        acc[...] = jnp.zeros_like(acc)

        def group(g, carry):
            lanes = pl.ds(pl.multiple_of(g * LANES, LANES), LANES)

            def token_f(t, st):
                rows = pl.ds(sb * SUBS * CHUNK + t, SUBS, stride=CHUNK)
                sm = stepm[g, rows, :]
                dx = step2[g, rows, :] * conv2[g, rows, :]
                out = []
                for n in range(NSTATE):
                    dec = jnp.exp2(sm * (rate_ref[n, :, lanes] * LOG2E))
                    dec_s[t, n] = dec
                    pri_s[t, n] = st[n]
                    out.append(dec * st[n] + dx * bx[t, n])
                return tuple(out)

            st = tuple(starts_ref[0, n, sub, lanes] for n in range(NSTATE))
            st = lax.fori_loop(0, CHUNK, token_f, st, unroll=FWD_UNROLL)
            for n in range(NSTATE):
                pri_s[CHUNK, n] = st[n]

            def token_b(i, carried):
                t = CHUNK - 1 - i
                fl, ga = carried
                rows = pl.ds(sb * SUBS * CHUNK + t, SUBS, stride=CHUNK)
                size = step2[g, rows, :]
                conv = conv2[g, rows, :]
                gy = gy2[g, rows, :]
                dx = size * conv
                along, gsz = [], []
                nfl, nga = [], []
                for n in range(NSTATE):
                    grad = gy * bx[t, NSTATE + n] + fl[n]
                    dg = dec_s[t, n] * grad
                    th = dg * pri_s[t, n]
                    along.append(grad * bx[t, n])
                    gsz.append(th * rate_ref[n, :, lanes])
                    acc[t, n] += grad * dx
                    acc[t, NSTATE + n] += pri_s[t + 1, n] * gy
                    nfl.append(dg)
                    nga.append(ga[n] + th * size)
                along = tree(along)
                gs2[g, rows, :] = tree(gsz) + conv * along
                gc2[g, rows, :] = size * along
                return (tuple(nfl), tuple(nga))

            fl = tuple(flow[n, sub, lanes] for n in range(NSTATE))
            ga = tuple(grate_ref[n, :, lanes] for n in range(NSTATE))
            fl, ga = lax.fori_loop(0, CHUNK, token_b, (fl, ga), unroll=BWD_UNROLL)
            for n in range(NSTATE):
                flow[n, sub, lanes] = fl[n]
                grate_ref[n, :, lanes] = ga[n]
            return carry

        lax.fori_loop(0, width // LANES, group, 0)
        lane_sums(acc, proj_ref, sb, chunk)
    skip = chan_row(rest_ref, KCONV + NSTATE + 2)
    for q in range(seqs):
        collect(gconv_ref, q, gc2)
        gconv_ref[q] += skip * gy_ref[q]
        gstep = jnp.concatenate([gs2[g, pl.ds(q * CHUNK, CHUNK), :] for g in range(width // LANES)], axis=1)
        grad = gstep * jax.nn.sigmoid(dt_products(dt_ref, small_ref, rest_ref, q))
        gbias_ref[...] += jnp.sum(grad.reshape(CHUNK // SUBS, SUBS, width), axis=0)
        low = grad.astype(bf16)
        glow_ref[q] = low
        at = pl.multiple_of(q * (TOKENS + BC_ROWS) + chunk * CHUNK, CHUNK)
        proj_ref[pl.ds(at, CHUNK), :] = dot(low, small_ref[:, pl.ds(RANK, RANK)], ((1,), (0,)))


def whole(shape):
    return pl.BlockSpec(shape, lambda i, *_: (0,) * len(shape))


def scan_specs(seqs, width, small, rest, chunk_of):
    def tokens(columns):
        return pl.BlockSpec((seqs, CHUNK, columns), lambda i: (0, chunk_of(i), 0))

    starts = pl.BlockSpec((1, NSTATE, seqs, width), lambda i: (chunk_of(i), 0, 0, 0))
    ins = [
        tokens(RANK), tokens(MASKS), tokens(width), whole((seqs * BC_ROWS, LANES)), whole(small.shape), whole(rest.shape),
    ]
    return tokens, starts, ins


def scan_forward(dt_in, masks, conv, bc, small, rest):
    seqs, length, width = conv.shape
    chunks = length // CHUNK
    tokens, starts, ins = scan_specs(seqs, width, small, rest, lambda i: i)
    tall = pltpu.VMEM((width // LANES, seqs * CHUNK, LANES), f32)
    return pl.pallas_call(
        scan_fwd_kernel,
        grid=(chunks,),
        in_specs=ins,
        out_specs=[tokens(width), starts],
        out_shape=[
            jax.ShapeDtypeStruct(conv.shape, f32),
            jax.ShapeDtypeStruct((chunks, NSTATE, seqs, width), f32),
        ],
        scratch_shapes=[
            pltpu.VMEM((NSTATE, seqs, width), f32),
            pltpu.VMEM((CHUNK, 2 * NSTATE, SUBS, LANES), f32),
            tall, tall, tall,
            pltpu.VMEM((NSTATE, SUBS, width), f32),
        ],
        compiler_params=pltpu.CompilerParams(vmem_limit_bytes=50 * 2**20),
        cost_estimate=pl.CostEstimate(
            flops=8 * conv.size * NSTATE, bytes_accessed=100 * 10**6, transcendentals=conv.size * NSTATE
        ),
        name="scan_forward",
    )(dt_in, masks, conv, bc, small, rest)


def scan_backward(dt_in, masks, conv, bc, small, rest, starts, grad_y):
    seqs, length, width = conv.shape
    chunks = length // CHUNK
    tokens, start_spec, ins = scan_specs(seqs, width, small, rest, lambda i: chunks - 1 - i)
    packed = (seqs * (TOKENS + BC_ROWS), LANES)
    tall = pltpu.VMEM((width // LANES, seqs * CHUNK, LANES), f32)
    return pl.pallas_call(
        scan_bwd_kernel,
        grid=(chunks,),
        in_specs=ins + [start_spec, tokens(width)],
        out_specs=[
            tokens(width), tokens(width), whole(packed),
            whole((NSTATE, SUBS, width)), whole((SUBS, width)),
        ],
        out_shape=[
            jax.ShapeDtypeStruct(conv.shape, f32),
            jax.ShapeDtypeStruct(conv.shape, bf16),
            jax.ShapeDtypeStruct(packed, f32),
            jax.ShapeDtypeStruct((NSTATE, SUBS, width), f32),
            jax.ShapeDtypeStruct((SUBS, width), f32),
        ],
        scratch_shapes=[
            pltpu.VMEM((NSTATE, seqs, width), f32),
            pltpu.VMEM((CHUNK, 2 * NSTATE, SUBS, LANES), f32),
            tall, tall, tall, tall, tall, tall,
            pltpu.VMEM((CHUNK, NSTATE, SUBS, LANES), f32),
            pltpu.VMEM((CHUNK + 1, NSTATE, SUBS, LANES), f32),
            pltpu.VMEM((CHUNK, 2 * NSTATE, SUBS, LANES), f32),
            pltpu.VMEM((NSTATE, SUBS, width), f32),
        ],
        compiler_params=pltpu.CompilerParams(vmem_limit_bytes=56 * 2**20),
        cost_estimate=pl.CostEstimate(
            flops=24 * conv.size * NSTATE, bytes_accessed=300 * 10**6, transcendentals=conv.size * NSTATE
        ),
        name="scan_backward",
    )(dt_in, masks, conv, bc, small, rest, starts, grad_y)


def put_combined(place_ref, blocks, w_gate, w_out):
    @pl.when(pl.program_id(0) == 0)
    def _():
        for k, block in enumerate(blocks):
            at = place_ref[2] ^ k
            rows, width = block.shape[0] // 2, block.shape[1]
            w_gate[pl.ds(pl.multiple_of(at * rows, rows), rows), :] = block[pl.ds(0, rows), :]
            if w_out is not None:
                count = w_out.shape[1] // width
                sub = rows // count
                for i in range(count):
                    part = block[pl.ds(rows + i * sub, sub), :]
                    w_out[pl.ds(pl.multiple_of(at * sub, sub), sub), pl.ds(i * width, width)] = part


def put_blocks(place_ref, blocks, out):
    @pl.when(pl.program_id(0) == 0)
    def _():
        for k, block in enumerate(blocks):
            rows = block.shape[0]
            out[pl.ds(pl.multiple_of((place_ref[2] ^ k) * rows, rows), rows), :] = block[...]


def normalised(hid):
    residual = hid.astype(f32)
    return residual * lax.rsqrt(jnp.mean(residual * residual, axis=1, keepdims=True) + norm_eps)


def earlier_rows(inner, masks):
    terms = []
    for k in range(KCONV - 1):
        terms.append(pltpu.roll(inner, KCONV - 1 - k, 0) * masks[:, k : k + 1])
    return terms + [inner]


def conv_sum(terms, chan_ref):
    total = chan_row(chan_ref, KCONV + NSTATE)
    for k, term in enumerate(terms):
        total = total + chan_row(chan_ref, k) * term
    return total


def put_columns(ref, start, values):
    count = values.shape[0]
    for i in range(values.shape[1] // LANES):
        ref[0, pl.ds(start + i * count, count), :] = values[:, i * LANES : (i + 1) * LANES]


def token_masks(ids):
    length = ids.shape[1]
    at = lax.broadcasted_iota(jnp.int32, (SUBS, length), 1)
    row = lax.broadcasted_iota(jnp.int32, (SUBS, length), 0)
    every = jnp.broadcast_to(ids, (SUBS, length))
    rows = jnp.zeros((SUBS, length), f32)
    for k in range(KCONV):
        offset = max(KCONV - 1 - k, 1)
        same = (pltpu.roll(every, offset, 1) == every) & (at >= offset)
        if k == KCONV - 1:
            same = ~same
        rows = jnp.where((row == k) & same, 1.0, rows)
    unit = lax.broadcasted_iota(jnp.int32, (length, length), 0) == lax.broadcasted_iota(jnp.int32, (length, length), 1)
    columns = dot(unit.astype(bf16), rows.astype(bf16), ((1,), (1,)))
    column = lax.broadcasted_iota(jnp.int32, columns.shape, 1)
    return jnp.where(column == KCONV - 1, columns * CUT, columns)


def front_kernel(gain_parts, planes, place_ref, hid_ref, ids_ref, *refs):
    gains = refs[:1]
    smalls, blocks = ([ref.at[k] for k in range(planes)] for ref in refs[1:3])
    normed_ref, inner_ref, conv_ref, proj_ref, mask_ref, small_ref, rest_ref, gain_ref, weights = refs[3:]
    put_blocks(place_ref, blocks, weights)
    put_blocks(place_ref, smalls, small_ref)

    @pl.when(pl.program_id(0) == 0)
    def _():
        rest_ref[...] = small_ref[:, pl.ds(2 * RANK, LANES)].astype(f32).T
        if gain_parts == 1:
            gain_ref[...] = gains[0][0]
        else:
            for e in range(2):
                for k in range(planes):
                    columns = gains[0].shape[2]
                    at = ((place_ref[2] ^ k) * 2 + (place_ref[1] ^ e)) * columns
                    gain_ref[:, pl.ds(pl.multiple_of(at, columns), columns)] = gains[0][e * planes + k]

    normed = (normalised(hid_ref[0]) * gain_ref[...]).astype(bf16)
    normed_ref[0] = normed
    inner = dot(normed, weights[...], ((1,), (0,)))
    inner_ref[0] = inner
    masks = token_masks(ids_ref[0])
    mask_ref[0] = masks
    pre = conv_sum(earlier_rows(inner, masks), rest_ref)
    conv = jax.nn.silu(pre).astype(bf16)
    conv_ref[0] = conv
    proj_ref[0, pl.ds(0, TOKENS), :] = dot(conv, small_ref[:, pl.ds(0, RANK)], ((1,), (0,)))
    put_columns(proj_ref, TOKENS, dot(rest_ref[pl.ds(0, CH), :].astype(bf16), conv, ((1,), (1,))))


def per_sequence(kernel, place, stacked, fixed, outs, scratch, flops, name):
    seqs = stacked[0].shape[0]
    half = seqs // 2
    index = {
        "every": lambda i, p: ((i + half) % seqs, 0, 0),
        "other": lambda i, p: (jnp.minimum(i, half - 1), 0, 0),
        "own": lambda i, p: (jnp.maximum(i - half, 0), 0, 0),
    }

    def block(shape, kind="every"):
        return pl.BlockSpec((1,) + tuple(shape[1:]), index[kind])

    return pl.pallas_call(
        kernel,
        grid_spec=pltpu.PrefetchScalarGridSpec(
            num_scalar_prefetch=1,
            grid=(seqs,),
            in_specs=[block(v.shape) for v in stacked] + [whole(v.shape) for v in fixed],
            out_specs=[whole(shape) if kind == "whole" else block(shape, kind) for shape, _, kind in outs],
            scratch_shapes=scratch,
        ),
        out_shape=[jax.ShapeDtypeStruct(shape, dtype) for shape, dtype, _ in outs],
        compiler_params=pltpu.CompilerParams(vmem_limit_bytes=56 * 2**20),
        cost_estimate=pl.CostEstimate(flops=flops, bytes_accessed=40 * 10**6, transcendentals=0),
        name=name,
    )(place, *stacked, *fixed)


def put_part(part, own_ref, other_ref):
    half = pl.num_programs(0) // 2

    @pl.when(pl.program_id(0) < half)
    def _():
        other_ref[0] = part.astype(bf16)

    @pl.when(pl.program_id(0) >= half)
    def _():
        own_ref[0] = part.astype(bf16)


def front(place, hidden_all, ids, gains, small_blocks, inner_blocks):
    seqs, length, model = hidden_all.shape
    planes, _, width = inner_blocks.shape
    packed = TOKENS + BC_ROWS

    def kernel(*refs):
        front_kernel(gains.shape[0], planes, *refs)

    columns = small_blocks.shape[2]
    return per_sequence(
        kernel,
        place,
        [hidden_all, ids],
        [gains, small_blocks, inner_blocks],
        [
            ((seqs, length, model), bf16, "every"),
            ((seqs, length, width), f32, "every"),
            ((seqs, length, width), bf16, "every"),
            ((seqs, packed, RANK), f32, "every"),
            ((seqs, length, MASKS), f32, "every"),
            ((width, columns), bf16, "whole"),
            ((LANES, width), f32, "whole"),
            ((1, model), f32, "whole"),
        ],
        [pltpu.VMEM((model, width), bf16)],
        2 * seqs * length * model * width,
        "front",
    )


def middle(place, normed, upstream, scanned, conv_out, rest, blocks):
    seqs, length, model = normed.shape
    width = conv_out.shape[2]
    planes = len(blocks)

    def kernel(place_ref, normed_ref, up_ref, y_ref, conv_ref, chan_ref, *refs):
        own_ref, other_ref, mixed_ref, gy_ref, ggate_ref, gskip_ref, w_gate, w_out = refs[planes:]
        put_combined(place_ref, refs[:planes], w_gate, w_out)

        @pl.when(pl.program_id(0) == 0)
        def _():
            gskip_ref[...] = jnp.zeros_like(gskip_ref)

        gate = dot(normed_ref[0], w_gate[...], ((1,), (0,)))
        conv = conv_ref[0].astype(f32)
        sigma = jax.nn.sigmoid(gate)
        act = gate * sigma
        mixer = y_ref[0] + chan_row(chan_ref, KCONV + NSTATE + 2) * conv
        mixed = (mixer * act).astype(bf16)
        mixed_ref[0] = mixed
        put_part(dot(mixed, w_out[...], ((1,), (0,))), own_ref, other_ref)
        grad_mixed = dot(up_ref[0], w_out[...], ((1,), (1,)))
        gy = grad_mixed * act
        gy_ref[0] = gy
        ggate_ref[0] = (grad_mixed * mixer * (sigma * (1.0 + gate * (1.0 - sigma)))).astype(bf16)
        gskip_ref[...] += jnp.sum((gy * conv).reshape(length // SUBS, SUBS, width), axis=0)

    return per_sequence(
        kernel,
        place,
        [normed, upstream, scanned, conv_out],
        [rest, *blocks],
        [
            ((seqs // 2, length, model), bf16, "own"),
            ((seqs // 2, length, model), bf16, "other"),
            ((seqs, length, width), bf16, "every"),
            ((seqs, length, width), f32, "every"),
            ((seqs, length, width), bf16, "every"),
            ((SUBS, width), f32, "whole"),
        ],
        [pltpu.VMEM((model, width), bf16), pltpu.VMEM((width, model), bf16)],
        6 * seqs * length * model * width,
        "middle",
    )


def back_conv(place, grad_conv, gp_dt, gp_bc, inner, conv_out, masks, small, rest):
    seqs, length, width = grad_conv.shape

    def kernel(
        place_ref, gconv_ref, gdt_ref, gbc_ref, inner_ref, conv_ref, mask_ref, small_ref, rest_ref,
        ginner_ref, sums_ref, gxbc_ref,
    ):
        @pl.when(pl.program_id(0) == 0)
        def _():
            sums_ref[...] = jnp.zeros_like(sums_ref)
            gxbc_ref[...] = jnp.zeros_like(gxbc_ref)

        masks_now = mask_ref[0]
        terms = earlier_rows(inner_ref[0], masks_now)
        pre = conv_sum(terms, rest_ref)
        packed = gbc_ref[0].astype(bf16)
        gbc = jnp.concatenate([packed[i * CH : (i + 1) * CH] for i in range(length // LANES)], axis=1)
        gxbc_ref[...] += dot(gbc, conv_ref[0], ((1,), (0,)))
        total = gconv_ref[0] + dot(gdt_ref[0], small_ref[:, pl.ds(0, RANK)], ((1,), (1,)))
        total = total + dot(gbc, rest_ref[pl.ds(0, CH), :].astype(bf16), ((0,), (0,)))
        grad = total * silu_slope(pre)
        for k in range(KCONV):
            sums_ref[k] += jnp.sum((grad * terms[k]).reshape(length // SUBS, SUBS, width), axis=0)
        sums_ref[KCONV] += jnp.sum(grad.reshape(length // SUBS, SUBS, width), axis=0)
        ginner = chan_row(rest_ref, KCONV - 1) * grad
        for k in range(KCONV - 1):
            moved = pltpu.roll(grad * masks_now[:, k : k + 1], length - (KCONV - 1 - k), 0)
            ginner = ginner + chan_row(rest_ref, k) * moved
        ginner_ref[0] = ginner.astype(bf16)

    return per_sequence(
        kernel,
        place,
        [grad_conv, gp_dt, gp_bc, inner, conv_out, masks],
        [small, rest],
        [
            ((seqs, length, width), bf16, "every"),
            ((KCONV + 1, SUBS, width), f32, "whole"),
            ((CH, width), f32, "whole"),
        ],
        [],
        2 * seqs * length * width * RANK,
        "back_conv",
    )


def back_normed(place, grad_inner, grad_gate, hidden_all, inner_blocks, blocks):
    seqs, length, width = grad_inner.shape
    model = hidden_all.shape[2]
    planes = len(blocks)

    def kernel(place_ref, ginner_ref, ggate_ref, hid_ref, *refs):
        inners, gates = [refs[0].at[k] for k in range(planes)], refs[1 : 1 + planes]
        own_ref, other_ref, ggain_ref, w_inner, w_gate = refs[1 + planes :]
        put_blocks(place_ref, inners, w_inner)
        put_combined(place_ref, gates, w_gate, None)

        @pl.when(pl.program_id(0) == 0)
        def _():
            ggain_ref[...] = jnp.zeros_like(ggain_ref)

        part = dot(ginner_ref[0], w_inner[...], ((1,), (1,))) + dot(ggate_ref[0], w_gate[...], ((1,), (1,)))
        put_part(part, own_ref, other_ref)
        ggain_ref[...] += jnp.sum((part * normalised(hid_ref[0])).reshape(length // SUBS, SUBS, model), axis=0)

    return per_sequence(
        kernel,
        place,
        [grad_inner, grad_gate, hidden_all],
        [inner_blocks, *blocks],
        [
            ((seqs // 2, length, model), bf16, "own"),
            ((seqs // 2, length, model), bf16, "other"),
            ((SUBS, model), f32, "whole"),
        ],
        [pltpu.VMEM((model, width), bf16), pltpu.VMEM((model, width), bf16)],
        4 * seqs * length * model * width,
        "back_normed",
    )


MESH = pl.DeviceIdType.MESH


class Peers:
    def __init__(self):
        self.r = lax.axis_index("rep")
        shard = lax.axis_index("shard")
        self.z, self.c = shard // 2, shard % 2

    @staticmethod
    def flip(i, k):
        return (i, i + 1 - 2 * (i % 2), (i + 2) % 4, 3 - i)[k]

    def rep(self, k):
        return {"rep": self.flip(self.r, k)}

    def plane(self, k):
        return {"shard": 2 * self.flip(self.z, k) + self.c}

    def core(self):
        return {"shard": 2 * self.z + 1 - self.c}

    def greet(self, planes):
        devices = [self.core()] + [self.rep(k) for k in (1, 2, 3)]
        if planes:
            devices += [self.plane(k) for k in (1, 2, 3)]
        barrier = pltpu.get_barrier_semaphore()
        for device in devices:
            pl.semaphore_signal(barrier, inc=1, device_id=device, device_id_type=MESH)
        pl.semaphore_wait(barrier, len(devices))


class Sends:
    def __init__(self, send_sems, recv_sems):
        self.send_sems, self.recv_sems = send_sems, recv_sems
        self.made = {}

    def make(self, slot, source, target, device):
        copy = pltpu.make_async_remote_copy(
            src_ref=source,
            dst_ref=target,
            send_sem=self.send_sems.at[slot],
            recv_sem=self.recv_sems.at[slot],
            device_id=device,
            device_id_type=MESH,
        )
        self.made[slot] = copy
        return copy

    def start(self, slot, source, target, device):
        self.make(slot, source, target, device).start()

    def arrived(self, *slots):
        for slot in slots:
            self.made[slot].wait_recv()

    def sent(self, *slots):
        for slot in slots:
            self.made[slot].wait_send()


def gather_first_kernel(
    hid, cot, in_own, in_other, small, gain, ids,
    hid_all, cot_all, weights, gate, small_all, gain_all, ids_all, send_sems, recv_sems, local_sems,
):
    me = Peers()
    net = Sends(send_sems, recv_sems)
    rows = in_own.shape[0]
    width = in_own.shape[1] // 2
    half = hid.shape[0] // 2
    low, high = pl.ds(0, half), pl.ds(half, half)
    inside = (me.z == 1) | (me.z == 2)
    outside = (me.z == 0) | (me.z == 3)
    mine = pl.ds(pl.multiple_of(me.c * rows, rows), rows)
    local = [
        pltpu.make_async_copy(hid, hid_all.at[0], local_sems.at[0]),
        pltpu.make_async_copy(cot, cot_all.at[0], local_sems.at[1]),
    ]
    for copy in local:
        copy.start()
    weights[0, mine, :] = in_own[:, :width]
    gate[mine, :] = in_own[:, width:]
    small_all[0] = small[...]
    gain_all[0] = gain[...]
    ids_all[0] = ids[...]
    me.greet(True)
    net.start(0, in_other.at[:, pl.ds(0, width)], weights.at[0, mine], me.core())
    net.start(26, in_other.at[:, pl.ds(width, width)], gate.at[mine], me.core())
    for k in (1, 2, 3):
        net.start(k, ids, ids_all.at[k], me.rep(k))
        net.start(3 + k, gain, gain_all.at[k], me.plane(k))
        net.start(6 + k, small, small_all.at[k], me.plane(k))
    net.start(10, hid.at[high], hid_all.at[1, high], me.rep(1))
    net.start(11, hid.at[low], hid_all.at[2, low], me.rep(2))
    net.start(12, hid.at[low], hid_all.at[1, low], me.rep(1))
    net.start(13, hid.at[high], hid_all.at[2, high], me.rep(2))
    net.start(14, hid, hid_all.at[4], me.core())
    net.arrived(0)
    own = weights.at[0]
    net.start(15, own, weights.at[2], me.plane(2))
    net.start(16, own, weights.at[1], me.plane(1))
    across = net.make(17, own, weights.at[3], me.plane(3))
    net.arrived(1, 2, 3, 4, 5, 6)
    net.start(18, ids_all.at[pl.ds(0, 4)], ids_all.at[pl.ds(4, 4)], me.core())
    net.start(19, gain_all.at[pl.ds(0, 4)], gain_all.at[pl.ds(4, 4)], me.core())
    net.arrived(10, 11)
    net.start(20, hid_all.at[1, high], hid_all.at[3, high], me.rep(2))
    net.start(21, hid_all.at[2, low], hid_all.at[3, low], me.rep(1))
    net.start(27, cot.at[high], cot_all.at[1, high], me.rep(1))
    net.start(28, cot.at[low], cot_all.at[2, low], me.rep(2))
    net.start(29, cot.at[low], cot_all.at[1, low], me.rep(1))
    net.start(30, cot.at[high], cot_all.at[2, high], me.rep(2))
    net.start(31, cot, cot_all.at[4], me.core())
    net.arrived(12)
    net.start(22, hid_all.at[1], hid_all.at[5], me.core())
    net.arrived(13)
    net.start(23, hid_all.at[2], hid_all.at[6], me.core())
    net.arrived(15)
    onward = net.make(24, weights.at[2], weights.at[3], me.plane(1))

    @pl.when(inside)
    def _():
        across.start()
        onward.start()

    net.arrived(20, 21)
    net.start(25, hid_all.at[3], hid_all.at[7], me.core())
    net.arrived(16)

    @pl.when(inside)
    def _():
        across.wait_recv()

    @pl.when(outside)
    def _():
        onward.wait_recv()

    net.arrived(27, 28)
    net.start(32, cot_all.at[1, high], cot_all.at[3, high], me.rep(2))
    net.start(33, cot_all.at[2, low], cot_all.at[3, low], me.rep(1))
    net.arrived(29)
    net.start(34, cot_all.at[1], cot_all.at[5], me.core())
    net.arrived(30)
    net.start(35, cot_all.at[2], cot_all.at[6], me.core())
    net.arrived(32, 33)
    net.start(36, cot_all.at[3], cot_all.at[7], me.core())
    net.arrived(7, 8, 9, 14, 18, 19, 22, 23, 25, 26, 31, 34, 35, 36)
    for copy in local:
        copy.wait()
    net.sent(*[slot for slot in net.made if slot not in (17, 24)])

    @pl.when(inside)
    def _():
        across.wait_send()
        onward.wait_send()


def gather_first(hid, cot, in_own, in_other, small, gain, ids):
    length, model = hid.shape
    rows, width = in_own.shape[0], in_own.shape[1] // 2
    anywhere = pl.BlockSpec(memory_space=pl.ANY)
    vmem = pl.BlockSpec(memory_space=pltpu.VMEM)
    return pl.pallas_call(
        gather_first_kernel,
        in_specs=[vmem] * 7,
        out_specs=[anywhere] * 2 + [vmem] * 5,
        out_shape=[
            jax.ShapeDtypeStruct((8, length, model), bf16),
            jax.ShapeDtypeStruct((8, length, model), bf16),
            jax.ShapeDtypeStruct((4, 2 * rows, width), bf16),
            jax.ShapeDtypeStruct((2 * rows, width), bf16),
            jax.ShapeDtypeStruct((4,) + small.shape, bf16),
            jax.ShapeDtypeStruct((8,) + gain.shape, f32),
            jax.ShapeDtypeStruct((8,) + ids.shape, f32),
        ],
        scratch_shapes=[
            pltpu.SemaphoreType.DMA((37,)),
            pltpu.SemaphoreType.DMA((37,)),
            pltpu.SemaphoreType.DMA((2,)),
        ],
        compiler_params=pltpu.CompilerParams(
            collective_id=1, has_side_effects=True, vmem_limit_bytes=MOST
        ),
        cost_estimate=pl.CostEstimate(flops=0, bytes_accessed=100 * 10**6, transcendentals=0),
        name="gather_first",
    )(hid, cot, in_own, in_other, small, gain, ids)


def reduce_plane_kernel(part, dt_all, bc_all, near, pair, far, send_sems, recv_sems):
    me = Peers()
    net = Sends(send_sems, recv_sems)
    tokens = dt_all.shape[1]
    me.greet(False)
    for k in (1, 2, 3, 0):
        net.start(k, part.at[4 + k], near.at[k], me.core())
    for k in (1, 2, 3):
        net.arrived(k)
        pair[k - 1] = part[k] + near[k]
        net.start(3 + k, pair.at[k - 1], far.at[k - 1], me.rep(k))
    net.arrived(0)
    total = part[0] + near[0]
    for k in (1, 2, 3):
        net.arrived(3 + k)
        total = total + far[k - 1]
    dt_all[0] = total[:tokens].astype(bf16)
    bc_all[0] = total[tokens:]
    for k in (1, 2, 3):
        net.start(6 + k, dt_all.at[0], dt_all.at[k], me.rep(k))
        net.start(9 + k, bc_all.at[0], bc_all.at[k], me.rep(k))
    net.start(13, dt_all.at[0], dt_all.at[4], me.core())
    net.start(14, bc_all.at[0], bc_all.at[4], me.core())
    for k in (1, 2, 3):
        net.arrived(6 + k, 9 + k)
        net.start(14 + k, dt_all.at[k], dt_all.at[4 + k], me.core())
        net.start(17 + k, bc_all.at[k], bc_all.at[4 + k], me.core())
    net.arrived(13, 14, 15, 16, 17, 18, 19, 20)
    net.sent(*net.made)


def reduce_plane(part, collective):
    seqs, rows, _ = part.shape
    tokens = rows - 2 * 2 * NSTATE
    vmem = pl.BlockSpec(memory_space=pltpu.VMEM)
    return pl.pallas_call(
        reduce_plane_kernel,
        in_specs=[vmem],
        out_specs=[vmem, vmem],
        out_shape=[
            jax.ShapeDtypeStruct((seqs, tokens, RANK), bf16),
            jax.ShapeDtypeStruct((seqs, rows - tokens, RANK), f32),
        ],
        scratch_shapes=[
            pltpu.VMEM((4, rows, RANK), f32),
            pltpu.VMEM((3, rows, RANK), f32),
            pltpu.VMEM((3, rows, RANK), f32),
            pltpu.SemaphoreType.DMA((21,)),
            pltpu.SemaphoreType.DMA((21,)),
        ],
        compiler_params=pltpu.CompilerParams(
            collective_id=collective, has_side_effects=True, vmem_limit_bytes=16 * 2**20
        ),
        cost_estimate=pl.CostEstimate(flops=0, bytes_accessed=50 * 10**6, transcendentals=0),
        name="reduce_plane",
    )(part)


def finish_kernel(
    part, other_part, gin, small, grad_normed, pieces, small_all,
    own_part, core_part, pair, far_one, far_two, from_one, from_two,
    blocks, ends, middle_block, block_one, block_two, two_out, total, small_own, small_in, small_total,
    send_sems, recv_sems, local_sems,
):
    me = Peers()
    net = Sends(send_sems, recv_sems)
    half = part.shape[1] // 2
    low, high = pl.ds(0, half), pl.ds(half, half)
    rows = gin.shape[0] // 4
    small_rows = small.shape[0] // 4
    own_rows = rows // 2
    inside = (me.z == 1) | (me.z == 2)
    outside = (me.z == 0) | (me.z == 3)

    def block(ref, k, size):
        return ref.at[pl.ds(pl.multiple_of(me.flip(me.z, k) * size, size), size)]

    local = [
        pltpu.make_async_copy(part, own_part, local_sems.at[0]),
        pltpu.make_async_copy(block(gin, 0, rows), blocks.at[0], local_sems.at[1]),
        pltpu.make_async_copy(block(gin, 2, rows), blocks.at[1], local_sems.at[2]),
        pltpu.make_async_copy(block(small, 0, small_rows), small_own, local_sems.at[3]),
    ]
    for copy in local:
        copy.start()
    me.greet(True)
    for i, k in enumerate((3, 1, 2, 0)):
        net.start(i, other_part.at[k], core_part.at[k], me.core())
    to_ends = net.make(7, block(gin, 3, rows), ends, me.plane(1))
    to_middle = net.make(8, block(gin, 3, rows), middle_block, me.plane(3))

    @pl.when(outside)
    def _():
        to_ends.start()

    @pl.when(inside)
    def _():
        to_middle.start()

    two = net.make(9, two_out, block_two, me.plane(2))
    local[2].wait()
    local[0].wait()
    for i, k in enumerate((3, 1, 2)):
        net.arrived(i)
        pair[k - 1] = (own_part[k].astype(f32) + core_part[k].astype(f32)).astype(bf16)
        if k == 3:
            net.start(11, pair.at[2, low], far_one, me.rep(1))
            net.start(12, pair.at[2, high], far_two, me.rep(2))
        elif k == 1:
            net.start(13, pair.at[0, low], from_one.at[low], me.rep(1))
        else:
            net.start(14, pair.at[1, high], from_two.at[high], me.rep(2))

    @pl.when(outside)
    def _():
        to_ends.wait_send()
        two_out[...] = blocks[1]
        two.start()

    net.start(10, block(gin, 1, rows), block_one, me.plane(1))

    @pl.when(inside)
    def _():
        to_ends.wait_recv()
        two_out[...] = (blocks[1].astype(f32) + ends[...].astype(f32)).astype(bf16)
        two.start()

    for k in (1, 2, 3):
        net.start(3 + k, block(small, k, small_rows), small_in.at[k - 1], me.plane(k))
    net.arrived(11)
    pair[1, low] = (pair[1, low].astype(f32) + far_one[...].astype(f32)).astype(bf16)
    net.start(15, pair.at[1, low], from_two.at[low], me.rep(2))
    net.arrived(12)
    pair[0, high] = (pair[0, high].astype(f32) + far_two[...].astype(f32)).astype(bf16)
    net.start(16, pair.at[0, high], from_one.at[high], me.rep(1))
    local[1].wait()
    net.arrived(10, 9)
    summed = blocks[0].astype(f32) + block_one[...].astype(f32) + block_two[...].astype(f32)

    @pl.when(inside)
    def _():
        to_middle.wait_recv()
        total[...] = (summed + middle_block[...].astype(f32)).astype(bf16)

    @pl.when(outside)
    def _():
        total[...] = summed.astype(bf16)

    mine = total.at[pl.ds(pl.multiple_of(me.c * own_rows, own_rows), own_rows)]
    other = total.at[pl.ds(pl.multiple_of((1 - me.c) * own_rows, own_rows), own_rows)]
    net.start(20, other, pieces.at[4], me.core())
    kept = pltpu.make_async_copy(mine, pieces.at[0], local_sems.at[5])
    kept.start()
    for k in (1, 2, 3):
        net.start(20 + k, mine, pieces.at[k], me.rep(k))
    net.arrived(20)
    for k in (1, 2, 3):
        net.start(23 + k, pieces.at[4], pieces.at[4 + k], me.rep(k))
    local[3].wait()
    net.arrived(4, 5, 6)
    small_total[...] = small_own[...] + small_in[0] + small_in[1] + small_in[2]
    kept_small = pltpu.make_async_copy(small_total, small_all.at[0], local_sems.at[4])
    kept_small.start()
    for k in (1, 2, 3):
        net.start(16 + k, small_total, small_all.at[k], me.rep(k))
    net.arrived(3)
    net.arrived(13, 14, 15, 16)
    grad_normed[...] = (
        own_part[0].astype(f32) + core_part[0].astype(f32) + from_one[...].astype(f32) + from_two[...].astype(f32)
    )
    net.arrived(17, 18, 19, 21, 22, 23, 24, 25, 26)
    kept.wait()
    kept_small.wait()
    net.sent(*[slot for slot in net.made if slot not in (7, 8)])

    @pl.when(inside)
    def _():
        to_middle.wait_send()


def finish(part, other_part, gin, small):
    _, length, model = part.shape
    rows, width = gin.shape[0] // 4, gin.shape[1]
    small_rows, cols = small.shape[0] // 4, small.shape[1]
    anywhere = pl.BlockSpec(memory_space=pl.ANY)
    big = (length, model)
    return pl.pallas_call(
        finish_kernel,
        in_specs=[anywhere] * 4,
        out_specs=[pl.BlockSpec(memory_space=pltpu.VMEM), anywhere, anywhere],
        out_shape=[
            jax.ShapeDtypeStruct(big, f32),
            jax.ShapeDtypeStruct((8, rows // 2, width), bf16),
            jax.ShapeDtypeStruct((4, small_rows, cols), f32),
        ],
        scratch_shapes=[
            pltpu.VMEM((4,) + big, bf16),
            pltpu.VMEM((4,) + big, bf16),
            pltpu.VMEM((3,) + big, bf16),
            pltpu.VMEM((length // 2, model), bf16),
            pltpu.VMEM((length // 2, model), bf16),
            pltpu.VMEM(big, bf16),
            pltpu.VMEM(big, bf16),
            pltpu.VMEM((2, rows, width), bf16),
            pltpu.VMEM((rows, width), bf16),
            pltpu.VMEM((rows, width), bf16),
            pltpu.VMEM((rows, width), bf16),
            pltpu.VMEM((rows, width), bf16),
            pltpu.VMEM((rows, width), bf16),
            pltpu.VMEM((rows, width), bf16),
            pltpu.VMEM((small_rows, cols), f32),
            pltpu.VMEM((3, small_rows, cols), f32),
            pltpu.VMEM((small_rows, cols), f32),
            pltpu.SemaphoreType.DMA((27,)),
            pltpu.SemaphoreType.DMA((27,)),
            pltpu.SemaphoreType.DMA((6,)),
        ],
        compiler_params=pltpu.CompilerParams(
            collective_id=4, has_side_effects=True, vmem_limit_bytes=MOST
        ),
        cost_estimate=pl.CostEstimate(flops=0, bytes_accessed=150 * 10**6, transcendentals=0),
        name="finish",
    )(part, other_part, gin, small)


class Links:
    def __init__(self, reps, shard_size):
        self.reps, self.shard_size = reps, shard_size
        self.planes = shard_size // 2
        self.r = lax.axis_index("rep")
        shard = lax.axis_index("shard")
        self.plane, self.c = shard // 2, shard % 2

    def rep(self, value, k):
        return lax.ppermute(value, "rep", [(i, i ^ k) for i in range(self.reps)])

    def core(self, value):
        return lax.ppermute(value, "shard", [(i, i ^ 1) for i in range(self.shard_size)])

    def planes_pairs(self, pairs):
        return [(2 * a + core, 2 * b + core) for a, b in pairs for core in range(2)]

    def z(self, value, pairs):
        return lax.ppermute(value, "shard", self.planes_pairs(pairs))

    def z_xor(self, value, k):
        return self.z(value, [(i, i ^ k) for i in range(self.planes)])

    def gather_rep(self, value):
        if self.reps != 4:
            return [value] + [self.rep(value, k) for k in range(1, self.reps)]
        half = value.shape[0] // 2
        one, two = self.rep(value, 1), self.rep(value, 2)
        return [value, one, two, self.across(one, two, half)]

    def gather_rep_list(self, value):
        return [value] + [self.rep(value, k) for k in range(1, self.reps)]

    def gather_plane(self, value):
        near = jnp.stack([value] + [self.rep(value, k) for k in range(1, self.reps)])
        return jnp.concatenate([near, self.core(near)], axis=0)

    def scatter_plane(self, partial, wire):
        reps = self.reps
        pair = partial[:reps].astype(f32) + self.core(partial[reps:].astype(wire)).astype(f32)
        total = pair[0]
        for k in range(1, reps):
            total = total + self.rep(pair[k].astype(wire), k).astype(f32)
        return total

    def place_z(self, values):
        rows = values[0].shape[0]
        out = jnp.zeros((self.planes * rows,) + values[0].shape[1:], values[0].dtype)
        start = (0,) * (values[0].ndim - 1)
        for k, value in enumerate(values):
            out = lax.dynamic_update_slice(out, value, ((self.plane ^ k) * rows,) + start)
        return out

    def gather_z_list(self, value):
        return [value] + [self.z_xor(value, k) for k in range(1, self.planes)]

    def gather_z(self, value):
        return self.place_z(self.gather_z_list(value))

    def block_z(self, value, k):
        rows = value.shape[0] // self.planes
        return lax.dynamic_slice_in_dim(value, (self.plane ^ k) * rows, rows, 0)

    def send_z(self, value):
        return [self.z_xor(self.block_z(value, k), k) for k in range(1, self.planes)]

    def sum_z(self, value, moved):
        total = self.block_z(value, 0).astype(f32)
        for other in moved:
            total = total + other.astype(f32)
        return total.astype(value.dtype)

    def send_half(self, part, k):
        return self.rep(part[k : 2 * k], k)

    def sum_halves(self, part, moved):
        k = self.reps // 2
        while k > 1:
            part = (part[:k].astype(f32) + moved.astype(f32)).astype(part.dtype)
            k //= 2
            moved = self.send_half(part, k)
        return part[0].astype(f32) + moved[0].astype(f32)

    def add_pair(self, part, far):
        return (part.astype(f32) + far.astype(f32)).astype(bf16)

    def pair_rows(self, own, other):
        first = jnp.where(self.c == 0, own, other)
        second = jnp.where(self.c == 0, other, own)
        return jnp.stack([first, second])

    def order_reps(self, values):
        return order(values, self.r)

    def sum_plane(self, part, length, collective):
        if self.reps == 4 and self.planes == 4:
            return reduce_plane(part, collective)
        total = self.gather_plane(self.scatter_plane(part, f32))
        return total[:, :length].astype(bf16), total[:, length:]


def adam_step(master, first, second, gradient, rate, decays):
    first_new = beta_first * first + (1.0 - beta_first) * gradient
    second_new = beta_second * second + (1.0 - beta_second) * gradient * gradient
    update = (
        first_new
        / (1.0 - beta_first**ADAM_STEP)
        / (jnp.sqrt(second_new / (1.0 - beta_second**ADAM_STEP)) + adam_eps)
    )
    if decays:
        update = update + weight_decay * master
    return (first_new, second_new, master - rate * update)


def adam_in_kernel(reps, place_ref, *refs):
    pieces = refs[: 2 * reps]
    master_ref, first_ref, second_ref = refs[2 * reps : 2 * reps + 3]
    first_out, second_out, master_out = refs[-3:]
    r, c = place_ref[0], place_ref[1]
    sub = LANES
    for e in range(2):
        for k in range(reps):
            at = ((c ^ e) * reps + (r ^ k)) * sub
            lanes = pl.ds(pl.multiple_of(at, sub), sub)
            gradient = pieces[e * reps + k][...].astype(f32)
            first, second, master = adam_step(
                master_ref[:, lanes], first_ref[:, lanes], second_ref[:, lanes], gradient,
                learn_rates[0], with_decay[0],
            )
            first_out[:, lanes] = first
            second_out[:, lanes] = second
            master_out[:, lanes] = master


def adam_in(place, half, pieces, master, first, second, earlier):
    rows, columns = master.shape
    reps = len(pieces) // 2
    sub = LANES
    block = 2 * reps * sub
    steps = columns // 2 // block
    wide = pl.BlockSpec((rows, block), lambda i, p: (0, half * steps + i))
    thin = [pl.BlockSpec((rows, sub), functools.partial(lambda at, i, p: (at, i), at)) for _, at in pieces]
    anywhere = pl.BlockSpec(memory_space=pl.ANY)
    aliases = {1 + 2 * reps + 3 + i: i for i in range(len(earlier))}
    return pl.pallas_call(
        functools.partial(adam_in_kernel, reps),
        grid_spec=pltpu.PrefetchScalarGridSpec(
            num_scalar_prefetch=1,
            grid=(steps,),
            in_specs=thin + [wide] * 3 + [anywhere] * len(earlier),
            out_specs=[wide] * 3,
        ),
        out_shape=[jax.ShapeDtypeStruct(master.shape, f32)] * 3,
        input_output_aliases=aliases,
        compiler_params=pltpu.CompilerParams(vmem_limit_bytes=MOST),
        cost_estimate=pl.CostEstimate(flops=10 * master.size, bytes_accessed=13 * master.size, transcendentals=master.size),
        name="adam_in",
    )(place, *[array for array, _ in pieces], master, first, second, *earlier)


def adam_out_kernel(place_ref, *refs):
    reps = len(refs) - 6
    master_ref, first_ref, second_ref, first_out, second_out, master_out = refs[reps:]
    sub, wide = master_ref.shape[0], refs[0].shape[1]
    for k in range(reps):

        @pl.when(pl.program_id(0) == k)
        def _():
            for j in range(master_ref.shape[1] // wide):
                lanes = pl.ds(j * wide, wide)
                first_out[:, lanes], second_out[:, lanes], master_out[:, lanes] = adam_step(
                    master_ref[:, lanes], first_ref[:, lanes], second_ref[:, lanes],
                    refs[k][pl.ds(j * sub, sub), :].astype(f32), learn_rates[3], with_decay[3],
                )


def adam_out(place, pieces, master, first, second):
    rows, columns = master.shape
    reps = len(pieces)
    high, wide = pieces[0].shape
    mine = pl.BlockSpec((rows // reps, columns), lambda k, p: (p[0] ^ k, 0))
    piece = pl.BlockSpec((high // 2, wide), lambda k, p: (1, 0))
    return pl.pallas_call(
        adam_out_kernel,
        grid_spec=pltpu.PrefetchScalarGridSpec(
            num_scalar_prefetch=1,
            grid=(reps,),
            in_specs=[piece] * reps + [mine] * 3,
            out_specs=[mine] * 3,
        ),
        out_shape=[jax.ShapeDtypeStruct(master.shape, f32)] * 3,
        compiler_params=pltpu.CompilerParams(vmem_limit_bytes=MOST),
        cost_estimate=pl.CostEstimate(flops=10 * master.size, bytes_accessed=26 * master.size, transcendentals=master.size),
        name="adam_out",
    )(place, *pieces, master, first, second)


def slice_in_kernel(place_ref, own_ref, other_ref, out_ref):
    out_ref[0] = own_ref[...].astype(bf16)
    out_ref[1] = other_ref[...].astype(bf16)


def slice_in(place, master, reps):
    rows, columns = master.shape
    blocks = columns // (2 * reps * LANES)

    def of_core(e):
        return pl.BlockSpec((rows, LANES), lambda b, p: (0, (2 * b + (p[1] ^ e)) * reps + p[0]))

    return pl.pallas_call(
        slice_in_kernel,
        grid_spec=pltpu.PrefetchScalarGridSpec(
            num_scalar_prefetch=1,
            grid=(blocks,),
            in_specs=[of_core(0), of_core(1)],
            out_specs=pl.BlockSpec((2, rows, LANES), lambda b, p: (0, 0, b)),
        ),
        out_shape=jax.ShapeDtypeStruct((2, rows, blocks * LANES), bf16),
        name="slice_in",
    )(place, master, master)


def after(value, *earlier):
    return lax.optimization_barrier((value, *earlier))[0]


def after_all(values, *earlier):
    return list(lax.optimization_barrier((*values, *earlier))[: len(values)])


def to_columns(values, width):
    *lead, rows, columns = values.shape
    blocks = values.reshape(*lead, rows, columns // width, width)
    return jnp.swapaxes(blocks, -3, -2).reshape(*lead, rows * columns // width, width)


def order(values, index):
    bit = 1
    while bit < len(values):
        swap = (index & bit) != 0
        values = [jnp.where(swap, values[i ^ bit], values[i]) for i in range(len(values))]
        bit *= 2
    return jnp.stack(values)


def shards(
    reps, shard_size,
    hidden, segments, cotangent,
    in_master, in_first, in_second,
    x_master, x_first, x_second,
    dt_master, dt_first, dt_second,
    out_master, out_first, out_second,
    chan_master, chan_first, chan_second,
    gain_master, gain_first, gain_second,
):
    net = Links(reps, shard_size)
    planes, r, c = net.planes, net.r, net.c
    length, model = hidden.shape[1:]
    in_rows = in_master.shape[0]
    own_chan = out_master.shape[0]
    sub = own_chan // reps
    width = planes * sub
    xcols = x_master.shape[1]
    chan_cols = chan_master.shape[1]
    seqs = 2 * reps

    def sub_rows(value):
        return lax.dynamic_slice_in_dim(value, r * sub, sub, 0)

    def own_rows(rows):
        rows = rows.reshape(2, in_rows, width)
        own = lax.dynamic_index_in_dim(rows, c, 0, keepdims=False)
        return own, net.core(lax.dynamic_index_in_dim(rows, 1 - c, 0, keepdims=False))

    def full_in(pieces):
        own = net.order_reps(pieces[:reps])
        other = net.order_reps(pieces[reps:])
        every = net.pair_rows(own, other).reshape(2, reps, in_rows, planes, sub)
        return every.transpose(2, 3, 0, 1, 4).reshape(in_rows, width * seqs).astype(f32)

    place = jnp.stack([r, c, net.plane]).astype(jnp.int32)
    own_hidden = hidden[0]
    tiled = sub % LANES == 0
    fast = tiled and reps == 4 and planes == 4
    if tiled:
        in_own, in_other = slice_in(place, in_master, reps)
    else:
        in_view = in_master.reshape(in_rows, 2, planes, 2, reps, sub)
        in_mine = lax.dynamic_index_in_dim(in_view, r, 4, keepdims=False).astype(bf16)
        in_own = lax.dynamic_index_in_dim(in_mine, c, 3, keepdims=False).reshape(in_rows, 2 * width)
        in_other = lax.dynamic_index_in_dim(in_mine, 1 - c, 3, keepdims=False).reshape(in_rows, 2 * width)
    x_mine = sub_rows(x_master)
    small = jnp.concatenate([x_mine[:, :RANK], sub_rows(dt_master), x_mine[:, RANK:], sub_rows(chan_master)], axis=1)
    small = jnp.pad(small.astype(bf16), ((0, 0), (0, -small.shape[1] % LANES)))
    out_mine = sub_rows(out_master).astype(bf16)
    own_gain = lax.reduce_precision(gain_master, 8, 7)[None]
    own_ids = segments.astype(f32)
    if fast:
        hidden_all, upstream, inner_blocks, gate_pair, small_blocks, gains, ids = gather_first(
            own_hidden, cotangent[0], in_own, in_other, small, own_gain, own_ids
        )
    else:
        ids = net.gather_plane(own_ids).reshape(seqs, 1, length)
        gain_pair = net.pair_rows(own_gain[0], net.core(own_gain[0])).reshape(2 * in_rows)
        gains = net.gather_z(gain_pair).reshape(1, 1, model)
        small_blocks = jnp.stack(net.gather_z_list(small))
        in_pair = net.pair_rows(in_own, net.core(in_other)).reshape(2 * in_rows, 2 * width)
        inner_blocks = jnp.stack(net.gather_z_list(in_pair[:, :width]))
        hidden_all = net.gather_plane(own_hidden)
        upstream = net.gather_plane(cotangent[0])
        gate_pair = in_pair[:, width:]
    blocks = net.gather_z_list(jnp.concatenate([gate_pair, to_columns(out_mine, width)]))
    normed, inner, conv_out, proj_part, masks, small_all, rest, gain = front(
        place, hidden_all, ids, gains, small_blocks, inner_blocks
    )
    dt_in, bc = net.sum_plane(proj_part, length, 2)
    bc = bc.reshape(-1, LANES)
    scanned, starts = scan_forward(dt_in, masks, conv_out, bc, small_all, rest)
    out_own, out_other, mixed, grad_y, grad_gate, grad_skip = middle(
        place, normed, upstream, scanned, conv_out, rest, blocks
    )
    out_far = net.core(out_other)
    grad_out = dot(mixed.reshape(-1, width), upstream.reshape(-1, model), ((0,), (0,))).astype(bf16)
    flat_normed = normed.reshape(-1, model)
    gin_gate = dot(flat_normed, grad_gate.reshape(-1, width), ((0,), (0,))).astype(bf16)
    grad_rows = jnp.concatenate(
        [gin_gate.reshape(planes, -1, width), to_columns(grad_out.reshape(planes, sub, model), width)], axis=1
    ).reshape(-1, width)
    grad_rows_moved = net.send_z(grad_rows)
    pair = net.add_pair(out_own, out_far)
    out_first_half = net.send_half(pair, reps // 2)
    grad_y = after(grad_y, grad_rows, pair)

    grad_conv, grad_dtlow, proj_back, grad_rates, grad_dtbias = scan_backward(
        dt_in, masks, conv_out, bc, small_all, rest, starts, grad_y
    )
    grad_rates = jnp.sum(grad_rates, axis=1).T
    rates = -jnp.exp(rest[CH + KCONV : CH + KCONV + NSTATE].T)
    grad_dt = dot(grad_dtlow.reshape(-1, width), dt_in.reshape(-1, RANK), ((0,), (0,)))
    out_sum = net.sum_halves(pair, after(out_first_half, proj_back))
    layer_output = (hidden[0].astype(f32) + out_sum).astype(bf16)
    grad_rows = net.sum_z(grad_rows, after_all(grad_rows_moved, proj_back))
    gate_rows = own_rows(grad_rows[: 2 * in_rows])
    pieces = jnp.concatenate([*gate_rows, grad_rows[2 * in_rows :]])
    proj_back = after(proj_back, pieces)
    gp_dt, gp_bc = net.sum_plane(proj_back.reshape(seqs, TOKENS + BC_ROWS, LANES), length, 3)
    pieces = net.gather_rep_list(after(pieces, gp_dt))
    grad_xdt = dot(conv_out.reshape(-1, width), gp_dt.reshape(-1, RANK), ((0,), (0,)))
    grad_inner, conv_sums, grad_xbc = back_conv(
        place, grad_conv, gp_dt, gp_bc, inner, conv_out, masks, small_all, rest
    )
    grad_x = jnp.concatenate([grad_xdt, grad_xbc.T], axis=1)
    gin_inner = dot(flat_normed, grad_inner.reshape(-1, width), ((0,), (0,))).astype(bf16)
    back_own, back_other, grad_gain = back_normed(place, grad_inner, grad_gate, hidden_all, inner_blocks, blocks)
    out_new = adam_out(
        place, pieces, out_master, out_first, out_second
    )
    grad_small = jnp.concatenate(
        [
            grad_x,
            grad_dt,
            jnp.sum(conv_sums[:KCONV], axis=1).T,
            grad_rates * rates,
            jnp.sum(conv_sums[KCONV], axis=0)[:, None],
            jnp.sum(grad_dtbias, axis=0)[:, None],
            jnp.sum(grad_skip, axis=0)[:, None],
            jnp.sum(grad_gain, axis=0).reshape(width, reps),
        ],
        axis=1,
    )
    if fast:
        grad_small = jnp.pad(grad_small, ((0, 0), (0, -grad_small.shape[1] % LANES)))
        grad_small = after(grad_small, *pieces)
        grad_normed, inner_pieces, small_sum = finish(back_own, back_other, gin_inner, grad_small)
        inner_pieces = [(inner_pieces.reshape(-1, width), e * reps + k) for e in range(2) for k in range(reps)]
        small_sum = net.order_reps(list(small_sum))
    else:
        grad_normed = net.scatter_plane(jnp.concatenate([back_own, back_other]), bf16)
        inner_own_rows, inner_other_rows = own_rows(net.sum_z(gin_inner, net.send_z(gin_inner)))
        inner_pieces = net.gather_rep(inner_own_rows) + net.gather_rep(inner_other_rows)
        small_sum = net.order_reps(net.gather_rep(net.sum_z(grad_small, net.send_z(grad_small))))
    own_res = hidden[0].astype(f32)
    own_inv = lax.rsqrt(jnp.mean(own_res * own_res, axis=1, keepdims=True) + norm_eps)
    grad_scaled = grad_normed * gain
    input_grad = (
        own_inv * grad_scaled
        - own_res * own_inv**3 * jnp.mean(grad_scaled * own_res, axis=1, keepdims=True)
        + cotangent[0].astype(f32)
    ).astype(bf16)

    if tiled:
        gate_pieces = [(pieces[k], e) for e in range(2) for k in range(reps)]
        in_new = adam_in(place, 1, gate_pieces, in_master, in_first, in_second, ())
        in_new = adam_in(place, 0, inner_pieces, in_master, in_first, in_second, in_new)
    else:
        gate_pieces = [pieces[k][e * in_rows : (e + 1) * in_rows] for e in range(2) for k in range(reps)]
        in_sum = jnp.concatenate([full_in(inner_pieces), full_in(gate_pieces)], axis=1)
        in_new = adam_step(in_master, in_first, in_second, in_sum, learn_rates[0], with_decay[0])
    gain_cols = slice(xcols + RANK + chan_cols, xcols + RANK + chan_cols + reps)
    gain_two = jnp.sum(small_sum[:, :, gain_cols], axis=0).reshape(2, in_rows)
    gain_own = lax.dynamic_index_in_dim(gain_two, c, 0, keepdims=False)
    gain_sum = gain_own + net.core(lax.dynamic_index_in_dim(gain_two, 1 - c, 0, keepdims=False))
    small_sum = small_sum.reshape(own_chan, -1)
    x_sum = small_sum[:, :xcols]
    dt_sum = small_sum[:, xcols : xcols + RANK]
    chan_sum = small_sum[:, xcols + RANK : xcols + RANK + chan_cols]

    def update(position, master, first, second, gradient):
        return adam_step(master, first, second, gradient, learn_rates[position], with_decay[position])

    updated = (
        *in_new,
        *update(1, x_master, x_first, x_second, x_sum),
        *update(2, dt_master, dt_first, dt_second, dt_sum),
        *out_new,
        *update(4, chan_master, chan_first, chan_second, chan_sum),
        *update(5, gain_master, gain_first, gain_second, gain_sum),
    )
    return (layer_output[None], input_grad[None], *updated)


def solution(mesh):
    token = P(("rep", "shard"), None, None)
    rows = P("shard", None)
    placed = (token, P(("rep", "shard"), None), token) + (rows,) * 15 + (P("shard"),) * 3
    return jax.shard_map(
        functools.partial(shards, mesh.shape["rep"], mesh.shape["shard"]),
        mesh=mesh,
        in_specs=placed,
        out_specs=(token, token) + (rows,) * 15 + (P("shard"),) * 3,
        check_vma=False,
    )
```

```python
import functools

import jax
import jax.numpy as jnp
from jax import lax
from jax.experimental import pallas as pl
from jax.experimental.pallas import tpu as pltpu
from jax.sharding import PartitionSpec as P

NSTATE = 16
RANK = 128
KCONV = 4
ADAM_STEP = 10
CHUNK = 32
LANES = 128
SUBS = 8
CUT = 1e30
MASKS = 8
MOST = 58 * 2**20
TOKENS = 256
BC_ROWS = TOKENS * 2 * NSTATE // LANES
CH = 2 * NSTATE
FWD_UNROLL = 8
BWD_UNROLL = 4
LOG2E = 1.4426950408889634

norm_eps = 1e-05
beta_first = 0.9
beta_second = 0.95
adam_eps = 1e-08
weight_decay = 0.1
learn_rates = (0.044, 0.03, 0.18, 0.09, 1.0, 0.6)
with_decay = (True, True, True, True, False, False)

bf16 = jnp.bfloat16
f32 = jnp.float32


def silu_slope(values):
    sigma = jax.nn.sigmoid(values)
    return sigma * (1.0 + values * (1.0 - sigma))


def dot(a, b, dims):
    return lax.dot_general(a, b, (dims, ((), ())), preferred_element_type=f32)


def expand_inputs(bc_ref, bx, sb, chunk):
    per = LANES // CHUNK
    packed = BC_ROWS
    first = sb * SUBS * packed + (chunk // per) * 2 * NSTATE
    v = jnp.concatenate([bc_ref[pl.ds(first + n, SUBS, stride=packed), :] for n in range(2 * NSTATE)], axis=0)
    v = pltpu.roll(v, (per - chunk % per) % per * CHUNK, 1)[:, :CHUNK]
    high = v.astype(bf16)
    rest = v - high.astype(f32)
    middle = rest.astype(bf16)
    low = (rest - middle.astype(f32)).astype(bf16)
    pieces = jnp.concatenate([high, middle, low], axis=1)
    token = lax.broadcasted_iota(jnp.int32, (3 * CHUNK, LANES), 0) % CHUNK
    for t in range(CHUNK):
        bx[t] = dot(pieces, (token == t).astype(bf16), ((1,), (0,))).reshape(2 * NSTATE, SUBS, LANES)


def lane_sums(acc, out_ref, sb, chunk):
    rows = 2 * NSTATE * SUBS
    per = LANES // CHUNK
    lane = lax.broadcasted_iota(jnp.int32, (2 * LANES, LANES), 1) - chunk % per * CHUNK
    total = jnp.zeros((rows, LANES), f32)
    for t in range(CHUNK):
        v = acc[t].reshape(rows, LANES)
        high = v.astype(bf16)
        low = (v - high.astype(f32)).astype(bf16)
        total = total + dot(jnp.concatenate([high, low], axis=1), (lane == t).astype(bf16), ((1,), (0,)))
    packed = BC_ROWS + TOKENS
    first = sb * SUBS * packed + TOKENS + (chunk // per) * 2 * NSTATE
    for n in range(2 * NSTATE):
        at = pl.ds(first + n, SUBS, stride=packed)
        out_ref[at, :] = out_ref[at, :] + total[n * SUBS : (n + 1) * SUBS]


def spread(scratch, q, values):
    for g in range(scratch.shape[0]):
        scratch[g, pl.ds(q * CHUNK, CHUNK), :] = values[:, g * LANES : (g + 1) * LANES]


def collect(ref, q, scratch):
    for g in range(scratch.shape[0]):
        ref[q, :, pl.ds(g * LANES, LANES)] = scratch[g, pl.ds(q * CHUNK, CHUNK), :]


def tree(values):
    while len(values) > 1:
        values = [a + b for a, b in zip(values[::2], values[1::2])]
    return values[0]


def softplus(v):
    return jnp.maximum(v, 0.0) + jnp.log1p(jnp.exp(-jnp.abs(v)))


def chan_row(rest_ref, column):
    return rest_ref[pl.ds(CH + column, 1), :]


def dt_products(dt_ref, small_ref, rest_ref, q):
    w_dt = small_ref[:, pl.ds(RANK, RANK)]
    return dot(dt_ref[q], w_dt, ((1,), (1,))) + chan_row(rest_ref, KCONV + NSTATE + 1)


def put_rates(rest_ref, rate_ref):
    for n in range(NSTATE):
        row = -jnp.exp(chan_row(rest_ref, KCONV + n))
        rate_ref[n] = jnp.broadcast_to(row, rate_ref.shape[1:])


def scan_fwd_kernel(
    dt_ref, mask_ref, conv_ref, bc_ref, small_ref, rest_ref, y_ref, starts_ref, state, bx, stepm, drive, ys, rate_ref
):
    seqs = dt_ref.shape[0]
    width = conv_ref.shape[2]

    @pl.when(pl.program_id(0) == 0)
    def _():
        state[...] = jnp.zeros_like(state)
        put_rates(rest_ref, rate_ref)

    starts_ref[0] = state[...]
    for q in range(seqs):
        step = softplus(dt_products(dt_ref, small_ref, rest_ref, q))
        spread(stepm, q, step + mask_ref[q, :, pl.ds(KCONV - 1, 1)])
        spread(drive, q, step * conv_ref[q].astype(f32))
    for sb in range(seqs // SUBS):
        expand_inputs(bc_ref, bx, sb, pl.program_id(0))
        sub = pl.ds(sb * SUBS, SUBS)

        def group(g, carry):
            lanes = pl.ds(pl.multiple_of(g * LANES, LANES), LANES)
            rates = [rate_ref[n, :, lanes] * LOG2E for n in range(NSTATE)]

            def token(t, st):
                rows = pl.ds(sb * SUBS * CHUNK + t, SUBS, stride=CHUNK)
                sm = stepm[g, rows, :]
                dx = drive[g, rows, :]
                parts = []
                out = []
                for n in range(NSTATE):
                    dec = jnp.exp2(sm * rates[n])
                    s_n = dec * st[n] + dx * bx[t, n]
                    out.append(s_n)
                    parts.append(s_n * bx[t, NSTATE + n])
                ys[g, rows, :] = tree(parts)
                return tuple(out)

            st = tuple(state[n, sub, lanes] for n in range(NSTATE))
            st = lax.fori_loop(0, CHUNK, token, st, unroll=FWD_UNROLL)
            for n in range(NSTATE):
                state[n, sub, lanes] = st[n]
            return carry

        lax.fori_loop(0, width // LANES, group, 0)
    for q in range(seqs):
        collect(y_ref, q, ys)


def scan_bwd_kernel(
    dt_ref, mask_ref, conv_ref, bc_ref, small_ref, rest_ref, starts_ref, gy_ref,
    gconv_ref, glow_ref, proj_ref, grate_ref, gbias_ref,
    flow, bx, stepm, step2, conv2, gy2, gs2, gc2, dec_s, pri_s, acc, rate_ref,
):
    seqs = dt_ref.shape[0]
    width = conv_ref.shape[2]
    chunk = pl.num_programs(0) - 1 - pl.program_id(0)

    @pl.when(pl.program_id(0) == 0)
    def _():
        flow[...] = jnp.zeros_like(flow)
        proj_ref[...] = jnp.zeros_like(proj_ref)
        put_rates(rest_ref, rate_ref)
        grate_ref[...] = jnp.zeros_like(grate_ref)
        gbias_ref[...] = jnp.zeros_like(gbias_ref)

    for q in range(seqs):
        step = softplus(dt_products(dt_ref, small_ref, rest_ref, q))
        spread(step2, q, step)
        spread(stepm, q, step + mask_ref[q, :, pl.ds(KCONV - 1, 1)])
        spread(conv2, q, conv_ref[q].astype(f32))
        spread(gy2, q, gy_ref[q])
    for sb in range(seqs // SUBS):
        expand_inputs(bc_ref, bx, sb, chunk)
        sub = pl.ds(sb * SUBS, SUBS)
        acc[...] = jnp.zeros_like(acc)

        def group(g, carry):
            lanes = pl.ds(pl.multiple_of(g * LANES, LANES), LANES)

            def token_f(t, st):
                rows = pl.ds(sb * SUBS * CHUNK + t, SUBS, stride=CHUNK)
                sm = stepm[g, rows, :]
                dx = step2[g, rows, :] * conv2[g, rows, :]
                out = []
                for n in range(NSTATE):
                    dec = jnp.exp2(sm * (rate_ref[n, :, lanes] * LOG2E))
                    dec_s[t, n] = dec
                    pri_s[t, n] = st[n]
                    out.append(dec * st[n] + dx * bx[t, n])
                return tuple(out)

            st = tuple(starts_ref[0, n, sub, lanes] for n in range(NSTATE))
            st = lax.fori_loop(0, CHUNK, token_f, st, unroll=FWD_UNROLL)
            for n in range(NSTATE):
                pri_s[CHUNK, n] = st[n]

            def token_b(i, carried):
                t = CHUNK - 1 - i
                fl, ga = carried
                rows = pl.ds(sb * SUBS * CHUNK + t, SUBS, stride=CHUNK)
                size = step2[g, rows, :]
                conv = conv2[g, rows, :]
                gy = gy2[g, rows, :]
                dx = size * conv
                along, gsz = [], []
                nfl, nga = [], []
                for n in range(NSTATE):
                    grad = gy * bx[t, NSTATE + n] + fl[n]
                    dg = dec_s[t, n] * grad
                    th = dg * pri_s[t, n]
                    along.append(grad * bx[t, n])
                    gsz.append(th * rate_ref[n, :, lanes])
                    acc[t, n] += grad * dx
                    acc[t, NSTATE + n] += pri_s[t + 1, n] * gy
                    nfl.append(dg)
                    nga.append(ga[n] + th * size)
                along = tree(along)
                gs2[g, rows, :] = tree(gsz) + conv * along
                gc2[g, rows, :] = size * along
                return (tuple(nfl), tuple(nga))

            fl = tuple(flow[n, sub, lanes] for n in range(NSTATE))
            ga = tuple(grate_ref[n, :, lanes] for n in range(NSTATE))
            fl, ga = lax.fori_loop(0, CHUNK, token_b, (fl, ga), unroll=BWD_UNROLL)
            for n in range(NSTATE):
                flow[n, sub, lanes] = fl[n]
                grate_ref[n, :, lanes] = ga[n]
            return carry

        lax.fori_loop(0, width // LANES, group, 0)
        lane_sums(acc, proj_ref, sb, chunk)
    skip = chan_row(rest_ref, KCONV + NSTATE + 2)
    for q in range(seqs):
        collect(gconv_ref, q, gc2)
        gconv_ref[q] += skip * gy_ref[q]
        gstep = jnp.concatenate([gs2[g, pl.ds(q * CHUNK, CHUNK), :] for g in range(width // LANES)], axis=1)
        grad = gstep * jax.nn.sigmoid(dt_products(dt_ref, small_ref, rest_ref, q))
        gbias_ref[...] += jnp.sum(grad.reshape(CHUNK // SUBS, SUBS, width), axis=0)
        low = grad.astype(bf16)
        glow_ref[q] = low
        at = pl.multiple_of(q * (TOKENS + BC_ROWS) + chunk * CHUNK, CHUNK)
        proj_ref[pl.ds(at, CHUNK), :] = dot(low, small_ref[:, pl.ds(RANK, RANK)], ((1,), (0,)))


def whole(shape):
    return pl.BlockSpec(shape, lambda i, *_: (0,) * len(shape))


def scan_specs(seqs, width, small, rest, chunk_of):
    def tokens(columns):
        return pl.BlockSpec((seqs, CHUNK, columns), lambda i: (0, chunk_of(i), 0))

    starts = pl.BlockSpec((1, NSTATE, seqs, width), lambda i: (chunk_of(i), 0, 0, 0))
    ins = [
        tokens(RANK), tokens(MASKS), tokens(width), whole((seqs * BC_ROWS, LANES)), whole(small.shape), whole(rest.shape),
    ]
    return tokens, starts, ins


def scan_forward(dt_in, masks, conv, bc, small, rest):
    seqs, length, width = conv.shape
    chunks = length // CHUNK
    tokens, starts, ins = scan_specs(seqs, width, small, rest, lambda i: i)
    tall = pltpu.VMEM((width // LANES, seqs * CHUNK, LANES), f32)
    return pl.pallas_call(
        scan_fwd_kernel,
        grid=(chunks,),
        in_specs=ins,
        out_specs=[tokens(width), starts],
        out_shape=[
            jax.ShapeDtypeStruct(conv.shape, f32),
            jax.ShapeDtypeStruct((chunks, NSTATE, seqs, width), f32),
        ],
        scratch_shapes=[
            pltpu.VMEM((NSTATE, seqs, width), f32),
            pltpu.VMEM((CHUNK, 2 * NSTATE, SUBS, LANES), f32),
            tall, tall, tall,
            pltpu.VMEM((NSTATE, SUBS, width), f32),
        ],
        compiler_params=pltpu.CompilerParams(vmem_limit_bytes=50 * 2**20),
        cost_estimate=pl.CostEstimate(
            flops=8 * conv.size * NSTATE, bytes_accessed=100 * 10**6, transcendentals=conv.size * NSTATE
        ),
        name="scan_forward",
    )(dt_in, masks, conv, bc, small, rest)


def scan_backward(dt_in, masks, conv, bc, small, rest, starts, grad_y):
    seqs, length, width = conv.shape
    chunks = length // CHUNK
    tokens, start_spec, ins = scan_specs(seqs, width, small, rest, lambda i: chunks - 1 - i)
    packed = (seqs * (TOKENS + BC_ROWS), LANES)
    tall = pltpu.VMEM((width // LANES, seqs * CHUNK, LANES), f32)
    return pl.pallas_call(
        scan_bwd_kernel,
        grid=(chunks,),
        in_specs=ins + [start_spec, tokens(width)],
        out_specs=[
            tokens(width), tokens(width), whole(packed),
            whole((NSTATE, SUBS, width)), whole((SUBS, width)),
        ],
        out_shape=[
            jax.ShapeDtypeStruct(conv.shape, f32),
            jax.ShapeDtypeStruct(conv.shape, bf16),
            jax.ShapeDtypeStruct(packed, f32),
            jax.ShapeDtypeStruct((NSTATE, SUBS, width), f32),
            jax.ShapeDtypeStruct((SUBS, width), f32),
        ],
        scratch_shapes=[
            pltpu.VMEM((NSTATE, seqs, width), f32),
            pltpu.VMEM((CHUNK, 2 * NSTATE, SUBS, LANES), f32),
            tall, tall, tall, tall, tall, tall,
            pltpu.VMEM((CHUNK, NSTATE, SUBS, LANES), f32),
            pltpu.VMEM((CHUNK + 1, NSTATE, SUBS, LANES), f32),
            pltpu.VMEM((CHUNK, 2 * NSTATE, SUBS, LANES), f32),
            pltpu.VMEM((NSTATE, SUBS, width), f32),
        ],
        compiler_params=pltpu.CompilerParams(vmem_limit_bytes=56 * 2**20),
        cost_estimate=pl.CostEstimate(
            flops=24 * conv.size * NSTATE, bytes_accessed=300 * 10**6, transcendentals=conv.size * NSTATE
        ),
        name="scan_backward",
    )(dt_in, masks, conv, bc, small, rest, starts, grad_y)


def put_combined(place_ref, blocks, w_gate, w_out):
    @pl.when(pl.program_id(0) == 0)
    def _():
        for k, block in enumerate(blocks):
            at = place_ref[2] ^ k
            rows, width = block.shape[0] // 2, block.shape[1]
            w_gate[pl.ds(pl.multiple_of(at * rows, rows), rows), :] = block[pl.ds(0, rows), :]
            if w_out is not None:
                count = w_out.shape[1] // width
                sub = rows // count
                for i in range(count):
                    part = block[pl.ds(rows + i * sub, sub), :]
                    w_out[pl.ds(pl.multiple_of(at * sub, sub), sub), pl.ds(i * width, width)] = part


def put_blocks(place_ref, blocks, out):
    @pl.when(pl.program_id(0) == 0)
    def _():
        for k, block in enumerate(blocks):
            rows = block.shape[0]
            out[pl.ds(pl.multiple_of((place_ref[2] ^ k) * rows, rows), rows), :] = block[...]


def normalised(hid):
    residual = hid.astype(f32)
    return residual * lax.rsqrt(jnp.mean(residual * residual, axis=1, keepdims=True) + norm_eps)


def earlier_rows(inner, masks):
    terms = []
    for k in range(KCONV - 1):
        terms.append(pltpu.roll(inner, KCONV - 1 - k, 0) * masks[:, k : k + 1])
    return terms + [inner]


def conv_sum(terms, chan_ref):
    total = chan_row(chan_ref, KCONV + NSTATE)
    for k, term in enumerate(terms):
        total = total + chan_row(chan_ref, k) * term
    return total


def put_columns(ref, start, values):
    count = values.shape[0]
    for i in range(values.shape[1] // LANES):
        ref[0, pl.ds(start + i * count, count), :] = values[:, i * LANES : (i + 1) * LANES]


def token_masks(ids):
    length = ids.shape[1]
    at = lax.broadcasted_iota(jnp.int32, (SUBS, length), 1)
    row = lax.broadcasted_iota(jnp.int32, (SUBS, length), 0)
    every = jnp.broadcast_to(ids, (SUBS, length))
    rows = jnp.zeros((SUBS, length), f32)
    for k in range(KCONV):
        offset = max(KCONV - 1 - k, 1)
        same = (pltpu.roll(every, offset, 1) == every) & (at >= offset)
        if k == KCONV - 1:
            same = ~same
        rows = jnp.where((row == k) & same, 1.0, rows)
    unit = lax.broadcasted_iota(jnp.int32, (length, length), 0) == lax.broadcasted_iota(jnp.int32, (length, length), 1)
    columns = dot(unit.astype(bf16), rows.astype(bf16), ((1,), (1,)))
    column = lax.broadcasted_iota(jnp.int32, columns.shape, 1)
    return jnp.where(column == KCONV - 1, columns * CUT, columns)


def front_kernel(gain_parts, planes, place_ref, hid_ref, ids_ref, *refs):
    gains = refs[:1]
    smalls, blocks = ([ref.at[k] for k in range(planes)] for ref in refs[1:3])
    normed_ref, inner_ref, conv_ref, proj_ref, mask_ref, small_ref, rest_ref, gain_ref, weights = refs[3:]
    put_blocks(place_ref, blocks, weights)
    put_blocks(place_ref, smalls, small_ref)

    @pl.when(pl.program_id(0) == 0)
    def _():
        rest_ref[...] = small_ref[:, pl.ds(2 * RANK, LANES)].astype(f32).T
        if gain_parts == 1:
            gain_ref[...] = gains[0][0]
        else:
            for e in range(2):
                for k in range(planes):
                    columns = gains[0].shape[2]
                    at = ((place_ref[2] ^ k) * 2 + (place_ref[1] ^ e)) * columns
                    gain_ref[:, pl.ds(pl.multiple_of(at, columns), columns)] = gains[0][e * planes + k]

    normed = (normalised(hid_ref[0]) * gain_ref[...]).astype(bf16)
    normed_ref[0] = normed
    inner = dot(normed, weights[...], ((1,), (0,)))
    inner_ref[0] = inner
    masks = token_masks(ids_ref[0])
    mask_ref[0] = masks
    pre = conv_sum(earlier_rows(inner, masks), rest_ref)
    conv = jax.nn.silu(pre).astype(bf16)
    conv_ref[0] = conv
    proj_ref[0, pl.ds(0, TOKENS), :] = dot(conv, small_ref[:, pl.ds(0, RANK)], ((1,), (0,)))
    put_columns(proj_ref, TOKENS, dot(rest_ref[pl.ds(0, CH), :].astype(bf16), conv, ((1,), (1,))))


def per_sequence(kernel, place, stacked, fixed, outs, scratch, flops, name):
    seqs = stacked[0].shape[0]
    half = seqs // 2
    index = {
        "every": lambda i, p: ((i + half) % seqs, 0, 0),
        "other": lambda i, p: (jnp.minimum(i, half - 1), 0, 0),
        "own": lambda i, p: (jnp.maximum(i - half, 0), 0, 0),
    }

    def block(shape, kind="every"):
        return pl.BlockSpec((1,) + tuple(shape[1:]), index[kind])

    return pl.pallas_call(
        kernel,
        grid_spec=pltpu.PrefetchScalarGridSpec(
            num_scalar_prefetch=1,
            grid=(seqs,),
            in_specs=[block(v.shape) for v in stacked] + [whole(v.shape) for v in fixed],
            out_specs=[whole(shape) if kind == "whole" else block(shape, kind) for shape, _, kind in outs],
            scratch_shapes=scratch,
        ),
        out_shape=[jax.ShapeDtypeStruct(shape, dtype) for shape, dtype, _ in outs],
        compiler_params=pltpu.CompilerParams(vmem_limit_bytes=56 * 2**20),
        cost_estimate=pl.CostEstimate(flops=flops, bytes_accessed=40 * 10**6, transcendentals=0),
        name=name,
    )(place, *stacked, *fixed)


def put_part(part, own_ref, other_ref):
    half = pl.num_programs(0) // 2

    @pl.when(pl.program_id(0) < half)
    def _():
        other_ref[0] = part.astype(bf16)

    @pl.when(pl.program_id(0) >= half)
    def _():
        own_ref[0] = part.astype(bf16)


def front(place, hidden_all, ids, gains, small_blocks, inner_blocks):
    seqs, length, model = hidden_all.shape
    planes, _, width = inner_blocks.shape
    packed = TOKENS + BC_ROWS

    def kernel(*refs):
        front_kernel(gains.shape[0], planes, *refs)

    columns = small_blocks.shape[2]
    return per_sequence(
        kernel,
        place,
        [hidden_all, ids],
        [gains, small_blocks, inner_blocks],
        [
            ((seqs, length, model), bf16, "every"),
            ((seqs, length, width), f32, "every"),
            ((seqs, length, width), bf16, "every"),
            ((seqs, packed, RANK), f32, "every"),
            ((seqs, length, MASKS), f32, "every"),
            ((width, columns), bf16, "whole"),
            ((LANES, width), f32, "whole"),
            ((1, model), f32, "whole"),
        ],
        [pltpu.VMEM((model, width), bf16)],
        2 * seqs * length * model * width,
        "front",
    )


def middle(place, normed, upstream, scanned, conv_out, rest, blocks):
    seqs, length, model = normed.shape
    width = conv_out.shape[2]
    planes = len(blocks)

    def kernel(place_ref, normed_ref, up_ref, y_ref, conv_ref, chan_ref, *refs):
        own_ref, other_ref, mixed_ref, gy_ref, ggate_ref, gskip_ref, w_gate, w_out = refs[planes:]
        put_combined(place_ref, refs[:planes], w_gate, w_out)

        @pl.when(pl.program_id(0) == 0)
        def _():
            gskip_ref[...] = jnp.zeros_like(gskip_ref)

        gate = dot(normed_ref[0], w_gate[...], ((1,), (0,)))
        conv = conv_ref[0].astype(f32)
        sigma = jax.nn.sigmoid(gate)
        act = gate * sigma
        mixer = y_ref[0] + chan_row(chan_ref, KCONV + NSTATE + 2) * conv
        mixed = (mixer * act).astype(bf16)
        mixed_ref[0] = mixed
        put_part(dot(mixed, w_out[...], ((1,), (0,))), own_ref, other_ref)
        grad_mixed = dot(up_ref[0], w_out[...], ((1,), (1,)))
        gy = grad_mixed * act
        gy_ref[0] = gy
        ggate_ref[0] = (grad_mixed * mixer * (sigma * (1.0 + gate * (1.0 - sigma)))).astype(bf16)
        gskip_ref[...] += jnp.sum((gy * conv).reshape(length // SUBS, SUBS, width), axis=0)

    return per_sequence(
        kernel,
        place,
        [normed, upstream, scanned, conv_out],
        [rest, *blocks],
        [
            ((seqs // 2, length, model), bf16, "own"),
            ((seqs // 2, length, model), bf16, "other"),
            ((seqs, length, width), bf16, "every"),
            ((seqs, length, width), f32, "every"),
            ((seqs, length, width), bf16, "every"),
            ((SUBS, width), f32, "whole"),
        ],
        [pltpu.VMEM((model, width), bf16), pltpu.VMEM((width, model), bf16)],
        6 * seqs * length * model * width,
        "middle",
    )


def back_conv(place, grad_conv, gp_dt, gp_bc, inner, conv_out, masks, small, rest):
    seqs, length, width = grad_conv.shape

    def kernel(
        place_ref, gconv_ref, gdt_ref, gbc_ref, inner_ref, conv_ref, mask_ref, small_ref, rest_ref,
        ginner_ref, sums_ref, gxbc_ref,
    ):
        @pl.when(pl.program_id(0) == 0)
        def _():
            sums_ref[...] = jnp.zeros_like(sums_ref)
            gxbc_ref[...] = jnp.zeros_like(gxbc_ref)

        masks_now = mask_ref[0]
        terms = earlier_rows(inner_ref[0], masks_now)
        pre = conv_sum(terms, rest_ref)
        packed = gbc_ref[0].astype(bf16)
        gbc = jnp.concatenate([packed[i * CH : (i + 1) * CH] for i in range(length // LANES)], axis=1)
        gxbc_ref[...] += dot(gbc, conv_ref[0], ((1,), (0,)))
        total = gconv_ref[0] + dot(gdt_ref[0], small_ref[:, pl.ds(0, RANK)], ((1,), (1,)))
        total = total + dot(gbc, rest_ref[pl.ds(0, CH), :].astype(bf16), ((0,), (0,)))
        grad = total * silu_slope(pre)
        for k in range(KCONV):
            sums_ref[k] += jnp.sum((grad * terms[k]).reshape(length // SUBS, SUBS, width), axis=0)
        sums_ref[KCONV] += jnp.sum(grad.reshape(length // SUBS, SUBS, width), axis=0)
        ginner = chan_row(rest_ref, KCONV - 1) * grad
        for k in range(KCONV - 1):
            moved = pltpu.roll(grad * masks_now[:, k : k + 1], length - (KCONV - 1 - k), 0)
            ginner = ginner + chan_row(rest_ref, k) * moved
        ginner_ref[0] = ginner.astype(bf16)

    return per_sequence(
        kernel,
        place,
        [grad_conv, gp_dt, gp_bc, inner, conv_out, masks],
        [small, rest],
        [
            ((seqs, length, width), bf16, "every"),
            ((KCONV + 1, SUBS, width), f32, "whole"),
            ((CH, width), f32, "whole"),
        ],
        [],
        2 * seqs * length * width * RANK,
        "back_conv",
    )


def back_normed(place, grad_inner, grad_gate, hidden_all, inner_blocks, blocks):
    seqs, length, width = grad_inner.shape
    model = hidden_all.shape[2]
    planes = len(blocks)

    def kernel(place_ref, ginner_ref, ggate_ref, hid_ref, *refs):
        inners, gates = [refs[0].at[k] for k in range(planes)], refs[1 : 1 + planes]
        own_ref, other_ref, ggain_ref, w_inner, w_gate = refs[1 + planes :]
        put_blocks(place_ref, inners, w_inner)
        put_combined(place_ref, gates, w_gate, None)

        @pl.when(pl.program_id(0) == 0)
        def _():
            ggain_ref[...] = jnp.zeros_like(ggain_ref)

        part = dot(ginner_ref[0], w_inner[...], ((1,), (1,))) + dot(ggate_ref[0], w_gate[...], ((1,), (1,)))
        put_part(part, own_ref, other_ref)
        ggain_ref[...] += jnp.sum((part * normalised(hid_ref[0])).reshape(length // SUBS, SUBS, model), axis=0)

    return per_sequence(
        kernel,
        place,
        [grad_inner, grad_gate, hidden_all],
        [inner_blocks, *blocks],
        [
            ((seqs // 2, length, model), bf16, "own"),
            ((seqs // 2, length, model), bf16, "other"),
            ((SUBS, model), f32, "whole"),
        ],
        [pltpu.VMEM((model, width), bf16), pltpu.VMEM((model, width), bf16)],
        4 * seqs * length * model * width,
        "back_normed",
    )


MESH = pl.DeviceIdType.MESH


class Peers:
    def __init__(self):
        self.r = lax.axis_index("rep")
        shard = lax.axis_index("shard")
        self.z, self.c = shard // 2, shard % 2

    @staticmethod
    def flip(i, k):
        return (i, i + 1 - 2 * (i % 2), (i + 2) % 4, 3 - i)[k]

    def rep(self, k):
        return {"rep": self.flip(self.r, k)}

    def plane(self, k):
        return {"shard": 2 * self.flip(self.z, k) + self.c}

    def core(self):
        return {"shard": 2 * self.z + 1 - self.c}

    def greet(self, planes):
        devices = [self.core()] + [self.rep(k) for k in (1, 2, 3)]
        if planes:
            devices += [self.plane(k) for k in (1, 2, 3)]
        barrier = pltpu.get_barrier_semaphore()
        for device in devices:
            pl.semaphore_signal(barrier, inc=1, device_id=device, device_id_type=MESH)
        pl.semaphore_wait(barrier, len(devices))


class Sends:
    def __init__(self, send_sems, recv_sems):
        self.send_sems, self.recv_sems = send_sems, recv_sems
        self.made = {}

    def make(self, slot, source, target, device):
        copy = pltpu.make_async_remote_copy(
            src_ref=source,
            dst_ref=target,
            send_sem=self.send_sems.at[slot],
            recv_sem=self.recv_sems.at[slot],
            device_id=device,
            device_id_type=MESH,
        )
        self.made[slot] = copy
        return copy

    def start(self, slot, source, target, device):
        self.make(slot, source, target, device).start()

    def arrived(self, *slots):
        for slot in slots:
            self.made[slot].wait_recv()

    def sent(self, *slots):
        for slot in slots:
            self.made[slot].wait_send()


def gather_first_kernel(
    hid, cot, in_own, in_other, small, gain, ids,
    hid_all, cot_all, weights, gate, small_all, gain_all, ids_all, send_sems, recv_sems, local_sems,
):
    me = Peers()
    net = Sends(send_sems, recv_sems)
    rows = in_own.shape[0]
    width = in_own.shape[1] // 2
    half = hid.shape[0] // 2
    low, high = pl.ds(0, half), pl.ds(half, half)
    inside = (me.z == 1) | (me.z == 2)
    outside = (me.z == 0) | (me.z == 3)
    mine = pl.ds(pl.multiple_of(me.c * rows, rows), rows)
    local = [
        pltpu.make_async_copy(hid, hid_all.at[0], local_sems.at[0]),
        pltpu.make_async_copy(cot, cot_all.at[0], local_sems.at[1]),
    ]
    for copy in local:
        copy.start()
    weights[0, mine, :] = in_own[:, :width]
    gate[mine, :] = in_own[:, width:]
    small_all[0] = small[...]
    gain_all[0] = gain[...]
    ids_all[0] = ids[...]
    me.greet(True)
    net.start(0, in_other.at[:, pl.ds(0, width)], weights.at[0, mine], me.core())
    net.start(26, in_other.at[:, pl.ds(width, width)], gate.at[mine], me.core())
    for k in (1, 2, 3):
        net.start(k, ids, ids_all.at[k], me.rep(k))
        net.start(3 + k, gain, gain_all.at[k], me.plane(k))
        net.start(6 + k, small, small_all.at[k], me.plane(k))
    net.start(10, hid.at[high], hid_all.at[1, high], me.rep(1))
    net.start(11, hid.at[low], hid_all.at[2, low], me.rep(2))
    net.start(12, hid.at[low], hid_all.at[1, low], me.rep(1))
    net.start(13, hid.at[high], hid_all.at[2, high], me.rep(2))
    net.start(14, hid, hid_all.at[4], me.core())
    net.arrived(0)
    own = weights.at[0]
    net.start(15, own, weights.at[2], me.plane(2))
    net.start(16, own, weights.at[1], me.plane(1))
    across = net.make(17, own, weights.at[3], me.plane(3))
    net.arrived(1, 2, 3, 4, 5, 6)
    net.start(18, ids_all.at[pl.ds(0, 4)], ids_all.at[pl.ds(4, 4)], me.core())
    net.start(19, gain_all.at[pl.ds(0, 4)], gain_all.at[pl.ds(4, 4)], me.core())
    net.arrived(10, 11)
    net.start(20, hid_all.at[1, high], hid_all.at[3, high], me.rep(2))
    net.start(21, hid_all.at[2, low], hid_all.at[3, low], me.rep(1))
    net.start(27, cot.at[high], cot_all.at[1, high], me.rep(1))
    net.start(28, cot.at[low], cot_all.at[2, low], me.rep(2))
    net.start(29, cot.at[low], cot_all.at[1, low], me.rep(1))
    net.start(30, cot.at[high], cot_all.at[2, high], me.rep(2))
    net.start(31, cot, cot_all.at[4], me.core())
    net.arrived(12)
    net.start(22, hid_all.at[1], hid_all.at[5], me.core())
    net.arrived(13)
    net.start(23, hid_all.at[2], hid_all.at[6], me.core())
    net.arrived(15)
    onward = net.make(24, weights.at[2], weights.at[3], me.plane(1))

    @pl.when(inside)
    def _():
        across.start()
        onward.start()

    net.arrived(20, 21)
    net.start(25, hid_all.at[3], hid_all.at[7], me.core())
    net.arrived(16)

    @pl.when(inside)
    def _():
        across.wait_recv()

    @pl.when(outside)
    def _():
        onward.wait_recv()

    net.arrived(27, 28)
    net.start(32, cot_all.at[1, high], cot_all.at[3, high], me.rep(2))
    net.start(33, cot_all.at[2, low], cot_all.at[3, low], me.rep(1))
    net.arrived(29)
    net.start(34, cot_all.at[1], cot_all.at[5], me.core())
    net.arrived(30)
    net.start(35, cot_all.at[2], cot_all.at[6], me.core())
    net.arrived(32, 33)
    net.start(36, cot_all.at[3], cot_all.at[7], me.core())
    net.arrived(7, 8, 9, 14, 18, 19, 22, 23, 25, 26, 31, 34, 35, 36)
    for copy in local:
        copy.wait()
    net.sent(*[slot for slot in net.made if slot not in (17, 24)])

    @pl.when(inside)
    def _():
        across.wait_send()
        onward.wait_send()


def gather_first(hid, cot, in_own, in_other, small, gain, ids):
    length, model = hid.shape
    rows, width = in_own.shape[0], in_own.shape[1] // 2
    anywhere = pl.BlockSpec(memory_space=pl.ANY)
    vmem = pl.BlockSpec(memory_space=pltpu.VMEM)
    return pl.pallas_call(
        gather_first_kernel,
        in_specs=[vmem] * 7,
        out_specs=[anywhere] * 2 + [vmem] * 5,
        out_shape=[
            jax.ShapeDtypeStruct((8, length, model), bf16),
            jax.ShapeDtypeStruct((8, length, model), bf16),
            jax.ShapeDtypeStruct((4, 2 * rows, width), bf16),
            jax.ShapeDtypeStruct((2 * rows, width), bf16),
            jax.ShapeDtypeStruct((4,) + small.shape, bf16),
            jax.ShapeDtypeStruct((8,) + gain.shape, f32),
            jax.ShapeDtypeStruct((8,) + ids.shape, f32),
        ],
        scratch_shapes=[
            pltpu.SemaphoreType.DMA((37,)),
            pltpu.SemaphoreType.DMA((37,)),
            pltpu.SemaphoreType.DMA((2,)),
        ],
        compiler_params=pltpu.CompilerParams(
            collective_id=1, has_side_effects=True, vmem_limit_bytes=MOST
        ),
        cost_estimate=pl.CostEstimate(flops=0, bytes_accessed=100 * 10**6, transcendentals=0),
        name="gather_first",
    )(hid, cot, in_own, in_other, small, gain, ids)


def reduce_plane_kernel(part, dt_all, bc_all, near, pair, far, send_sems, recv_sems):
    me = Peers()
    net = Sends(send_sems, recv_sems)
    tokens = dt_all.shape[1]
    me.greet(False)
    for k in (1, 2, 3, 0):
        net.start(k, part.at[4 + k], near.at[k], me.core())
    for k in (1, 2, 3):
        net.arrived(k)
        pair[k - 1] = part[k] + near[k]
        net.start(3 + k, pair.at[k - 1], far.at[k - 1], me.rep(k))
    net.arrived(0)
    total = part[0] + near[0]
    for k in (1, 2, 3):
        net.arrived(3 + k)
        total = total + far[k - 1]
    dt_all[0] = total[:tokens].astype(bf16)
    bc_all[0] = total[tokens:]
    for k in (1, 2, 3):
        net.start(6 + k, dt_all.at[0], dt_all.at[k], me.rep(k))
        net.start(9 + k, bc_all.at[0], bc_all.at[k], me.rep(k))
    net.start(13, dt_all.at[0], dt_all.at[4], me.core())
    net.start(14, bc_all.at[0], bc_all.at[4], me.core())
    for k in (1, 2, 3):
        net.arrived(6 + k, 9 + k)
        net.start(14 + k, dt_all.at[k], dt_all.at[4 + k], me.core())
        net.start(17 + k, bc_all.at[k], bc_all.at[4 + k], me.core())
    net.arrived(13, 14, 15, 16, 17, 18, 19, 20)
    net.sent(*net.made)


def reduce_plane(part, collective):
    seqs, rows, _ = part.shape
    tokens = rows - 2 * 2 * NSTATE
    vmem = pl.BlockSpec(memory_space=pltpu.VMEM)
    return pl.pallas_call(
        reduce_plane_kernel,
        in_specs=[vmem],
        out_specs=[vmem, vmem],
        out_shape=[
            jax.ShapeDtypeStruct((seqs, tokens, RANK), bf16),
            jax.ShapeDtypeStruct((seqs, rows - tokens, RANK), f32),
        ],
        scratch_shapes=[
            pltpu.VMEM((4, rows, RANK), f32),
            pltpu.VMEM((3, rows, RANK), f32),
            pltpu.VMEM((3, rows, RANK), f32),
            pltpu.SemaphoreType.DMA((21,)),
            pltpu.SemaphoreType.DMA((21,)),
        ],
        compiler_params=pltpu.CompilerParams(
            collective_id=collective, has_side_effects=True, vmem_limit_bytes=16 * 2**20
        ),
        cost_estimate=pl.CostEstimate(flops=0, bytes_accessed=50 * 10**6, transcendentals=0),
        name="reduce_plane",
    )(part)


def finish_kernel(
    part, other_part, gin, small, grad_normed, pieces, small_all,
    own_part, core_part, pair, far_one, far_two, from_one, from_two,
    blocks, ends, middle_block, block_one, block_two, two_out, total, small_own, small_in, small_total,
    send_sems, recv_sems, local_sems,
):
    me = Peers()
    net = Sends(send_sems, recv_sems)
    half = part.shape[1] // 2
    low, high = pl.ds(0, half), pl.ds(half, half)
    rows = gin.shape[0] // 4
    small_rows = small.shape[0] // 4
    own_rows = rows // 2
    inside = (me.z == 1) | (me.z == 2)
    outside = (me.z == 0) | (me.z == 3)

    def block(ref, k, size):
        return ref.at[pl.ds(pl.multiple_of(me.flip(me.z, k) * size, size), size)]

    local = [
        pltpu.make_async_copy(part, own_part, local_sems.at[0]),
        pltpu.make_async_copy(block(gin, 0, rows), blocks.at[0], local_sems.at[1]),
        pltpu.make_async_copy(block(gin, 2, rows), blocks.at[1], local_sems.at[2]),
        pltpu.make_async_copy(block(small, 0, small_rows), small_own, local_sems.at[3]),
    ]
    for copy in local:
        copy.start()
    me.greet(True)
    for i, k in enumerate((3, 1, 2, 0)):
        net.start(i, other_part.at[k], core_part.at[k], me.core())
    to_ends = net.make(7, block(gin, 3, rows), ends, me.plane(1))
    to_middle = net.make(8, block(gin, 3, rows), middle_block, me.plane(3))

    @pl.when(outside)
    def _():
        to_ends.start()

    @pl.when(inside)
    def _():
        to_middle.start()

    two = net.make(9, two_out, block_two, me.plane(2))
    local[2].wait()
    local[0].wait()
    for i, k in enumerate((3, 1, 2)):
        net.arrived(i)
        pair[k - 1] = (own_part[k].astype(f32) + core_part[k].astype(f32)).astype(bf16)
        if k == 3:
            net.start(11, pair.at[2, low], far_one, me.rep(1))
            net.start(12, pair.at[2, high], far_two, me.rep(2))
        elif k == 1:
            net.start(13, pair.at[0, low], from_one.at[low], me.rep(1))
        else:
            net.start(14, pair.at[1, high], from_two.at[high], me.rep(2))

    @pl.when(outside)
    def _():
        to_ends.wait_send()
        two_out[...] = blocks[1]
        two.start()

    net.start(10, block(gin, 1, rows), block_one, me.plane(1))

    @pl.when(inside)
    def _():
        to_ends.wait_recv()
        two_out[...] = (blocks[1].astype(f32) + ends[...].astype(f32)).astype(bf16)
        two.start()

    for k in (1, 2, 3):
        net.start(3 + k, block(small, k, small_rows), small_in.at[k - 1], me.plane(k))
    net.arrived(11)
    pair[1, low] = (pair[1, low].astype(f32) + far_one[...].astype(f32)).astype(bf16)
    net.start(15, pair.at[1, low], from_two.at[low], me.rep(2))
    net.arrived(12)
    pair[0, high] = (pair[0, high].astype(f32) + far_two[...].astype(f32)).astype(bf16)
    net.start(16, pair.at[0, high], from_one.at[high], me.rep(1))
    local[1].wait()
    net.arrived(10, 9)
    summed = blocks[0].astype(f32) + block_one[...].astype(f32) + block_two[...].astype(f32)

    @pl.when(inside)
    def _():
        to_middle.wait_recv()
        total[...] = (summed + middle_block[...].astype(f32)).astype(bf16)

    @pl.when(outside)
    def _():
        total[...] = summed.astype(bf16)

    mine = total.at[pl.ds(pl.multiple_of(me.c * own_rows, own_rows), own_rows)]
    other = total.at[pl.ds(pl.multiple_of((1 - me.c) * own_rows, own_rows), own_rows)]
    net.start(20, other, pieces.at[4], me.core())
    kept = pltpu.make_async_copy(mine, pieces.at[0], local_sems.at[5])
    kept.start()
    for k in (1, 2, 3):
        net.start(20 + k, mine, pieces.at[k], me.rep(k))
    net.arrived(20)
    for k in (1, 2, 3):
        net.start(23 + k, pieces.at[4], pieces.at[4 + k], me.rep(k))
    local[3].wait()
    net.arrived(4, 5, 6)
    small_total[...] = small_own[...].astype(f32) + sum(small_in[k].astype(f32) for k in range(3))
    kept_small = pltpu.make_async_copy(small_total, small_all.at[0], local_sems.at[4])
    kept_small.start()
    for k in (1, 2, 3):
        net.start(16 + k, small_total, small_all.at[k], me.rep(k))
    net.arrived(3)
    net.arrived(13, 14, 15, 16)
    grad_normed[...] = (
        own_part[0].astype(f32) + core_part[0].astype(f32) + from_one[...].astype(f32) + from_two[...].astype(f32)
    )
    net.arrived(17, 18, 19, 21, 22, 23, 24, 25, 26)
    kept.wait()
    kept_small.wait()
    net.sent(*[slot for slot in net.made if slot not in (7, 8)])

    @pl.when(inside)
    def _():
        to_middle.wait_send()


def finish(part, other_part, gin, small):
    _, length, model = part.shape
    rows, width = gin.shape[0] // 4, gin.shape[1]
    small_rows, cols = small.shape[0] // 4, small.shape[1]
    anywhere = pl.BlockSpec(memory_space=pl.ANY)
    big = (length, model)
    return pl.pallas_call(
        finish_kernel,
        in_specs=[anywhere] * 4,
        out_specs=[pl.BlockSpec(memory_space=pltpu.VMEM), anywhere, anywhere],
        out_shape=[
            jax.ShapeDtypeStruct(big, f32),
            jax.ShapeDtypeStruct((8, rows // 2, width), bf16),
            jax.ShapeDtypeStruct((4, small_rows, cols), f32),
        ],
        scratch_shapes=[
            pltpu.VMEM((4,) + big, bf16),
            pltpu.VMEM((4,) + big, bf16),
            pltpu.VMEM((3,) + big, bf16),
            pltpu.VMEM((length // 2, model), bf16),
            pltpu.VMEM((length // 2, model), bf16),
            pltpu.VMEM(big, bf16),
            pltpu.VMEM(big, bf16),
            pltpu.VMEM((2, rows, width), bf16),
            pltpu.VMEM((rows, width), bf16),
            pltpu.VMEM((rows, width), bf16),
            pltpu.VMEM((rows, width), bf16),
            pltpu.VMEM((rows, width), bf16),
            pltpu.VMEM((rows, width), bf16),
            pltpu.VMEM((rows, width), bf16),
            pltpu.VMEM((small_rows, cols), bf16),
            pltpu.VMEM((3, small_rows, cols), bf16),
            pltpu.VMEM((small_rows, cols), f32),
            pltpu.SemaphoreType.DMA((27,)),
            pltpu.SemaphoreType.DMA((27,)),
            pltpu.SemaphoreType.DMA((6,)),
        ],
        compiler_params=pltpu.CompilerParams(
            collective_id=4, has_side_effects=True, vmem_limit_bytes=MOST
        ),
        cost_estimate=pl.CostEstimate(flops=0, bytes_accessed=150 * 10**6, transcendentals=0),
        name="finish",
    )(part, other_part, gin, small)


class Links:
    def __init__(self, reps, shard_size):
        self.reps, self.shard_size = reps, shard_size
        self.planes = shard_size // 2
        self.r = lax.axis_index("rep")
        shard = lax.axis_index("shard")
        self.plane, self.c = shard // 2, shard % 2

    def rep(self, value, k):
        return lax.ppermute(value, "rep", [(i, i ^ k) for i in range(self.reps)])

    def core(self, value):
        return lax.ppermute(value, "shard", [(i, i ^ 1) for i in range(self.shard_size)])

    def planes_pairs(self, pairs):
        return [(2 * a + core, 2 * b + core) for a, b in pairs for core in range(2)]

    def z(self, value, pairs):
        return lax.ppermute(value, "shard", self.planes_pairs(pairs))

    def z_xor(self, value, k):
        return self.z(value, [(i, i ^ k) for i in range(self.planes)])

    def gather_rep(self, value):
        if self.reps != 4:
            return [value] + [self.rep(value, k) for k in range(1, self.reps)]
        half = value.shape[0] // 2
        one, two = self.rep(value, 1), self.rep(value, 2)
        return [value, one, two, self.across(one, two, half)]

    def gather_rep_list(self, value):
        return [value] + [self.rep(value, k) for k in range(1, self.reps)]

    def gather_plane(self, value):
        near = jnp.stack([value] + [self.rep(value, k) for k in range(1, self.reps)])
        return jnp.concatenate([near, self.core(near)], axis=0)

    def scatter_plane(self, partial, wire):
        reps = self.reps
        pair = partial[:reps].astype(f32) + self.core(partial[reps:].astype(wire)).astype(f32)
        total = pair[0]
        for k in range(1, reps):
            total = total + self.rep(pair[k].astype(wire), k).astype(f32)
        return total

    def place_z(self, values):
        rows = values[0].shape[0]
        out = jnp.zeros((self.planes * rows,) + values[0].shape[1:], values[0].dtype)
        start = (0,) * (values[0].ndim - 1)
        for k, value in enumerate(values):
            out = lax.dynamic_update_slice(out, value, ((self.plane ^ k) * rows,) + start)
        return out

    def gather_z_list(self, value):
        return [value] + [self.z_xor(value, k) for k in range(1, self.planes)]

    def gather_z(self, value):
        return self.place_z(self.gather_z_list(value))

    def block_z(self, value, k):
        rows = value.shape[0] // self.planes
        return lax.dynamic_slice_in_dim(value, (self.plane ^ k) * rows, rows, 0)

    def send_z(self, value):
        return [self.z_xor(self.block_z(value, k), k) for k in range(1, self.planes)]

    def sum_z(self, value, moved):
        total = self.block_z(value, 0).astype(f32)
        for other in moved:
            total = total + other.astype(f32)
        return total.astype(value.dtype)

    def send_half(self, part, k):
        return self.rep(part[k : 2 * k], k)

    def sum_halves(self, part, moved):
        k = self.reps // 2
        while k > 1:
            part = (part[:k].astype(f32) + moved.astype(f32)).astype(part.dtype)
            k //= 2
            moved = self.send_half(part, k)
        return part[0].astype(f32) + moved[0].astype(f32)

    def add_pair(self, part, far):
        return (part.astype(f32) + far.astype(f32)).astype(bf16)

    def pair_rows(self, own, other):
        first = jnp.where(self.c == 0, own, other)
        second = jnp.where(self.c == 0, other, own)
        return jnp.stack([first, second])

    def order_reps(self, values):
        return order(values, self.r)

    def sum_plane(self, part, length, collective):
        if self.reps == 4 and self.planes == 4:
            return reduce_plane(part, collective)
        total = self.gather_plane(self.scatter_plane(part, f32))
        return total[:, :length].astype(bf16), total[:, length:]


def adam_step(master, first, second, gradient, rate, decays):
    first_new = beta_first * first + (1.0 - beta_first) * gradient
    second_new = beta_second * second + (1.0 - beta_second) * gradient * gradient
    update = (
        first_new
        / (1.0 - beta_first**ADAM_STEP)
        / (jnp.sqrt(second_new / (1.0 - beta_second**ADAM_STEP)) + adam_eps)
    )
    if decays:
        update = update + weight_decay * master
    return (first_new, second_new, master - rate * update)


def adam_in_kernel(reps, place_ref, *refs):
    pieces = refs[: 2 * reps]
    master_ref, first_ref, second_ref = refs[2 * reps : 2 * reps + 3]
    first_out, second_out, master_out = refs[-3:]
    r, c = place_ref[0], place_ref[1]
    sub = LANES
    for e in range(2):
        for k in range(reps):
            at = ((c ^ e) * reps + (r ^ k)) * sub
            lanes = pl.ds(pl.multiple_of(at, sub), sub)
            gradient = pieces[e * reps + k][...].astype(f32)
            first, second, master = adam_step(
                master_ref[:, lanes], first_ref[:, lanes], second_ref[:, lanes], gradient,
                learn_rates[0], with_decay[0],
            )
            first_out[:, lanes] = first
            second_out[:, lanes] = second
            master_out[:, lanes] = master


def adam_in(place, half, pieces, master, first, second, earlier):
    rows, columns = master.shape
    reps = len(pieces) // 2
    sub = LANES
    block = 2 * reps * sub
    steps = columns // 2 // block
    wide = pl.BlockSpec((rows, block), lambda i, p: (0, half * steps + i))
    thin = [pl.BlockSpec((rows, sub), functools.partial(lambda at, i, p: (at, i), at)) for _, at in pieces]
    anywhere = pl.BlockSpec(memory_space=pl.ANY)
    aliases = {1 + 2 * reps + 3 + i: i for i in range(len(earlier))}
    return pl.pallas_call(
        functools.partial(adam_in_kernel, reps),
        grid_spec=pltpu.PrefetchScalarGridSpec(
            num_scalar_prefetch=1,
            grid=(steps,),
            in_specs=thin + [wide] * 3 + [anywhere] * len(earlier),
            out_specs=[wide] * 3,
        ),
        out_shape=[jax.ShapeDtypeStruct(master.shape, f32)] * 3,
        input_output_aliases=aliases,
        compiler_params=pltpu.CompilerParams(vmem_limit_bytes=MOST),
        cost_estimate=pl.CostEstimate(flops=10 * master.size, bytes_accessed=13 * master.size, transcendentals=master.size),
        name="adam_in",
    )(place, *[array for array, _ in pieces], master, first, second, *earlier)


def adam_out_kernel(place_ref, *refs):
    reps = len(refs) - 6
    master_ref, first_ref, second_ref, first_out, second_out, master_out = refs[reps:]
    sub, wide = master_ref.shape[0], refs[0].shape[1]
    for k in range(reps):

        @pl.when(pl.program_id(0) == k)
        def _():
            for j in range(master_ref.shape[1] // wide):
                lanes = pl.ds(j * wide, wide)
                first_out[:, lanes], second_out[:, lanes], master_out[:, lanes] = adam_step(
                    master_ref[:, lanes], first_ref[:, lanes], second_ref[:, lanes],
                    refs[k][pl.ds(j * sub, sub), :].astype(f32), learn_rates[3], with_decay[3],
                )


def adam_out(place, pieces, master, first, second):
    rows, columns = master.shape
    reps = len(pieces)
    high, wide = pieces[0].shape
    mine = pl.BlockSpec((rows // reps, columns), lambda k, p: (p[0] ^ k, 0))
    piece = pl.BlockSpec((high // 2, wide), lambda k, p: (1, 0))
    return pl.pallas_call(
        adam_out_kernel,
        grid_spec=pltpu.PrefetchScalarGridSpec(
            num_scalar_prefetch=1,
            grid=(reps,),
            in_specs=[piece] * reps + [mine] * 3,
            out_specs=[mine] * 3,
        ),
        out_shape=[jax.ShapeDtypeStruct(master.shape, f32)] * 3,
        compiler_params=pltpu.CompilerParams(vmem_limit_bytes=MOST),
        cost_estimate=pl.CostEstimate(flops=10 * master.size, bytes_accessed=26 * master.size, transcendentals=master.size),
        name="adam_out",
    )(place, *pieces, master, first, second)


def slice_in_kernel(place_ref, own_ref, other_ref, own_out, other_out):
    own_out[...] = own_ref[...].astype(bf16)
    other_out[...] = other_ref[...].astype(bf16)


def slice_in(place, master, reps):
    rows, columns = master.shape
    blocks = columns // (2 * reps * LANES)

    def of_core(e):
        return pl.BlockSpec((rows, LANES), lambda b, p: (0, (2 * b + (p[1] ^ e)) * reps + p[0]))

    return pl.pallas_call(
        slice_in_kernel,
        grid_spec=pltpu.PrefetchScalarGridSpec(
            num_scalar_prefetch=1,
            grid=(blocks,),
            in_specs=[of_core(0), of_core(1)],
            out_specs=[pl.BlockSpec((rows, LANES), lambda b, p: (0, b))] * 2,
        ),
        out_shape=[jax.ShapeDtypeStruct((rows, blocks * LANES), bf16)] * 2,
        name="slice_in",
    )(place, master, master)


def after(value, *earlier):
    return lax.optimization_barrier((value, *earlier))[0]


def after_all(values, *earlier):
    return list(lax.optimization_barrier((*values, *earlier))[: len(values)])


def to_columns(values, width):
    *lead, rows, columns = values.shape
    blocks = values.reshape(*lead, rows, columns // width, width)
    return jnp.swapaxes(blocks, -3, -2).reshape(*lead, rows * columns // width, width)


def order(values, index):
    bit = 1
    while bit < len(values):
        swap = (index & bit) != 0
        values = [jnp.where(swap, values[i ^ bit], values[i]) for i in range(len(values))]
        bit *= 2
    return jnp.stack(values)


def shards(
    reps, shard_size,
    hidden, segments, cotangent,
    in_master, in_first, in_second,
    x_master, x_first, x_second,
    dt_master, dt_first, dt_second,
    out_master, out_first, out_second,
    chan_master, chan_first, chan_second,
    gain_master, gain_first, gain_second,
):
    net = Links(reps, shard_size)
    planes, r, c = net.planes, net.r, net.c
    length, model = hidden.shape[1:]
    in_rows = in_master.shape[0]
    own_chan = out_master.shape[0]
    sub = own_chan // reps
    width = planes * sub
    xcols = x_master.shape[1]
    chan_cols = chan_master.shape[1]
    seqs = 2 * reps

    def sub_rows(value):
        return lax.dynamic_slice_in_dim(value, r * sub, sub, 0)

    def own_rows(rows):
        rows = rows.reshape(2, in_rows, width)
        own = lax.dynamic_index_in_dim(rows, c, 0, keepdims=False)
        return own, net.core(lax.dynamic_index_in_dim(rows, 1 - c, 0, keepdims=False))

    def full_in(pieces):
        own = net.order_reps(pieces[:reps])
        other = net.order_reps(pieces[reps:])
        every = net.pair_rows(own, other).reshape(2, reps, in_rows, planes, sub)
        return every.transpose(2, 3, 0, 1, 4).reshape(in_rows, width * seqs).astype(f32)

    place = jnp.stack([r, c, net.plane]).astype(jnp.int32)
    own_hidden = hidden[0]
    tiled = sub % LANES == 0
    fast = tiled and reps == 4 and planes == 4
    if tiled:
        in_own, in_other = slice_in(place, in_master, reps)
    else:
        in_view = in_master.reshape(in_rows, 2, planes, 2, reps, sub)
        in_mine = lax.dynamic_index_in_dim(in_view, r, 4, keepdims=False).astype(bf16)
        in_own = lax.dynamic_index_in_dim(in_mine, c, 3, keepdims=False).reshape(in_rows, 2 * width)
        in_other = lax.dynamic_index_in_dim(in_mine, 1 - c, 3, keepdims=False).reshape(in_rows, 2 * width)
    x_mine = sub_rows(x_master)
    small = jnp.concatenate([x_mine[:, :RANK], sub_rows(dt_master), x_mine[:, RANK:], sub_rows(chan_master)], axis=1)
    small = jnp.pad(small.astype(bf16), ((0, 0), (0, -small.shape[1] % LANES)))
    out_mine = sub_rows(out_master).astype(bf16)
    own_gain = lax.reduce_precision(gain_master, 8, 7)[None]
    own_ids = segments.astype(f32)
    if fast:
        hidden_all, upstream, inner_blocks, gate_pair, small_blocks, gains, ids = gather_first(
            own_hidden, cotangent[0], in_own, in_other, small, own_gain, own_ids
        )
    else:
        ids = net.gather_plane(own_ids).reshape(seqs, 1, length)
        gain_pair = net.pair_rows(own_gain[0], net.core(own_gain[0])).reshape(2 * in_rows)
        gains = net.gather_z(gain_pair).reshape(1, 1, model)
        small_blocks = jnp.stack(net.gather_z_list(small))
        in_pair = net.pair_rows(in_own, net.core(in_other)).reshape(2 * in_rows, 2 * width)
        inner_blocks = jnp.stack(net.gather_z_list(in_pair[:, :width]))
        hidden_all = net.gather_plane(own_hidden)
        upstream = net.gather_plane(cotangent[0])
        gate_pair = in_pair[:, width:]
    blocks = net.gather_z_list(jnp.concatenate([gate_pair, to_columns(out_mine, width)]))
    normed, inner, conv_out, proj_part, masks, small_all, rest, gain = front(
        place, hidden_all, ids, gains, small_blocks, inner_blocks
    )
    dt_in, bc = net.sum_plane(proj_part, length, 2)
    bc = bc.reshape(-1, LANES)
    scanned, starts = scan_forward(dt_in, masks, conv_out, bc, small_all, rest)
    out_own, out_other, mixed, grad_y, grad_gate, grad_skip = middle(
        place, normed, upstream, scanned, conv_out, rest, blocks
    )
    out_far = net.core(out_other)
    grad_out = dot(mixed.reshape(-1, width), upstream.reshape(-1, model), ((0,), (0,))).astype(bf16)
    flat_normed = normed.reshape(-1, model)
    gin_gate = dot(flat_normed, grad_gate.reshape(-1, width), ((0,), (0,))).astype(bf16)
    grad_rows = jnp.concatenate(
        [gin_gate.reshape(planes, -1, width), to_columns(grad_out.reshape(planes, sub, model), width)], axis=1
    ).reshape(-1, width)
    grad_rows_moved = net.send_z(grad_rows)
    pair = net.add_pair(out_own, out_far)
    out_first_half = net.send_half(pair, reps // 2)
    grad_y = after(grad_y, grad_rows, pair)

    grad_conv, grad_dtlow, proj_back, grad_rates, grad_dtbias = scan_backward(
        dt_in, masks, conv_out, bc, small_all, rest, starts, grad_y
    )
    grad_rates = jnp.sum(grad_rates, axis=1).T
    rates = -jnp.exp(rest[CH + KCONV : CH + KCONV + NSTATE].T)
    grad_dt = dot(grad_dtlow.reshape(-1, width), dt_in.reshape(-1, RANK), ((0,), (0,)))
    out_sum = net.sum_halves(pair, after(out_first_half, proj_back))
    layer_output = (hidden[0].astype(f32) + out_sum).astype(bf16)
    grad_rows = net.sum_z(grad_rows, after_all(grad_rows_moved, proj_back))
    gate_rows = own_rows(grad_rows[: 2 * in_rows])
    pieces = jnp.concatenate([*gate_rows, grad_rows[2 * in_rows :]])
    proj_back = after(proj_back, pieces)
    gp_dt, gp_bc = net.sum_plane(proj_back.reshape(seqs, TOKENS + BC_ROWS, LANES), length, 3)
    pieces = net.gather_rep_list(after(pieces, gp_dt))
    grad_xdt = dot(conv_out.reshape(-1, width), gp_dt.reshape(-1, RANK), ((0,), (0,)))
    grad_inner, conv_sums, grad_xbc = back_conv(
        place, grad_conv, gp_dt, gp_bc, inner, conv_out, masks, small_all, rest
    )
    grad_x = jnp.concatenate([grad_xdt, grad_xbc.T], axis=1)
    gin_inner = dot(flat_normed, grad_inner.reshape(-1, width), ((0,), (0,))).astype(bf16)
    back_own, back_other, grad_gain = back_normed(place, grad_inner, grad_gate, hidden_all, inner_blocks, blocks)
    out_new = adam_out(
        place, pieces, out_master, out_first, out_second
    )
    grad_small = jnp.concatenate(
        [
            grad_x,
            grad_dt,
            jnp.sum(conv_sums[:KCONV], axis=1).T,
            grad_rates * rates,
            jnp.sum(conv_sums[KCONV], axis=0)[:, None],
            jnp.sum(grad_dtbias, axis=0)[:, None],
            jnp.sum(grad_skip, axis=0)[:, None],
            jnp.sum(grad_gain, axis=0).reshape(width, reps),
        ],
        axis=1,
    )
    if fast:
        grad_small = jnp.pad(grad_small, ((0, 0), (0, -grad_small.shape[1] % LANES)))
        grad_small = after(grad_small.astype(bf16), *pieces)
        grad_normed, inner_pieces, small_sum = finish(back_own, back_other, gin_inner, grad_small)
        inner_pieces = [(inner_pieces.reshape(-1, width), e * reps + k) for e in range(2) for k in range(reps)]
        small_sum = net.order_reps(list(small_sum))
    else:
        grad_normed = net.scatter_plane(jnp.concatenate([back_own, back_other]), bf16)
        inner_own_rows, inner_other_rows = own_rows(net.sum_z(gin_inner, net.send_z(gin_inner)))
        inner_pieces = net.gather_rep(inner_own_rows) + net.gather_rep(inner_other_rows)
        small_sum = net.order_reps(net.gather_rep(net.sum_z(grad_small, net.send_z(grad_small))))
    own_res = hidden[0].astype(f32)
    own_inv = lax.rsqrt(jnp.mean(own_res * own_res, axis=1, keepdims=True) + norm_eps)
    grad_scaled = grad_normed * gain
    input_grad = (
        own_inv * grad_scaled
        - own_res * own_inv**3 * jnp.mean(grad_scaled * own_res, axis=1, keepdims=True)
        + cotangent[0].astype(f32)
    ).astype(bf16)

    if tiled:
        gate_pieces = [(pieces[k], e) for e in range(2) for k in range(reps)]
        in_new = adam_in(place, 1, gate_pieces, in_master, in_first, in_second, ())
        in_new = adam_in(place, 0, inner_pieces, in_master, in_first, in_second, in_new)
    else:
        gate_pieces = [pieces[k][e * in_rows : (e + 1) * in_rows] for e in range(2) for k in range(reps)]
        in_sum = jnp.concatenate([full_in(inner_pieces), full_in(gate_pieces)], axis=1)
        in_new = adam_step(in_master, in_first, in_second, in_sum, learn_rates[0], with_decay[0])
    gain_cols = slice(xcols + RANK + chan_cols, xcols + RANK + chan_cols + reps)
    gain_two = jnp.sum(small_sum[:, :, gain_cols], axis=0).reshape(2, in_rows)
    gain_own = lax.dynamic_index_in_dim(gain_two, c, 0, keepdims=False)
    gain_sum = gain_own + net.core(lax.dynamic_index_in_dim(gain_two, 1 - c, 0, keepdims=False))
    small_sum = small_sum.reshape(own_chan, -1)
    x_sum = small_sum[:, :xcols]
    dt_sum = small_sum[:, xcols : xcols + RANK]
    chan_sum = small_sum[:, xcols + RANK : xcols + RANK + chan_cols]

    def update(position, master, first, second, gradient):
        return adam_step(master, first, second, gradient, learn_rates[position], with_decay[position])

    updated = (
        *in_new,
        *update(1, x_master, x_first, x_second, x_sum),
        *update(2, dt_master, dt_first, dt_second, dt_sum),
        *out_new,
        *update(4, chan_master, chan_first, chan_second, chan_sum),
        *update(5, gain_master, gain_first, gain_second, gain_sum),
    )
    return (layer_output[None], input_grad[None], *updated)


def solution(mesh):
    token = P(("rep", "shard"), None, None)
    rows = P("shard", None)
    placed = (token, P(("rep", "shard"), None), token) + (rows,) * 15 + (P("shard"),) * 3
    return jax.shard_map(
        functools.partial(shards, mesh.shape["rep"], mesh.shape["shard"]),
        mesh=mesh,
        in_specs=placed,
        out_specs=(token, token) + (rows,) * 15 + (P("shard"),) * 3,
        check_vma=False,
    )
```
